32 devices in a mesh: query: 16 (over z, y, x), entity: 2 (over core).
Axes of the slice: x: 2, y: 2, z: 4, core: 2. Of those that a mesh axis runs over, the one named last changes fastest.
Arguments:
- anchor_ids: int32 [8192], P('query'), may hold values from 0 to 4095
- relation_ids: int32 [8192], P('query'), may hold values from 0 to 4130
- side_flags: int32 [8192], P('query'), may hold values from 0 to 1
- teacher_entities: bfloat16 [4096, 1000], P(('entity', 'query')), may hold values from -1.2 to 1.2, as said below
- student_entities: bfloat16 [4096, 128], P(('entity', 'query')), may hold values from -2.1 to 2.1, as said below
- teacher_relations: bfloat16 [4131, 1000], replicated, may hold values from -9 to 33, as said below
- student_relations: bfloat16 [4131, 128], replicated, may hold values from -9 to 63.6875, as said below
Outputs:
- divergence: float32 [8192], P('query')
- entity_grad: float32 [4096, 128], P(('entity', 'query'))
- query_grad: float32 [8192, 128], P('query')
The draws below stay inside these ranges and needn't reach their ends.
Inputs may be any that keep to these rules, and one draw needn't show every extreme that they name: `teacher_entities`: Real-valued embeddings. `student_entities`: Real-valued embeddings. `teacher_relations`: Real-valued embeddings. `student_relations`: Real-valued embeddings.
All inputs are finite; a program needn't handle non-finite values.
Results may differ from the reference program's by a relative error of at most 0.013.
Values may be sent and summed in bfloat16 or wider, within the bound.
No kernel may reach another device: no remote copies, remote signals or barrier semaphores. Data moves between devices by JAX's collectives and lax.ppermute only.
A program may use at most 128 MiB of HBM per device.

```python
import math
import jax
import jax.numpy as jnp
import numpy as np
from jax import lax

TW = 1000
SW = 128
REL = 4131
ENTITIES = 4096
QUERIES = 8192


def entity_table(key, width, sigma):
    first, second = jax.random.split(key, 2)
    third = jax.random.fold_in(key, 5)
    base = jax.random.truncated_normal(first, -4.0, 4.0, (ENTITIES, width), jnp.float32)
    scale = jnp.exp(jax.random.uniform(second, (ENTITIES, 1), jnp.float32, math.log(0.5), math.log(2.0)))
    table = base * scale * sigma
    fresh = jax.random.truncated_normal(third, -4.0, 4.0, (ENTITIES, width), jnp.float32) * sigma
    pairs = table.reshape(ENTITIES // 2, 2, width)
    noise = fresh.reshape(ENTITIES // 2, 2, width)
    partner = 0.985 * pairs[:, 0, :] + 0.3 * noise[:, 1, :]
    joined = jnp.stack([pairs[:, 0, :], partner], axis=1)
    return joined.reshape(ENTITIES, width)


def relation_table(key, width, per_entry, chance):
    half = width // 2
    first, second, third = jax.random.split(key, 3)
    base = jax.random.truncated_normal(first, -6.0, 6.0, (REL, width), jnp.float32) * 1.5
    strong = jax.random.bernoulli(second, chance, (REL, 1)).astype(jnp.float32)
    strength = jax.random.uniform(third, (REL, 1), jnp.float32, 1.0, 3.0)
    offset = strong * strength * (150.0 / (half * per_entry))
    columns = (jnp.arange(width)[None, :] < half).astype(jnp.float32)
    return base + offset * columns


def draw_teacher_entities(key, part):
    return entity_table(jax.random.fold_in(key, 11), TW, 0.12).astype(jnp.bfloat16)


def draw_student_entities(key, part):
    return entity_table(jax.random.fold_in(key, 23), SW, 0.22).astype(jnp.bfloat16)


def draw_teacher_relations(key, part):
    key = jax.random.fold_in(key, 37)
    chance = 0.0
    return relation_table(key, TW, 0.039, chance).astype(jnp.bfloat16)


def draw_student_relations(key, part):
    key = jax.random.fold_in(key, 41)
    chance = 0.0
    return relation_table(key, SW, 0.131, chance).astype(jnp.bfloat16)


def set_ends(drawn, rng, least, top_value):
    longest = drawn.shape.index(max(drawn.shape))
    spots = []
    for shift in (0, 1):
        where = [jax.random.randint(jax.random.fold_in(rng, axis), (), 0, length) for axis, length in enumerate(drawn.shape)]
        where[longest] = (where[longest] + shift) % drawn.shape[longest]
        spots.append(tuple(where))
    return drawn.at[spots[0]].set(least).at[spots[1]].set(top_value)


def rank_bounds(count, slope):
    portions = [(1 << 20) // math.isqrt(rank ** slope) + 1 for rank in range(1, count + 1)]
    spread = 1 + sum(portions) // (1 << 30)
    return np.cumsum(np.array([max(1, weight // spread) for weight in portions]))


def ranked_ids(rng, shape, number_of, skew):
    table = rank_bounds(number_of, skew)
    lot = jax.random.randint(jax.random.fold_in(rng, 1), shape, 0, int(table[number_of - 1]))
    rank = jnp.searchsorted(jnp.asarray(table, jnp.int32), lot, side="right")
    return jax.random.permutation(jax.random.fold_in(rng, 2), number_of)[rank].astype(jnp.int32)


def setup_inputs(seed: int = 0) -> dict:
    key_list = jax.random.split(jax.random.key(seed), 8)
    anchor_ids = set_ends(jax.random.randint(key_list[0], (QUERIES,), 0, ENTITIES), jax.random.fold_in(key_list[0], 1), 0, ENTITIES - 1).astype(jnp.int32)
    relation_ids = set_ends(ranked_ids(key_list[1], (QUERIES,), REL, 2), jax.random.fold_in(key_list[1], 3), 0, REL - 1).astype(jnp.int32)
    side_flags = set_ends(jax.random.randint(key_list[2], (QUERIES,), 0, 2), jax.random.fold_in(key_list[2], 1), 0, 1).astype(jnp.int32)
    teacher_entities = draw_teacher_entities(jax.random.fold_in(key_list[7], 71), 0)
    student_entities = draw_student_entities(jax.random.fold_in(key_list[7], 71), 0)
    teacher_relations = draw_teacher_relations(jax.random.fold_in(key_list[7], 71), 0)
    student_relations = draw_student_relations(jax.random.fold_in(key_list[7], 71), 0)
    return dict(anchor_ids=anchor_ids, relation_ids=relation_ids, side_flags=side_flags, teacher_entities=teacher_entities, student_entities=student_entities, teacher_relations=teacher_relations, student_relations=student_relations)


def query_vectors(anchor, relation, flags):
    half = anchor.shape[1] // 2
    sign = (2 * flags - 1).astype(jnp.float32)[:, None]
    a_re = anchor[:, :half]
    a_im = anchor[:, half:]
    r_re = relation[:, :half]
    r_im = relation[:, half:]
    real = a_re * r_re - sign * a_im * r_im
    imag = a_im * r_re + sign * a_re * r_im
    return jnp.concatenate([real, imag], axis=1).astype(jnp.bfloat16)


def reference(anchor_ids, relation_ids, side_flags, teacher_entities, student_entities, teacher_relations, student_relations):
    query_teacher = query_vectors(teacher_entities[anchor_ids].astype(jnp.float32), teacher_relations[relation_ids].astype(jnp.float32), side_flags)
    query_student = query_vectors(student_entities[anchor_ids].astype(jnp.float32), student_relations[relation_ids].astype(jnp.float32), side_flags)
    width = min(256, QUERIES)
    count = QUERIES // width
    teacher_blocks = query_teacher.reshape(count, width, TW)
    student_blocks = query_student.reshape(count, width, SW)

    def step(grad_total, items):
        q_teacher, q_student = items
        t = jnp.dot(q_teacher, teacher_entities.T, preferred_element_type=jnp.float32)
        s = jnp.dot(q_student, student_entities.T, preferred_element_type=jnp.float32)
        top_t = jnp.max(t, axis=1)
        top_s = jnp.max(s, axis=1)
        total_t = jnp.sum(jnp.exp(t - top_t[:, None]), axis=1)
        total_s = jnp.sum(jnp.exp(s - top_s[:, None]), axis=1)
        prob_t = jnp.exp(t - top_t[:, None]) / total_t[:, None]
        prob_s = jnp.exp(s - top_s[:, None]) / total_s[:, None]
        diverge = jnp.sum(prob_t * (t - s), axis=1) - top_t - jnp.log(total_t) + top_s + jnp.log(total_s)
        weights = (prob_s - prob_t).astype(jnp.bfloat16)
        grad_total = grad_total + jnp.dot(weights.T, q_student, preferred_element_type=jnp.float32)
        q_grad = jnp.dot(weights, student_entities, preferred_element_type=jnp.float32)
        return grad_total, (diverge, q_grad)

    start = jnp.zeros((ENTITIES, SW), jnp.float32)
    entity_grad, (diverge, q_grad) = lax.scan(step, start, (teacher_blocks, student_blocks))
    return diverge.reshape(QUERIES), entity_grad, q_grad.reshape(QUERIES, SW)
```

```python
import jax
import jax.numpy as jnp
import numpy as np
from jax import lax
from jax.sharding import PartitionSpec as P


def query_vectors(anchor, relation, flags):
    half = anchor.shape[1] // 2
    sign = (2 * flags - 1).astype(jnp.float32)[:, None]
    a_re = anchor[:, :half]
    a_im = anchor[:, half:]
    r_re = relation[:, :half]
    r_im = relation[:, half:]
    real = a_re * r_re - sign * a_im * r_im
    imag = a_im * r_re + sign * a_re * r_im
    return jnp.concatenate([real, imag], axis=1).astype(jnp.bfloat16)


def places(n):
    sides = 2 if n % 2 == 0 else 1
    m = n // sides
    order = list(range(m))
    if m % 2 == 0:
        order = [2 * z for z in range(m // 2)] + [2 * z + 1 for z in reversed(range(m // 2))]
    return [[order[p] * sides + x for x in range(sides)] for p in range(m)]


def spread_steps(m, across):
    held = [(0, 0)]
    steps = []
    while len(held) < m * (2 if across else 1):
        taken = []
        for shift in (1, -1, 0):
            if shift == 0 and not across:
                continue
            if shift:
                found = [((k, o), (k, (o + shift) % m)) for k, o in held]
            else:
                found = [((k, o), (1 - k, o)) for k, o in held]
            names = [t[2] for t in taken]
            found = [f for f in found if f[1] not in held and f[1] not in names]
            if found:
                best = min(found, key=lambda f: (f[1][0], -min(f[1][1], m - f[1][1]), f[1][1]))
                taken.append((shift,) + best)
        held += [t[2] for t in taken]
        steps.append(taken)
    return steps, held


def move(x, place, shift):
    m = len(place)
    pairs = []
    for p in range(m):
        for side in range(len(place[0])):
            source = place[(p + shift) % m][side] if shift else place[p][1 - side]
            pairs.append((source, place[p][side]))
    return lax.ppermute(x, "query", sorted(pairs))


def spread(x, n):
    place = places(n)
    m, sides = len(place), len(place[0])
    steps, held = spread_steps(m, sides == 2)
    have = {(0, 0): x}
    for step in steps:
        got = {new: move(have[old], place, shift) for shift, old, new in step}
        have.update(got)
    owner = np.zeros((n, n), np.int32)
    slot_of = np.zeros((n, n), np.int32)
    for p in range(m):
        for side in range(sides):
            me = place[p][side]
            for slot, (k, o) in enumerate(held):
                other = place[(p + o) % m][side ^ k]
                owner[me, slot] = other
                slot_of[me, other] = slot
    return [have[h] for h in held], owner, slot_of


def pair_moves(x, size, op):
    if size & (size - 1):
        return lax.psum(x, "entity") if op == "sum" else lax.pmax(x, "entity")
    far = 1
    while far < size:
        y = lax.ppermute(x, "entity", [(i, i ^ far) for i in range(size)])
        x = x + y if op == "sum" else jnp.maximum(x, y)
        far *= 2
    return x


def make(n, groups):
    def per_device(
        anchor_ids,
        relation_ids,
        side_flags,
        teacher_entities,
        student_entities,
        teacher_relations,
        student_relations,
    ):
        own, tw = teacher_entities.shape
        sw = student_entities.shape[1]
        slab = own * n
        packed = jnp.concatenate([student_entities, teacher_entities], axis=1)
        shards, owner, slot_of = spread(packed, n)
        me = lax.axis_index("query")
        my_slots = jnp.asarray(slot_of)[me]
        offset = lax.axis_index("entity") * slab
        local = anchor_ids - offset
        inside = ((local >= 0) & (local < slab))[:, None]
        safe = jnp.clip(local, 0, slab - 1)
        rows = jnp.take(my_slots, safe // own) * own + safe % own
        table = jnp.concatenate(shards, axis=0)
        part = jnp.where(inside, jnp.take(table, rows, axis=0), 0).astype(jnp.bfloat16)
        anchor = pair_moves(part, groups, "sum").astype(jnp.float32)
        query_teacher = query_vectors(
            anchor[:, sw:], jnp.take(teacher_relations, relation_ids, axis=0).astype(jnp.float32), side_flags
        )
        query_student = query_vectors(
            anchor[:, :sw], jnp.take(student_relations, relation_ids, axis=0).astype(jnp.float32), side_flags
        )
        t = jnp.dot(query_teacher, table[:, sw:].T, preferred_element_type=jnp.float32)
        s = jnp.dot(query_student, table[:, :sw].T, preferred_element_type=jnp.float32)
        top_t = jnp.max(t, axis=1)
        top_s = jnp.max(s, axis=1)
        best = pair_moves(jnp.stack([top_t, top_s]), groups, "max")
        top_t, top_s = best[0], best[1]
        expo_t = jnp.exp(t - top_t[:, None])
        expo_s = jnp.exp(s - top_s[:, None])
        sums = jnp.stack([jnp.sum(expo_t, axis=1), jnp.sum(expo_t * (t - s), axis=1), jnp.sum(expo_s, axis=1)])
        sums = pair_moves(sums, groups, "sum")
        total_t, weighted, total_s = sums[0], sums[1], sums[2]
        divergence = weighted / total_t - top_t - jnp.log(total_t) + top_s + jnp.log(total_s)
        weights = (expo_s / total_s[:, None] - expo_t / total_t[:, None]).astype(jnp.bfloat16)
        grad = jnp.dot(weights.T, query_student, preferred_element_type=jnp.float32)
        grad = jnp.take(grad.astype(jnp.bfloat16).reshape(n, own, sw), my_slots, axis=0)
        pieces = lax.all_to_all(grad, "query", 0, 0)
        entity_grad = jnp.sum(pieces.astype(jnp.float32), axis=0)
        q_grad = jnp.dot(weights, table[:, :sw], preferred_element_type=jnp.float32)
        query_grad = pair_moves(q_grad, groups, "sum")
        return (divergence, entity_grad, query_grad)

    return per_device


def solution(mesh):
    in_specs = (
        P("query"),
        P("query"),
        P("query"),
        P(("entity", "query"), None),
        P(("entity", "query"), None),
        P(),
        P(),
    )
    out_specs = (P("query"), P(("entity", "query"), None), P("query", None))
    return jax.shard_map(
        make(mesh.shape["query"], mesh.shape["entity"]),
        mesh=mesh, in_specs=in_specs, out_specs=out_specs, check_vma=False,
    )
```

```python
import functools

import jax
import jax.numpy as jnp
import numpy as np
from jax import lax
from jax.experimental import pallas as pl
from jax.experimental.pallas import tpu as pltpu
from jax.sharding import PartitionSpec as P

F32 = jnp.float32
BF16 = jnp.bfloat16
VMEM = pl.BlockSpec(memory_space=pltpu.VMEM)
SMEM = pl.BlockSpec(memory_space=pltpu.SMEM)
ANY = pl.BlockSpec(memory_space=pl.ANY)
MIB = 1 << 20


def places(n):
    sides = 2 if n % 2 == 0 else 1
    m = n // sides
    order = list(range(m))
    if m % 2 == 0:
        order = [2 * z for z in range(m // 2)] + [2 * z + 1 for z in reversed(range(m // 2))]
    return [[order[p] * sides + x for x in range(sides)] for p in range(m)]


def spread_steps(m, across):
    held = [(0, 0)]
    steps = []
    while len(held) < m * (2 if across else 1):
        taken = []
        for shift in (1, -1, 0):
            if shift == 0 and not across:
                continue
            if shift:
                found = [((k, o), (k, (o + shift) % m)) for k, o in held]
            else:
                found = [((k, o), (1 - k, o)) for k, o in held]
            names = [t[2] for t in taken]
            found = [f for f in found if f[1] not in held and f[1] not in names]
            if found:
                best = min(found, key=lambda f: (f[1][0], -min(f[1][1], m - f[1][1]), f[1][1]))
                taken.append((shift,) + best)
        held += [t[2] for t in taken]
        steps.append(taken)
    return steps, held


def move(x, place, shift):
    m = len(place)
    pairs = []
    for p in range(m):
        for side in range(len(place[0])):
            source = place[(p + shift) % m][side] if shift else place[p][1 - side]
            pairs.append((source, place[p][side]))
    return lax.ppermute(x, "query", sorted(pairs))


def owners(place, held, n):
    owner = np.zeros((n, n), np.int32)
    for p in range(len(place)):
        for side in range(len(place[0])):
            for slot, (k, o) in enumerate(held):
                owner[place[p][side], slot] = place[(p + o) % len(place)][side ^ k]
    return owner


def partner(x, size, far):
    return lax.ppermute(x, "entity", [(i, i ^ far) for i in range(size)])


class Shape:
    def __init__(self, tw, sw):
        self.tw, self.sw = tw, sw
        self.half = tw // 2
        self.wide = -(-self.half // 128) * 128
        self.re, self.im = sw, sw + self.wide
        self.total = sw + 2 * self.wide


def put_row(out, student, teacher, shape):
    out[:, : shape.sw] = student.astype(BF16)
    pad = jnp.zeros((teacher.shape[0], shape.wide - shape.half), F32)
    for start, at in ((0, shape.re), (shape.half, shape.im)):
        piece = teacher[:, start : start + shape.half]
        out[:, at : at + shape.wide] = jnp.concatenate([piece, pad], axis=1).astype(BF16)


def pack_kernel(shape, teacher_t, student, out):
    put_row(out, student[...].astype(F32), teacher_t[...].astype(F32).T, shape)


def pack(teacher, student, shape):
    return pl.pallas_call(
        functools.partial(pack_kernel, shape),
        out_shape=jax.ShapeDtypeStruct((teacher.shape[0], shape.total), BF16),
        in_specs=[VMEM, VMEM],
        out_specs=VMEM,
        name="pack_rows",
    )(teacher.T, student)


def relation_kernel(shape, first, rel, block, has_acc, ids, table_t, student, *rest):
    acc_in, (out, acc, acc_s) = (rest[0], rest[1:]) if has_acc else (None, rest)
    step = pl.program_id(0)
    base = (first + step) * block
    hot = (ids[...] - base == lax.broadcasted_iota(jnp.int32, (ids.shape[0], block), 1)).astype(F32).astype(BF16)
    lanes = lax.broadcasted_iota(jnp.int32, table_t.shape, 1)
    rows = lax.broadcasted_iota(jnp.int32, student.shape, 0)
    table = jnp.where(lanes < rel - base, table_t[...], jnp.zeros_like(table_t))
    small = jnp.where(rows < rel - base, student[...], jnp.zeros_like(student))
    part = lax.dot_general(hot, table, (((1,), (1,)), ((), ())), preferred_element_type=F32)
    part_s = jnp.dot(hot, small, preferred_element_type=F32)

    @pl.when(step == 0)
    def _():
        acc[...] = part
        acc_s[...] = part_s

    @pl.when(step > 0)
    def _():
        acc[...] += part
        acc_s[...] += part_s

    @pl.when(step == pl.num_programs(0) - 1)
    def _():
        put_row(out, acc_s[...], acc[...], shape)
        if has_acc:
            out[...] += acc_in[...]


def relation_rows(ids, table, student, acc, first, count, block, shape):
    rel, tw = table.shape
    q = ids.shape[0]
    whole = lambda i: (0, 0)
    operands = [ids, table.T, student]
    in_specs = [
        pl.BlockSpec((q, 1), whole),
        pl.BlockSpec((tw, block), lambda i: (0, first + i)),
        pl.BlockSpec((block, shape.sw), lambda i: (first + i, 0)),
    ]
    if acc is not None:
        operands.append(acc)
        in_specs.append(pl.BlockSpec((q, shape.total), whole))
    return pl.pallas_call(
        functools.partial(relation_kernel, shape, first, rel, block, acc is not None),
        grid=(count,),
        out_shape=jax.ShapeDtypeStruct((q, shape.total), BF16),
        in_specs=in_specs,
        out_specs=pl.BlockSpec((q, shape.total), whole),
        scratch_shapes=[pltpu.VMEM((q, tw), F32), pltpu.VMEM((q, shape.sw), F32)],
        compiler_params=pltpu.CompilerParams(vmem_limit_bytes=32 * MIB),
        cost_estimate=pl.CostEstimate(
            flops=2 * q * tw * block * count, bytes_accessed=2 * tw * block * count, transcendentals=0
        ),
        name="relation_rows",
    )(*operands)


def load_shards(shards, table, sems, own):
    copies = [
        pltpu.make_async_copy(shard, table.at[pl.ds(j * own, own)], sems.at[j]) for j, shard in enumerate(shards)
    ]
    for copy in copies:
        copy.start()
    return copies


def anchor_kernel(count, own, has_acc, bases, ids, *rest):
    acc_in, rest = (rest[0], rest[1:]) if has_acc else (None, rest)
    shards, (out, table, hot, sems) = rest[:count], rest[count:]
    copies = load_shards(shards, table, sems, own)
    q = ids.shape[0]
    lane = lax.broadcasted_iota(jnp.int32, (q, own), 1)
    for j in range(count):
        hot[:, j * own : (j + 1) * own] = (ids[...] - bases[j] == lane).astype(F32).astype(BF16)
    for copy in copies:
        copy.wait()
    found = jnp.dot(hot[...], table[...], preferred_element_type=F32).astype(BF16)
    out[...] = found + acc_in[...] if has_acc else found


def anchor_rows(bases, ids, shards, acc, shape):
    own = shards[0].shape[0]
    q, count = ids.shape[0], len(shards)
    operands = [bases, ids] + ([] if acc is None else [acc]) + list(shards)
    return pl.pallas_call(
        functools.partial(anchor_kernel, count, own, acc is not None),
        out_shape=jax.ShapeDtypeStruct((q, shape.total), BF16),
        in_specs=[SMEM, VMEM] + ([] if acc is None else [VMEM]) + [ANY] * count,
        out_specs=VMEM,
        scratch_shapes=[
            pltpu.VMEM((count * own, shape.total), BF16),
            pltpu.VMEM((q, count * own), BF16),
            pltpu.SemaphoreType.DMA((count,)),
        ],
        compiler_params=pltpu.CompilerParams(vmem_limit_bytes=40 * MIB),
        cost_estimate=pl.CostEstimate(
            flops=2 * q * count * own * shape.total,
            bytes_accessed=2 * (count * own + 2 * q) * shape.total,
            transcendentals=0,
        ),
        name="anchor_rows",
    )(*operands)


def score_kernel(shape, own, n, chunk, mine, other, relation, flags, *rest):
    shards, (t_out, s_out, stats, q_student, table, q_teacher, sems) = rest[:n], rest[n:]
    copies = load_shards(shards, table, sems, own)
    q = mine.shape[0]
    sw, wide = shape.sw, shape.wide
    rows = 128

    def build(i, _):
        at = pl.ds(pl.multiple_of(i * rows, rows), rows)
        g = (2 * flags[at, :] - 1).astype(F32)
        a = mine[at, :].astype(F32) + other[at, :].astype(F32)
        r = relation[at, :].astype(F32)
        a_re, a_im = a[:, shape.re : shape.re + wide], a[:, shape.im : shape.im + wide]
        r_re, r_im = r[:, shape.re : shape.re + wide], r[:, shape.im : shape.im + wide]
        q_teacher[at, :wide] = (a_re * r_re - g * a_im * r_im).astype(BF16)
        q_teacher[at, wide:] = (a_im * r_re + g * a_re * r_im).astype(BF16)
        a_s, r_s = a[:, :sw], r[:, :sw]
        a_x, r_x = pltpu.roll(a_s, sw // 2, 1), pltpu.roll(r_s, sw // 2, 1)
        low = lax.broadcasted_iota(jnp.int32, (rows, sw), 1) < sw // 2
        re2, im2 = jnp.where(low, r_s, r_x), jnp.where(low, r_x, r_s)
        q_student[at, :] = (a_s * re2 + jnp.where(low, -g, g) * a_x * im2).astype(BF16)
        return 0

    lax.fori_loop(0, q // rows, build, 0)
    for copy in copies:
        copy.wait()

    dims = (((1,), (1,)), ((), ()))

    def score(c, carry):
        top_t, total_t, weighted, top_s, total_s = carry
        at = pl.ds(pl.multiple_of(c * chunk, chunk), chunk)
        t = lax.dot_general(table[at, sw:], q_teacher[...], dims, preferred_element_type=F32)
        s = lax.dot_general(table[at, :sw], q_student[...], dims, preferred_element_type=F32)
        t_out[at, :] = t
        s_out[at, :] = s
        new_t = jnp.maximum(top_t, jnp.max(t, axis=0, keepdims=True))
        new_s = jnp.maximum(top_s, jnp.max(s, axis=0, keepdims=True))
        scale_t, scale_s = jnp.exp(top_t - new_t), jnp.exp(top_s - new_s)
        e = jnp.exp(t - new_t)
        total_t = total_t * scale_t + jnp.sum(e, axis=0, keepdims=True)
        weighted = weighted * scale_t + jnp.sum(e * (t - s), axis=0, keepdims=True)
        total_s = total_s * scale_s + jnp.sum(jnp.exp(s - new_s), axis=0, keepdims=True)
        return new_t, total_t, weighted, new_s, total_s

    lowest = jnp.full((1, q), -jnp.inf, F32)
    nothing = jnp.zeros((1, q), F32)
    found = lax.fori_loop(0, n * own // chunk, score, (lowest, nothing, nothing, lowest, nothing))
    stats[...] = jnp.concatenate(list(found) + [nothing] * 3, axis=0)


def scores(mine, other, relation, flags, shards, shape):
    n, own = len(shards), shards[0].shape[0]
    q = mine.shape[0]
    slab = n * own
    chunk = 512 if slab % 512 == 0 else own
    return pl.pallas_call(
        functools.partial(score_kernel, shape, own, n, chunk),
        out_shape=(
            jax.ShapeDtypeStruct((slab, q), F32),
            jax.ShapeDtypeStruct((slab, q), F32),
            jax.ShapeDtypeStruct((8, q), F32),
            jax.ShapeDtypeStruct((q, shape.sw), BF16),
        ),
        in_specs=[VMEM] * 4 + [ANY] * n,
        out_specs=(VMEM,) * 4,
        scratch_shapes=[
            pltpu.VMEM((slab, shape.total), BF16),
            pltpu.VMEM((q, 2 * shape.wide), BF16),
            pltpu.SemaphoreType.DMA((n,)),
        ],
        compiler_params=pltpu.CompilerParams(vmem_limit_bytes=44 * MIB),
        cost_estimate=pl.CostEstimate(
            flops=2 * q * slab * shape.total, bytes_accessed=2 * slab * shape.total + 8 * slab * q, transcendentals=2 * slab * q
        ),
        name="scores",
    )(mine, other, relation, flags, *shards)


def combine(a, b):
    top_t, top_s = jnp.maximum(a[0:1], b[0:1]), jnp.maximum(a[3:4], b[3:4])
    at, bt = jnp.exp(a[0:1] - top_t), jnp.exp(b[0:1] - top_t)
    as_, bs = jnp.exp(a[3:4] - top_s), jnp.exp(b[3:4] - top_s)
    total_t = a[1:2] * at + b[1:2] * bt
    weighted = a[2:3] * at + b[2:3] * bt
    total_s = a[4:5] * as_ + b[4:5] * bs
    return top_t, total_t, weighted, top_s, total_s


def grad_kernel(n, own, chunk, sw, owner, t_in, s_in, mine, other, q_student, *rest):
    shards, (divergence, e_grad, q_grad, table, sems) = rest[:n], rest[n:]
    copies = [
        pltpu.make_async_copy(shard.at[:, pl.ds(0, sw)], table.at[pl.ds(j * own, own)], sems.at[j])
        for j, shard in enumerate(shards)
    ]
    for copy in copies:
        copy.start()
    top_t, total_t, weighted, top_s, total_s = combine(mine[...], other[...])
    divergence[...] = weighted / total_t - top_t - jnp.log(total_t) + top_s + jnp.log(total_s)
    over_t, over_s = 1.0 / total_t, 1.0 / total_s
    for copy in copies:
        copy.wait()
    per = chunk // own

    def step(c, total):
        at = pl.ds(pl.multiple_of(c * chunk, chunk), chunk)
        prob_t = jnp.exp(t_in[at, :] - top_t) * over_t
        prob_s = jnp.exp(s_in[at, :] - top_s) * over_s
        weights = (prob_s - prob_t).astype(BF16)
        grad = jnp.dot(weights, q_student[...], preferred_element_type=F32).astype(BF16)
        for k in range(per):
            e_grad[owner[c * per + k]] = grad[k * own : (k + 1) * own, :]
        return total + lax.dot_general(
            table[at, :], weights, (((0,), (0,)), ((), ())), preferred_element_type=F32
        )

    q = q_student.shape[0]
    total = lax.fori_loop(0, n * own // chunk, step, jnp.zeros((sw, q), F32))
    q_grad[...] = total.T


def gradients(owner, t, s, mine, other, q_student, shards):
    n, own = len(shards), shards[0].shape[0]
    q, sw = q_student.shape
    slab = n * own
    chunk = 512 if slab % 512 == 0 else own
    return pl.pallas_call(
        functools.partial(grad_kernel, n, own, chunk, sw),
        out_shape=(
            jax.ShapeDtypeStruct((1, q), F32),
            jax.ShapeDtypeStruct((n, own, sw), BF16),
            jax.ShapeDtypeStruct((q, sw), F32),
        ),
        in_specs=[SMEM] + [VMEM] * 5 + [ANY] * n,
        out_specs=(VMEM,) * 3,
        scratch_shapes=[pltpu.VMEM((slab, sw), BF16), pltpu.SemaphoreType.DMA((n,))],
        compiler_params=pltpu.CompilerParams(vmem_limit_bytes=40 * MIB),
        cost_estimate=pl.CostEstimate(
            flops=4 * q * slab * sw, bytes_accessed=8 * slab * q, transcendentals=2 * slab * q
        ),
        name="gradients",
    )(owner, t, s, mine, other, q_student, *shards)


def make(n, groups):
    place = places(n)
    steps, held = spread_steps(len(place), len(place[0]) == 2)
    table = owners(place, held, n)

    def per_device(
        anchor_ids,
        relation_ids,
        side_flags,
        teacher_entities,
        student_entities,
        teacher_relations,
        student_relations,
    ):
        own, tw = teacher_entities.shape
        shape = Shape(tw, student_entities.shape[1])
        owner = jnp.asarray(table)[lax.axis_index("query")]
        bases = (owner + lax.axis_index("entity") * n) * own
        ids = anchor_ids[:, None]
        rel_ids = relation_ids[:, None]

        have = {(0, 0): pack(teacher_entities, student_entities, shape)}
        block = 768
        blocks = -(-teacher_relations.shape[0] // block)
        calls = min(3, len(steps))
        per_call = -(-blocks // calls)
        relation = None
        early = None
        for number, step in enumerate(steps):
            got = {new: move(have[old], place, shift) for shift, old, new in step}
            first = number * per_call
            if first < blocks:
                relation = relation_rows(
                    rel_ids, teacher_relations, student_relations, relation,
                    first, min(per_call, blocks - first), block, shape,
                )
            if number == len(steps) - 1:
                early = anchor_rows(bases, ids, [have[h] for h in held[: len(have)]], None, shape)
            count = len(have)
            have.update(got)
        shards = [have[h] for h in held]
        mine = anchor_rows(bases[count:], ids, shards[count:], early, shape)
        far = 1
        while far < groups // 2:
            mine = mine + partner(mine, groups, far)
            far *= 2
        other = partner(mine, groups, far)
        t, s, stats, q_student = scores(mine, other, relation, side_flags[:, None], shards, shape)
        far = 1
        while far < groups // 2:
            found = combine(stats, partner(stats, groups, far))
            stats = jnp.concatenate(list(found) + [jnp.zeros_like(found[0])] * 3, axis=0)
            far *= 2
        divergence, grad, q_grad = gradients(owner, t, s, stats, partner(stats, groups, far), q_student, shards)
        pieces = lax.all_to_all(grad, "query", 0, 0)
        entity_grad = jnp.sum(pieces.astype(F32), axis=0)
        far = 1
        while far < groups:
            q_grad = q_grad + partner(q_grad, groups, far)
            far *= 2
        return (divergence[0], entity_grad, q_grad)

    return per_device


def solution(mesh):
    in_specs = (
        P("query"),
        P("query"),
        P("query"),
        P(("entity", "query"), None),
        P(("entity", "query"), None),
        P(),
        P(),
    )
    out_specs = (P("query"), P(("entity", "query"), None), P("query", None))
    return jax.shard_map(
        make(mesh.shape["query"], mesh.shape["entity"]),
        mesh=mesh, in_specs=in_specs, out_specs=out_specs, check_vma=False,
    )
```

```python
import functools

import jax
import jax.numpy as jnp
import numpy as np
from jax import lax
from jax.experimental import pallas as pl
from jax.experimental.pallas import tpu as pltpu
from jax.sharding import PartitionSpec as P

F32 = jnp.float32
BF16 = jnp.bfloat16
VMEM = pl.BlockSpec(memory_space=pltpu.VMEM)
SMEM = pl.BlockSpec(memory_space=pltpu.SMEM)
ANY = pl.BlockSpec(memory_space=pl.ANY)
MIB = 1 << 20


def places(n):
    sides = 2 if n % 2 == 0 else 1
    m = n // sides
    order = list(range(m))
    if m % 2 == 0:
        order = [2 * z for z in range(m // 2)] + [2 * z + 1 for z in reversed(range(m // 2))]
    return [[order[p] * sides + x for x in range(sides)] for p in range(m)]


def spread_steps(m, across):
    held = [(0, 0)]
    steps = []
    while len(held) < m * (2 if across else 1):
        taken = []
        for shift in (1, -1, 0):
            if shift == 0 and not across:
                continue
            if shift:
                found = [((k, o), (k, (o + shift) % m)) for k, o in held]
            else:
                found = [((k, o), (1 - k, o)) for k, o in held]
            names = [t[2] for t in taken]
            found = [f for f in found if f[1] not in held and f[1] not in names]
            if found:
                best = min(found, key=lambda f: (f[1][0], -min(f[1][1], m - f[1][1]), f[1][1]))
                taken.append((shift,) + best)
        held += [t[2] for t in taken]
        steps.append(taken)
    return steps, held


def move(x, place, shift):
    m = len(place)
    pairs = []
    for p in range(m):
        for side in range(len(place[0])):
            source = place[(p + shift) % m][side] if shift else place[p][1 - side]
            pairs.append((source, place[p][side]))
    return lax.ppermute(x, "query", sorted(pairs))


def owners(place, held, n):
    owner = np.zeros((n, n), np.int32)
    for p in range(len(place)):
        for side in range(len(place[0])):
            for slot, (k, o) in enumerate(held):
                owner[place[p][side], slot] = place[(p + o) % len(place)][side ^ k]
    return owner


def partner(x, size, far):
    return lax.ppermute(x, "entity", [(i, i ^ far) for i in range(size)])


class Shape:
    def __init__(self, tw, sw):
        self.tw, self.sw = tw, sw
        self.half = tw // 2
        self.wide = -(-self.half // 128) * 128
        self.re, self.im = sw, sw + self.wide
        self.total = sw + 2 * self.wide


def put_row(out, student, teacher, shape):
    out[:, : shape.sw] = student.astype(BF16)
    pad = jnp.zeros((teacher.shape[0], shape.wide - shape.half), F32)
    for start, at in ((0, shape.re), (shape.half, shape.im)):
        piece = teacher[:, start : start + shape.half]
        out[:, at : at + shape.wide] = jnp.concatenate([piece, pad], axis=1).astype(BF16)


def pack_kernel(shape, teacher_t, student, out):
    put_row(out, student[...].astype(F32), teacher_t[...].astype(F32).T, shape)


def pack(teacher, student, shape):
    return pl.pallas_call(
        functools.partial(pack_kernel, shape),
        out_shape=jax.ShapeDtypeStruct((teacher.shape[0], shape.total), BF16),
        in_specs=[VMEM, VMEM],
        out_specs=VMEM,
        name="pack_rows",
    )(teacher.T, student)


def relation_kernel(shape, first, rel, block, edge, has_acc, ids, table_t, student, *rest):
    acc_in, (out, acc, acc_s) = (rest[0], rest[1:]) if has_acc else (None, rest)
    step = pl.program_id(0)
    base = (first + step) * block
    hot = (ids[...] - base == lax.broadcasted_iota(jnp.int32, (ids.shape[0], block), 1)).astype(F32).astype(BF16)
    table, small = table_t[...], student[...]
    if edge:
        lanes = lax.broadcasted_iota(jnp.int32, table_t.shape, 1)
        rows = lax.broadcasted_iota(jnp.int32, student.shape, 0)
        table = jnp.where(lanes < rel - base, table, jnp.zeros_like(table))
        small = jnp.where(rows < rel - base, small, jnp.zeros_like(small))
    part = lax.dot_general(hot, table, (((1,), (1,)), ((), ())), preferred_element_type=F32)
    part_s = jnp.dot(hot, small, preferred_element_type=F32)

    @pl.when(step == 0)
    def _():
        acc[...] = part
        acc_s[...] = part_s

    @pl.when(step > 0)
    def _():
        acc[...] += part
        acc_s[...] += part_s

    @pl.when(step == pl.num_programs(0) - 1)
    def _():
        put_row(out, acc_s[...], acc[...], shape)
        if has_acc:
            out[...] += acc_in[...]


def relation_rows(ids, table, student, acc, first, count, block, shape):
    rel, tw = table.shape
    q = ids.shape[0]
    whole = lambda i: (0, 0)
    operands = [ids, table.T, student]
    in_specs = [
        pl.BlockSpec((q, 1), whole),
        pl.BlockSpec((tw, block), lambda i: (0, first + i)),
        pl.BlockSpec((block, shape.sw), lambda i: (first + i, 0)),
    ]
    if acc is not None:
        operands.append(acc)
        in_specs.append(pl.BlockSpec((q, shape.total), whole))
    return pl.pallas_call(
        functools.partial(relation_kernel, shape, first, rel, block, (first + count) * block > rel, acc is not None),
        grid=(count,),
        out_shape=jax.ShapeDtypeStruct((q, shape.total), BF16),
        in_specs=in_specs,
        out_specs=pl.BlockSpec((q, shape.total), whole),
        scratch_shapes=[pltpu.VMEM((q, tw), F32), pltpu.VMEM((q, shape.sw), F32)],
        compiler_params=pltpu.CompilerParams(vmem_limit_bytes=56 * MIB),
        cost_estimate=pl.CostEstimate(
            flops=2 * q * tw * block * count, bytes_accessed=2 * tw * block * count, transcendentals=0
        ),
        name="relation_rows",
    )(*operands)


def load_shards(shards, table, sems, own):
    copies = [
        pltpu.make_async_copy(shard, table.at[pl.ds(j * own, own)], sems.at[j]) for j, shard in enumerate(shards)
    ]
    for copy in copies:
        copy.start()
    return copies


def anchor_kernel(count, own, has_acc, bases, ids, *rest):
    acc_in, rest = (rest[0], rest[1:]) if has_acc else (None, rest)
    shards, (out, table, hot, sems) = rest[:count], rest[count:]
    copies = load_shards(shards, table, sems, own)
    q = ids.shape[0]
    lane = lax.broadcasted_iota(jnp.int32, (q, own), 1)
    for j in range(count):
        hot[:, j * own : (j + 1) * own] = (ids[...] - bases[j] == lane).astype(F32).astype(BF16)
    for copy in copies:
        copy.wait()
    found = jnp.dot(hot[...], table[...], preferred_element_type=F32).astype(BF16)
    out[...] = found + acc_in[...] if has_acc else found


def anchor_rows(bases, ids, shards, acc, shape):
    own = shards[0].shape[0]
    q, count = ids.shape[0], len(shards)
    operands = [bases, ids] + ([] if acc is None else [acc]) + list(shards)
    return pl.pallas_call(
        functools.partial(anchor_kernel, count, own, acc is not None),
        out_shape=jax.ShapeDtypeStruct((q, shape.total), BF16),
        in_specs=[SMEM, VMEM] + ([] if acc is None else [VMEM]) + [ANY] * count,
        out_specs=VMEM,
        scratch_shapes=[
            pltpu.VMEM((count * own, shape.total), BF16),
            pltpu.VMEM((q, count * own), BF16),
            pltpu.SemaphoreType.DMA((count,)),
        ],
        compiler_params=pltpu.CompilerParams(vmem_limit_bytes=40 * MIB),
        cost_estimate=pl.CostEstimate(
            flops=2 * q * count * own * shape.total,
            bytes_accessed=2 * (count * own + 2 * q) * shape.total,
            transcendentals=0,
        ),
        name="anchor_rows",
    )(*operands)


def score_kernel(shape, own, n, chunk, mine, other, relation, flags, *rest):
    shards, (t_out, s_out, stats, q_student, table, q_teacher, sems) = rest[:n], rest[n:]
    copies = load_shards(shards, table, sems, own)
    q = mine.shape[0]
    sw, wide = shape.sw, shape.wide
    rows = 128

    def build(i, _):
        at = pl.ds(pl.multiple_of(i * rows, rows), rows)
        g = (2 * flags[at, :] - 1).astype(F32)
        a = mine[at, :].astype(F32) + other[at, :].astype(F32)
        r = relation[at, :].astype(F32)
        a_re, a_im = a[:, shape.re : shape.re + wide], a[:, shape.im : shape.im + wide]
        r_re, r_im = r[:, shape.re : shape.re + wide], r[:, shape.im : shape.im + wide]
        q_teacher[at, :wide] = (a_re * r_re - g * a_im * r_im).astype(BF16)
        q_teacher[at, wide:] = (a_im * r_re + g * a_re * r_im).astype(BF16)
        a_s, r_s = a[:, :sw], r[:, :sw]
        a_x, r_x = pltpu.roll(a_s, sw // 2, 1), pltpu.roll(r_s, sw // 2, 1)
        low = lax.broadcasted_iota(jnp.int32, (rows, sw), 1) < sw // 2
        re2, im2 = jnp.where(low, r_s, r_x), jnp.where(low, r_x, r_s)
        q_student[at, :] = (a_s * re2 + jnp.where(low, -g, g) * a_x * im2).astype(BF16)
        return 0

    lax.fori_loop(0, q // rows, build, 0)
    for copy in copies:
        copy.wait()

    dims = (((1,), (1,)), ((), ()))

    def score(c, carry):
        top_t, total_t, weighted, top_s, total_s = carry
        at = pl.ds(pl.multiple_of(c * chunk, chunk), chunk)
        t = lax.dot_general(table[at, sw:], q_teacher[...], dims, preferred_element_type=F32)
        s = lax.dot_general(table[at, :sw], q_student[...], dims, preferred_element_type=F32)
        t_out[at, :] = t
        s_out[at, :] = s
        new_t = jnp.maximum(top_t, jnp.max(t, axis=0, keepdims=True))
        new_s = jnp.maximum(top_s, jnp.max(s, axis=0, keepdims=True))
        scale_t, scale_s = jnp.exp(top_t - new_t), jnp.exp(top_s - new_s)
        e = jnp.exp(t - new_t)
        total_t = total_t * scale_t + jnp.sum(e, axis=0, keepdims=True)
        weighted = weighted * scale_t + jnp.sum(e * (t - s), axis=0, keepdims=True)
        total_s = total_s * scale_s + jnp.sum(jnp.exp(s - new_s), axis=0, keepdims=True)
        return new_t, total_t, weighted, new_s, total_s

    lowest = jnp.full((1, q), -jnp.inf, F32)
    nothing = jnp.zeros((1, q), F32)
    found = lax.fori_loop(0, n * own // chunk, score, (lowest, nothing, nothing, lowest, nothing), unroll=True)
    stats[...] = jnp.concatenate(list(found) + [nothing] * 3, axis=0)


def scores(mine, other, relation, flags, shards, shape):
    n, own = len(shards), shards[0].shape[0]
    q = mine.shape[0]
    slab = n * own
    chunk = 512 if slab % 512 == 0 else own
    return pl.pallas_call(
        functools.partial(score_kernel, shape, own, n, chunk),
        out_shape=(
            jax.ShapeDtypeStruct((slab, q), F32),
            jax.ShapeDtypeStruct((slab, q), F32),
            jax.ShapeDtypeStruct((8, q), F32),
            jax.ShapeDtypeStruct((q, shape.sw), BF16),
        ),
        in_specs=[VMEM] * 4 + [ANY] * n,
        out_specs=(VMEM,) * 4,
        scratch_shapes=[
            pltpu.VMEM((slab, shape.total), BF16),
            pltpu.VMEM((q, 2 * shape.wide), BF16),
            pltpu.SemaphoreType.DMA((n,)),
        ],
        compiler_params=pltpu.CompilerParams(vmem_limit_bytes=8 * slab * q + 2 * slab * shape.total + 10 * MIB),
        cost_estimate=pl.CostEstimate(
            flops=2 * q * slab * shape.total, bytes_accessed=2 * slab * shape.total + 8 * slab * q, transcendentals=2 * slab * q
        ),
        name="scores",
    )(mine, other, relation, flags, *shards)


def combine(a, b):
    top_t, top_s = jnp.maximum(a[0:1], b[0:1]), jnp.maximum(a[3:4], b[3:4])
    at, bt = jnp.exp(a[0:1] - top_t), jnp.exp(b[0:1] - top_t)
    as_, bs = jnp.exp(a[3:4] - top_s), jnp.exp(b[3:4] - top_s)
    total_t = a[1:2] * at + b[1:2] * bt
    weighted = a[2:3] * at + b[2:3] * bt
    total_s = a[4:5] * as_ + b[4:5] * bs
    return top_t, total_t, weighted, top_s, total_s


def grad_kernel(n, own, chunk, sw, order, t_in, s_in, mine, other, q_student, *rest):
    shards, (divergence, q_grad), outs = rest[:n], rest[n : n + 2], rest[n + 2 : -3]
    table, e_grad, sems = rest[-3:]
    copies = [
        pltpu.make_async_copy(shard.at[:, pl.ds(0, sw)], table.at[pl.ds(j * own, own)], sems.at[j])
        for j, shard in enumerate(shards)
    ]
    for copy in copies:
        copy.start()
    top_t, total_t, weighted, top_s, total_s = combine(mine[...], other[...])
    divergence[...] = weighted / total_t - top_t - jnp.log(total_t) + top_s + jnp.log(total_s)
    over_t, over_s = 1.0 / total_t, 1.0 / total_s
    for copy in copies:
        copy.wait()
    per = chunk // own

    def step(c, total):
        at = pl.ds(pl.multiple_of(c * chunk, chunk), chunk)
        prob_t = jnp.exp(t_in[at, :] - top_t) * over_t
        prob_s = jnp.exp(s_in[at, :] - top_s) * over_s
        weights = (prob_s - prob_t).astype(BF16)
        grad = jnp.dot(weights, q_student[...], preferred_element_type=F32).astype(BF16)
        for k in range(per):
            e_grad[order[c * per + k]] = grad[k * own : (k + 1) * own, :]
        return total + lax.dot_general(
            table[at, :], weights, (((0,), (0,)), ((), ())), preferred_element_type=F32
        )

    q = q_student.shape[0]
    total = lax.fori_loop(0, n * own // chunk, step, jnp.zeros((sw, q), F32), unroll=True)
    q_grad[...] = total.T
    count = n // len(outs)
    for d, out in enumerate(outs):
        out[...] = e_grad[d * count : (d + 1) * count]


def gradients(order, near, t, s, mine, other, q_student, shards):
    n, own = len(shards), shards[0].shape[0]
    q, sw = q_student.shape
    slab = n * own
    chunk = 512 if slab % 512 == 0 else own
    return pl.pallas_call(
        functools.partial(grad_kernel, n, own, chunk, sw),
        out_shape=(
            jax.ShapeDtypeStruct((1, q), F32),
            jax.ShapeDtypeStruct((q, sw), F32),
        )
        + (jax.ShapeDtypeStruct((n // near, own, sw), BF16),) * near,
        in_specs=[SMEM] + [VMEM] * 5 + [ANY] * n,
        out_specs=(VMEM,) * (2 + near),
        scratch_shapes=[
            pltpu.VMEM((slab, sw), BF16),
            pltpu.VMEM((n, own, sw), BF16),
            pltpu.SemaphoreType.DMA((n,)),
        ],
        compiler_params=pltpu.CompilerParams(vmem_limit_bytes=8 * slab * q + 10 * MIB),
        cost_estimate=pl.CostEstimate(
            flops=4 * q * slab * sw, bytes_accessed=8 * slab * q, transcendentals=2 * slab * q
        ),
        name="gradients",
    )(order, t, s, mine, other, q_student, *shards)


def add_kernel(count, *refs):
    terms, outs = refs[:count], refs[count:]
    for e, out in enumerate(outs):
        total = terms[0][e].astype(F32)
        for term in terms[1:]:
            total += term[e].astype(F32)
        out[...] = total.astype(out.dtype)


def add_blocks(terms):
    far, own, sw = terms[0].shape
    return pl.pallas_call(
        functools.partial(add_kernel, len(terms)),
        out_shape=(jax.ShapeDtypeStruct((own, sw), F32),)
        + (jax.ShapeDtypeStruct((own, sw), BF16),) * (far - 1),
        in_specs=[VMEM] * len(terms),
        out_specs=(VMEM,) * far,
        name="add_blocks",
    )(*terms)


def reduce_blocks(blocks, n):
    near, far = len(blocks), n // len(blocks)
    terms = [blocks[0]]
    for d in range(1, near):
        terms.append(lax.ppermute(blocks[d], "query", [(i, i ^ d) for i in range(n)]))
    sums = add_blocks(terms)
    total = sums[0]
    for e in range(1, far):
        pairs = [(h * near + r, (h + e) % far * near + r) for h in range(far) for r in range(near)]
        total = total + lax.ppermute(sums[e], "query", pairs).astype(F32)
    return total


def make(n, groups):
    place = places(n)
    steps, held = spread_steps(len(place), len(place[0]) == 2)
    table = owners(place, held, n)
    near = next(k for k in (4, 2, 1) if n % k == 0)
    me = np.arange(n)[:, None]
    position = ((table % near) ^ (me % near)) * (n // near) + (table // near - me // near) % (n // near)

    def per_device(
        anchor_ids,
        relation_ids,
        side_flags,
        teacher_entities,
        student_entities,
        teacher_relations,
        student_relations,
    ):
        own, tw = teacher_entities.shape
        shape = Shape(tw, student_entities.shape[1])
        owner, order = jnp.asarray(np.stack([table, position], axis=1))[lax.axis_index("query")]
        bases = (owner + lax.axis_index("entity") * n) * own
        ids = anchor_ids[:, None]
        rel_ids = relation_ids[:, None]

        have = {(0, 0): pack(teacher_entities, student_entities, shape)}
        block = 768
        blocks = -(-teacher_relations.shape[0] // block)
        calls = min(3, len(steps))
        per_call = -(-blocks // calls)
        relation = None
        early = None
        for number, step in enumerate(steps):
            got = {new: move(have[old], place, shift) for shift, old, new in step}
            first = number * per_call
            if first < blocks:
                relation = relation_rows(
                    rel_ids, teacher_relations, student_relations, relation,
                    first, min(per_call, blocks - first), block, shape,
                )
                last = step[-1][2]
                got[last], relation = lax.optimization_barrier((got[last], relation))
            if number == len(steps) - 1:
                early = anchor_rows(bases, ids, [have[h] for h in held[: len(have)]], None, shape)
            count = len(have)
            have.update(got)
        shards = [have[h] for h in held]
        mine = anchor_rows(bases[count:], ids, shards[count:], early, shape)
        far = 1
        while far < groups // 2:
            mine = mine + partner(mine, groups, far)
            far *= 2
        other = partner(mine, groups, far)
        t, s, stats, q_student = scores(mine, other, relation, side_flags[:, None], shards, shape)
        far = 1
        while far < groups // 2:
            found = combine(stats, partner(stats, groups, far))
            stats = jnp.concatenate(list(found) + [jnp.zeros_like(found[0])] * 3, axis=0)
            far *= 2
        divergence, q_grad, *blocks = gradients(
            order, near, t, s, stats, partner(stats, groups, far), q_student, shards
        )
        entity_grad = reduce_blocks(blocks, n)
        far = 1
        while far < groups:
            q_grad = q_grad + partner(q_grad, groups, far)
            far *= 2
        return (divergence[0], entity_grad, q_grad)

    return per_device


def solution(mesh):
    in_specs = (
        P("query"),
        P("query"),
        P("query"),
        P(("entity", "query"), None),
        P(("entity", "query"), None),
        P(),
        P(),
    )
    out_specs = (P("query"), P(("entity", "query"), None), P("query", None))
    return jax.shard_map(
        make(mesh.shape["query"], mesh.shape["entity"]),
        mesh=mesh, in_specs=in_specs, out_specs=out_specs, check_vma=False,
    )
```

```python
import functools

import jax
import jax.numpy as jnp
import numpy as np
from jax import lax
from jax.experimental import pallas as pl
from jax.experimental.pallas import tpu as pltpu
from jax.sharding import PartitionSpec as P

F32 = jnp.float32
BF16 = jnp.bfloat16
VMEM = pl.BlockSpec(memory_space=pltpu.VMEM)
SMEM = pl.BlockSpec(memory_space=pltpu.SMEM)
ANY = pl.BlockSpec(memory_space=pl.ANY)
MIB = 1 << 20


def places(n):
    sides = 2 if n % 2 == 0 else 1
    m = n // sides
    order = list(range(m))
    if m % 2 == 0:
        order = [2 * z for z in range(m // 2)] + [2 * z + 1 for z in reversed(range(m // 2))]
    return [[order[p] * sides + x for x in range(sides)] for p in range(m)]


def spread_steps(m, across):
    held = [(0, 0)]
    steps = []
    while len(held) < m * (2 if across else 1):
        taken = []
        for shift in (1, -1, 0):
            if shift == 0 and not across:
                continue
            if shift:
                found = [((k, o), (k, (o + shift) % m)) for k, o in held]
            else:
                found = [((k, o), (1 - k, o)) for k, o in held]
            names = [t[2] for t in taken]
            found = [f for f in found if f[1] not in held and f[1] not in names]
            if found:
                best = min(found, key=lambda f: (f[1][0], -min(f[1][1], m - f[1][1]), f[1][1]))
                taken.append((shift,) + best)
        held += [t[2] for t in taken]
        steps.append(taken)
    return steps, held


def move(x, place, shift):
    m = len(place)
    pairs = []
    for p in range(m):
        for side in range(len(place[0])):
            source = place[(p + shift) % m][side] if shift else place[p][1 - side]
            pairs.append((source, place[p][side]))
    return lax.ppermute(x, "query", sorted(pairs))


def owners(place, held, n):
    owner = np.zeros((n, n), np.int32)
    for p in range(len(place)):
        for side in range(len(place[0])):
            for slot, (k, o) in enumerate(held):
                owner[place[p][side], slot] = place[(p + o) % len(place)][side ^ k]
    return owner


def partner(x, size, far):
    return lax.ppermute(x, "entity", [(i, i ^ far) for i in range(size)])


class Shape:
    def __init__(self, tw, sw):
        self.tw, self.sw = tw, sw
        self.half = tw // 2
        self.wide = -(-self.half // 128) * 128
        self.re, self.im = sw, sw + self.wide
        self.total = sw + 2 * self.wide


def put_row(out, student, teacher, shape):
    out[:, : shape.sw] = student.astype(BF16)
    pad = jnp.zeros((teacher.shape[0], shape.wide - shape.half), F32)
    for start, at in ((0, shape.re), (shape.half, shape.im)):
        piece = teacher[:, start : start + shape.half]
        out[:, at : at + shape.wide] = jnp.concatenate([piece, pad], axis=1).astype(BF16)


def pack_kernel(shape, teacher_t, student, out):
    put_row(out, student[...].astype(F32), teacher_t[...].astype(F32).T, shape)


def pack(teacher, student, shape):
    return pl.pallas_call(
        functools.partial(pack_kernel, shape),
        out_shape=jax.ShapeDtypeStruct((teacher.shape[0], shape.total), BF16),
        in_specs=[VMEM, VMEM],
        out_specs=VMEM,
        compiler_params=pltpu.CompilerParams(vmem_limit_bytes=8 * MIB),
        name="pack_rows",
    )(teacher.T, student)


def relation_kernel(shape, first, rel, block, last, base, cols, table_t, student, *rest):
    acc_in, acc_s_in = rest[:2] if len(rest) > (1 if last else 2) else (None, None)
    start = (base[0] + first) * block
    ids = cols[:, 1:2] - start
    hot = (ids == lax.broadcasted_iota(jnp.int32, (cols.shape[0], block), 1)).astype(F32).astype(BF16)
    lanes = lax.broadcasted_iota(jnp.int32, table_t.shape, 1)
    rows = lax.broadcasted_iota(jnp.int32, student.shape, 0)
    table = jnp.where(lanes < rel - start, table_t[...], jnp.zeros_like(table_t))
    small = jnp.where(rows < rel - start, student[...], jnp.zeros_like(student))
    part = lax.dot_general(hot, table, (((1,), (1,)), ((), ())), preferred_element_type=F32)
    part_s = jnp.dot(hot, small, preferred_element_type=F32)
    if acc_in is not None:
        part = part + acc_in[...].astype(F32)
        part_s = part_s + acc_s_in[...].astype(F32)
    if last:
        put_row(rest[-1], part_s, part, shape)
    else:
        rest[-2][...] = part.astype(BF16)
        rest[-1][...] = part_s.astype(BF16)


def relation_rows(base, cols, table, student, acc, first, block, last, shape):
    rel, tw = table.shape
    q = cols.shape[0]
    final = -(-rel // block) - 1
    whole = lambda i, base: (0, 0)
    in_specs = [
        pl.BlockSpec((q, cols.shape[1]), whole),
        pl.BlockSpec((tw, block), lambda i, base: (0, jnp.minimum(base[0] + first, final))),
        pl.BlockSpec((block, shape.sw), lambda i, base: (jnp.minimum(base[0] + first, final), 0)),
    ]
    widths = [shape.total] if last else [tw, shape.sw]
    acc = acc or []
    found = pl.pallas_call(
        functools.partial(relation_kernel, shape, first, rel, block, last),
        out_shape=[jax.ShapeDtypeStruct((q, w), BF16) for w in widths],
        grid_spec=pltpu.PrefetchScalarGridSpec(
            num_scalar_prefetch=1,
            grid=(1,),
            in_specs=in_specs + [pl.BlockSpec(x.shape, whole) for x in acc],
            out_specs=[pl.BlockSpec((q, w), whole) for w in widths],
        ),
        compiler_params=pltpu.CompilerParams(vmem_limit_bytes=28 * MIB),
        cost_estimate=pl.CostEstimate(
            flops=2 * q * tw * block, bytes_accessed=2 * tw * block, transcendentals=0
        ),
        name="relation_rows",
    )(base, cols, table.T, student, *acc)
    return list(found)


def load_shards(shards, table, sems, own):
    copies = [
        pltpu.make_async_copy(shard, table.at[pl.ds(j * own, own)], sems.at[j]) for j, shard in enumerate(shards)
    ]
    for copy in copies:
        copy.start()
    return copies


def anchor_kernel(count, own, has_acc, bases, cols, *rest):
    acc_in, rest = (rest[0], rest[1:]) if has_acc else (None, rest)
    shards, (out, table, hot, sems) = rest[:count], rest[count:]
    copies = load_shards(shards, table, sems, own)
    q = cols.shape[0]
    ids = cols[:, 0:1]
    lane = lax.broadcasted_iota(jnp.int32, (q, own), 1)
    for j in range(count):
        hot[:, j * own : (j + 1) * own] = (ids - bases[j] == lane).astype(F32).astype(BF16)
    for copy in copies:
        copy.wait()
    found = jnp.dot(hot[...], table[...], preferred_element_type=F32).astype(BF16)
    out[...] = found + acc_in[...] if has_acc else found


def anchor_rows(bases, ids, shards, acc, shape):
    own = shards[0].shape[0]
    q, count = ids.shape[0], len(shards)
    operands = [bases, ids] + ([] if acc is None else [acc]) + list(shards)
    return pl.pallas_call(
        functools.partial(anchor_kernel, count, own, acc is not None),
        out_shape=jax.ShapeDtypeStruct((q, shape.total), BF16),
        in_specs=[SMEM, VMEM] + ([] if acc is None else [VMEM]) + [ANY] * count,
        out_specs=VMEM,
        scratch_shapes=[
            pltpu.VMEM((count * own, shape.total), BF16),
            pltpu.VMEM((q, count * own), BF16),
            pltpu.SemaphoreType.DMA((count,)),
        ],
        compiler_params=pltpu.CompilerParams(vmem_limit_bytes=2 * count * own * (shape.total + q) + 12 * MIB),
        cost_estimate=pl.CostEstimate(
            flops=2 * q * count * own * shape.total,
            bytes_accessed=2 * (count * own + 2 * q) * shape.total,
            transcendentals=0,
        ),
        name="anchor_rows",
    )(*operands)


def score_kernel(shape, own, n, chunk, mine, other, relation, relation_b, cols, *rest):
    shards, (t_out, s_out, stats, q_student, table, q_teacher, sems) = rest[:n], rest[n:]
    copies = load_shards(shards, table, sems, own)
    q = mine.shape[0]
    sw, wide = shape.sw, shape.wide
    rows = 128

    def build(i, _):
        at = pl.ds(pl.multiple_of(i * rows, rows), rows)
        g = (2 * cols[at, 2:3] - 1).astype(F32)
        a = mine[at, :].astype(F32) + other[at, :].astype(F32)
        r = relation[at, :].astype(F32) + relation_b[at, :].astype(F32)
        a_re, a_im = a[:, shape.re : shape.re + wide], a[:, shape.im : shape.im + wide]
        r_re, r_im = r[:, shape.re : shape.re + wide], r[:, shape.im : shape.im + wide]
        q_teacher[at, :wide] = (a_re * r_re - g * a_im * r_im).astype(BF16)
        q_teacher[at, wide:] = (a_im * r_re + g * a_re * r_im).astype(BF16)
        a_s, r_s = a[:, :sw], r[:, :sw]
        a_x, r_x = pltpu.roll(a_s, sw // 2, 1), pltpu.roll(r_s, sw // 2, 1)
        low = lax.broadcasted_iota(jnp.int32, (rows, sw), 1) < sw // 2
        re2, im2 = jnp.where(low, r_s, r_x), jnp.where(low, r_x, r_s)
        q_student[at, :] = (a_s * re2 + jnp.where(low, -g, g) * a_x * im2).astype(BF16)
        return 0

    lax.fori_loop(0, q // rows, build, 0)
    for copy in copies:
        copy.wait()

    dims = (((1,), (1,)), ((), ()))

    def score(c, carry):
        top_t, total_t, weighted, top_s, total_s = carry
        at = pl.ds(pl.multiple_of(c * chunk, chunk), chunk)
        t = lax.dot_general(table[at, sw:], q_teacher[...], dims, preferred_element_type=F32)
        s = lax.dot_general(table[at, :sw], q_student[...], dims, preferred_element_type=F32)
        t_out[at, :] = t
        s_out[at, :] = s
        new_t = jnp.maximum(top_t, jnp.max(t, axis=0, keepdims=True))
        new_s = jnp.maximum(top_s, jnp.max(s, axis=0, keepdims=True))
        scale_t, scale_s = jnp.exp(top_t - new_t), jnp.exp(top_s - new_s)
        e = jnp.exp(t - new_t)
        total_t = total_t * scale_t + jnp.sum(e, axis=0, keepdims=True)
        weighted = weighted * scale_t + jnp.sum(e * (t - s), axis=0, keepdims=True)
        total_s = total_s * scale_s + jnp.sum(jnp.exp(s - new_s), axis=0, keepdims=True)
        return new_t, total_t, weighted, new_s, total_s

    lowest = jnp.full((1, q), -jnp.inf, F32)
    nothing = jnp.zeros((1, q), F32)
    found = lax.fori_loop(0, n * own // chunk, score, (lowest, nothing, nothing, lowest, nothing), unroll=True)
    stats[...] = jnp.concatenate(list(found) + [nothing] * 3, axis=0)


def scores(mine, other, relation, relation_b, cols, shards, shape):
    n, own = len(shards), shards[0].shape[0]
    q = mine.shape[0]
    slab = n * own
    chunk = 512 if slab % 512 == 0 else own
    return pl.pallas_call(
        functools.partial(score_kernel, shape, own, n, chunk),
        out_shape=(
            jax.ShapeDtypeStruct((slab, q), F32),
            jax.ShapeDtypeStruct((slab, q), F32),
            jax.ShapeDtypeStruct((8, q), F32),
            jax.ShapeDtypeStruct((q, shape.sw), BF16),
        ),
        in_specs=[VMEM] * 5 + [ANY] * n,
        out_specs=(VMEM,) * 4,
        scratch_shapes=[
            pltpu.VMEM((slab, shape.total), BF16),
            pltpu.VMEM((q, 2 * shape.wide), BF16),
            pltpu.SemaphoreType.DMA((n,)),
        ],
        compiler_params=pltpu.CompilerParams(vmem_limit_bytes=8 * slab * q + 2 * slab * shape.total + 10 * MIB),
        cost_estimate=pl.CostEstimate(
            flops=2 * q * slab * shape.total, bytes_accessed=2 * slab * shape.total + 8 * slab * q, transcendentals=2 * slab * q
        ),
        name="scores",
    )(mine, other, relation, relation_b, cols, *shards)


def combine(a, b):
    top_t, top_s = jnp.maximum(a[0:1], b[0:1]), jnp.maximum(a[3:4], b[3:4])
    at, bt = jnp.exp(a[0:1] - top_t), jnp.exp(b[0:1] - top_t)
    as_, bs = jnp.exp(a[3:4] - top_s), jnp.exp(b[3:4] - top_s)
    total_t = a[1:2] * at + b[1:2] * bt
    weighted = a[2:3] * at + b[2:3] * bt
    total_s = a[4:5] * as_ + b[4:5] * bs
    return top_t, total_t, weighted, top_s, total_s


def grad_kernel(n, own, chunk, sw, order, t_in, s_in, mine, other, q_student, *rest):
    shards, (divergence, q_grad), outs = rest[:n], rest[n : n + 2], rest[n + 2 : -3]
    table, e_grad, sems = rest[-3:]
    copies = [
        pltpu.make_async_copy(shard.at[:, pl.ds(0, sw)], table.at[pl.ds(j * own, own)], sems.at[j])
        for j, shard in enumerate(shards)
    ]
    for copy in copies:
        copy.start()
    top_t, total_t, weighted, top_s, total_s = combine(mine[...], other[...])
    divergence[...] = weighted / total_t - top_t - jnp.log(total_t) + top_s + jnp.log(total_s)
    over_t, over_s = 1.0 / total_t, 1.0 / total_s
    for copy in copies:
        copy.wait()
    per = chunk // own

    def step(c, total):
        at = pl.ds(pl.multiple_of(c * chunk, chunk), chunk)
        prob_t = jnp.exp(t_in[at, :] - top_t) * over_t
        prob_s = jnp.exp(s_in[at, :] - top_s) * over_s
        weights = (prob_s - prob_t).astype(BF16)
        grad = jnp.dot(weights, q_student[...], preferred_element_type=F32).astype(BF16)
        for k in range(per):
            e_grad[order[c * per + k]] = grad[k * own : (k + 1) * own, :]
        return total + lax.dot_general(
            table[at, :], weights, (((0,), (0,)), ((), ())), preferred_element_type=F32
        )

    q = q_student.shape[0]
    total = lax.fori_loop(0, n * own // chunk, step, jnp.zeros((sw, q), F32), unroll=True)
    q_grad[...] = total.T
    count = n // len(outs)
    for d, out in enumerate(outs):
        out[...] = e_grad[d * count : (d + 1) * count]


def gradients(order, near, t, s, mine, other, q_student, shards):
    n, own = len(shards), shards[0].shape[0]
    q, sw = q_student.shape
    slab = n * own
    chunk = 512 if slab % 512 == 0 else own
    return pl.pallas_call(
        functools.partial(grad_kernel, n, own, chunk, sw),
        out_shape=(
            jax.ShapeDtypeStruct((1, q), F32),
            jax.ShapeDtypeStruct((q, sw), F32),
        )
        + (jax.ShapeDtypeStruct((n // near, own, sw), BF16),) * near,
        in_specs=[SMEM] + [VMEM] * 5 + [ANY] * n,
        out_specs=(VMEM,) * (2 + near),
        scratch_shapes=[
            pltpu.VMEM((slab, sw), BF16),
            pltpu.VMEM((n, own, sw), BF16),
            pltpu.SemaphoreType.DMA((n,)),
        ],
        compiler_params=pltpu.CompilerParams(vmem_limit_bytes=8 * slab * q + 10 * MIB),
        cost_estimate=pl.CostEstimate(
            flops=4 * q * slab * sw, bytes_accessed=8 * slab * q, transcendentals=2 * slab * q
        ),
        name="gradients",
    )(order, t, s, mine, other, q_student, *shards)


def add_kernel(count, *refs):
    terms, outs = refs[:count], refs[count:]
    for e, out in enumerate(outs):
        total = terms[0][e].astype(F32)
        for term in terms[1:]:
            total += term[e].astype(F32)
        out[...] = total.astype(out.dtype)


def add_blocks(terms):
    far, own, sw = terms[0].shape
    return pl.pallas_call(
        functools.partial(add_kernel, len(terms)),
        out_shape=(jax.ShapeDtypeStruct((own, sw), F32),)
        + (jax.ShapeDtypeStruct((own, sw), BF16),) * (far - 1),
        in_specs=[VMEM] * len(terms),
        out_specs=(VMEM,) * far,
        compiler_params=pltpu.CompilerParams(vmem_limit_bytes=8 * MIB),
        name="add_blocks",
    )(*terms)


def reduce_blocks(blocks, beside, n):
    near, far = len(blocks), n // len(blocks)
    terms = [blocks[0]]
    for d in range(1, near):
        terms.append(lax.ppermute(blocks[d], "query", [(i, i ^ d) for i in range(n)]))
    terms[-1], beside = lax.optimization_barrier((terms[-1], beside))
    sums = add_blocks(terms)
    total = sums[0]
    for e in range(1, far):
        pairs = [(h * near + r, (h + e) % far * near + r) for h in range(far) for r in range(near)]
        total = total + lax.ppermute(sums[e], "query", pairs).astype(F32)
    return total, beside


def make(n, groups):
    place = places(n)
    steps, held = spread_steps(len(place), len(place[0]) == 2)
    table = owners(place, held, n)
    near = next(k for k in (4, 2, 1) if n % k == 0)
    me = np.arange(n)[:, None]
    position = ((table % near) ^ (me % near)) * (n // near) + (table // near - me // near) % (n // near)

    def per_device(
        anchor_ids,
        relation_ids,
        side_flags,
        teacher_entities,
        student_entities,
        teacher_relations,
        student_relations,
    ):
        own, tw = teacher_entities.shape
        shape = Shape(tw, student_entities.shape[1])
        owner, order = jnp.asarray(np.stack([table, position], axis=1))[lax.axis_index("query")]
        bases = (owner + lax.axis_index("entity") * n) * own
        cols = jnp.stack([anchor_ids, relation_ids, side_flags], axis=1)

        have = {(0, 0): pack(teacher_entities, student_entities, shape)}
        block = 768
        per_core = -(-teacher_relations.shape[0] // (2 * block))
        base = (lax.axis_index("entity") % 2 * per_core).astype(jnp.int32)[None]
        relation, anchors, counted, todo = None, None, 0, list(range(per_core))
        marks, kept = [(0, 0)], {}
        for number, step in enumerate(steps):
            final = number == len(steps) - 1
            arrived, base, bases = lax.optimization_barrier(({h: have[h] for h in marks}, base, bases))
            kept.update(arrived)
            got = {new: move(have[old], place, shift) for shift, old, new in step}
            tied = None
            while todo and (final or tied is None):
                first = todo.pop(0)
                relation = relation_rows(
                    base, cols, teacher_relations, student_relations, relation, first, block, not todo, shape
                )
                if not todo:
                    relation_b = partner(relation[0], groups, 1)
                    relation = relation + [relation_b]
                tied = relation
            if tied is None or final:
                names = held[counted : len(have)]
                anchors = anchor_rows(bases[counted:], cols, [kept[h] for h in names], anchors, shape)
                counted = len(have)
                tied = anchors
            if not final:
                gate = step[0][2]
                got[gate], tied = lax.optimization_barrier((got[gate], tied))
                if isinstance(tied, list):
                    relation = tied
                else:
                    anchors = tied
            marks = list(got)
            have.update(got)
        relation, relation_b = relation
        kept.update({h: have[h] for h in marks})
        shards = [kept[h] for h in held]
        mine = anchor_rows(bases[counted:], cols, shards[counted:], anchors, shape)
        far = 1
        while far < groups // 2:
            mine = mine + partner(mine, groups, far)
            far *= 2
        other = partner(mine, groups, far)
        t, s, stats, q_student = scores(mine, other, relation, relation_b, cols, shards, shape)
        far = 1
        while far < groups // 2:
            found = combine(stats, partner(stats, groups, far))
            stats = jnp.concatenate(list(found) + [jnp.zeros_like(found[0])] * 3, axis=0)
            far *= 2
        divergence, q_grad, *blocks = gradients(
            order, near, t, s, stats, partner(stats, groups, far), q_student, shards
        )
        far = 1
        while far < groups:
            q_grad = q_grad + partner(q_grad, groups, far)
            far *= 2
        entity_grad, q_grad = reduce_blocks(blocks, q_grad, n)
        return (divergence[0], entity_grad, q_grad)

    return per_device


def solution(mesh):
    in_specs = (
        P("query"),
        P("query"),
        P("query"),
        P(("entity", "query"), None),
        P(("entity", "query"), None),
        P(),
        P(),
    )
    out_specs = (P("query"), P(("entity", "query"), None), P("query", None))
    return jax.shard_map(
        make(mesh.shape["query"], mesh.shape["entity"]),
        mesh=mesh, in_specs=in_specs, out_specs=out_specs, check_vma=False,
    )
```

```python
import functools

import jax
import jax.numpy as jnp
import numpy as np
from jax import lax
from jax.experimental import pallas as pl
from jax.experimental.pallas import tpu as pltpu
from jax.sharding import PartitionSpec as P

F32 = jnp.float32
BF16 = jnp.bfloat16
VMEM = pl.BlockSpec(memory_space=pltpu.VMEM)
SMEM = pl.BlockSpec(memory_space=pltpu.SMEM)
ANY = pl.BlockSpec(memory_space=pl.ANY)
MIB = 1 << 20


def places(n):
    sides = 2 if n % 2 == 0 else 1
    m = n // sides
    order = list(range(m))
    if m % 2 == 0:
        order = [2 * z for z in range(m // 2)] + [2 * z + 1 for z in reversed(range(m // 2))]
    return [[order[p] * sides + x for x in range(sides)] for p in range(m)]


def spread_steps(m, across):
    held = [(0, 0)]
    steps = []
    while len(held) < m * (2 if across else 1):
        taken = []
        for shift in (1, -1, 0):
            if shift == 0 and not across:
                continue
            if shift:
                found = [((k, o), (k, (o + shift) % m)) for k, o in held]
            else:
                found = [((k, o), (1 - k, o)) for k, o in held]
            names = [t[2] for t in taken]
            found = [f for f in found if f[1] not in held and f[1] not in names]
            if found:
                best = min(found, key=lambda f: (f[1][0], -min(f[1][1], m - f[1][1]), f[1][1]))
                taken.append((shift,) + best)
        held += [t[2] for t in taken]
        steps.append(taken)
    return steps, held


def move(x, place, shift):
    m = len(place)
    pairs = []
    for p in range(m):
        for side in range(len(place[0])):
            source = place[(p + shift) % m][side] if shift else place[p][1 - side]
            pairs.append((source, place[p][side]))
    return lax.ppermute(x, "query", sorted(pairs))


def owners(place, held, n):
    owner = np.zeros((n, n), np.int32)
    for p in range(len(place)):
        for side in range(len(place[0])):
            for slot, (k, o) in enumerate(held):
                owner[place[p][side], slot] = place[(p + o) % len(place)][side ^ k]
    return owner


def partner(x, size, far):
    return lax.ppermute(x, "entity", [(i, i ^ far) for i in range(size)])


class Shape:
    def __init__(self, tw, sw):
        self.tw, self.sw = tw, sw
        self.half = tw // 2
        self.wide = -(-self.half // 128) * 128
        self.re, self.im = sw, sw + self.wide
        self.total = sw + 2 * self.wide


def put_row(out, student, teacher, shape):
    out[:, : shape.sw] = student.astype(BF16)
    pad = jnp.zeros((teacher.shape[0], shape.wide - shape.half), F32)
    for start, at in ((0, shape.re), (shape.half, shape.im)):
        piece = teacher[:, start : start + shape.half]
        out[:, at : at + shape.wide] = jnp.concatenate([piece, pad], axis=1).astype(BF16)


def pack_kernel(shape, teacher_t, student, out):
    put_row(out, student[...].astype(F32), teacher_t[...].astype(F32).T, shape)


def pack(teacher, student, shape):
    return pl.pallas_call(
        functools.partial(pack_kernel, shape),
        out_shape=jax.ShapeDtypeStruct((teacher.shape[0], shape.total), BF16),
        in_specs=[VMEM, VMEM],
        out_specs=VMEM,
        compiler_params=pltpu.CompilerParams(vmem_limit_bytes=8 * MIB),
        name="pack_rows",
    )(teacher.T, student)


def relation_kernel(shape, rel, block, base, cols, table_t, student, out, acc, acc_s):
    step = pl.program_id(0)
    start = (base[0] + step) * block
    ids = cols[:, 1:2] - start
    hot = (ids == lax.broadcasted_iota(jnp.int32, (cols.shape[0], block), 1)).astype(F32).astype(BF16)
    lanes = lax.broadcasted_iota(jnp.int32, table_t.shape, 1)
    rows = lax.broadcasted_iota(jnp.int32, student.shape, 0)
    table = jnp.where(lanes < rel - start, table_t[...], jnp.zeros_like(table_t))
    small = jnp.where(rows < rel - start, student[...], jnp.zeros_like(student))
    part = lax.dot_general(hot, table, (((1,), (1,)), ((), ())), preferred_element_type=F32)
    part_s = jnp.dot(hot, small, preferred_element_type=F32)

    @pl.when(step == 0)
    def _():
        acc[...] = part
        acc_s[...] = part_s

    @pl.when(step > 0)
    def _():
        acc[...] += part
        acc_s[...] += part_s

    @pl.when(step == pl.num_programs(0) - 1)
    def _():
        put_row(out, acc_s[...], acc[...], shape)


def relation_rows(base, cols, table, student, count, block, shape):
    rel, tw = table.shape
    q = cols.shape[0]
    final = -(-rel // block) - 1
    whole = lambda i, base: (0, 0)
    return pl.pallas_call(
        functools.partial(relation_kernel, shape, rel, block),
        out_shape=jax.ShapeDtypeStruct((q, shape.total), BF16),
        grid_spec=pltpu.PrefetchScalarGridSpec(
            num_scalar_prefetch=1,
            grid=(count,),
            in_specs=[
                pl.BlockSpec((q, cols.shape[1]), whole),
                pl.BlockSpec((tw, block), lambda i, base: (0, jnp.minimum(base[0] + i, final))),
                pl.BlockSpec((block, shape.sw), lambda i, base: (jnp.minimum(base[0] + i, final), 0)),
            ],
            out_specs=pl.BlockSpec((q, shape.total), whole),
            scratch_shapes=[pltpu.VMEM((q, tw), F32), pltpu.VMEM((q, shape.sw), F32)],
        ),
        compiler_params=pltpu.CompilerParams(vmem_limit_bytes=56 * MIB),
        cost_estimate=pl.CostEstimate(
            flops=2 * q * tw * block * count, bytes_accessed=2 * tw * block * count, transcendentals=0
        ),
        name="relation_rows",
    )(base, cols, table.T, student)


def load_shards(shards, table, sems, own):
    copies = [
        pltpu.make_async_copy(shard, table.at[pl.ds(j * own, own)], sems.at[j]) for j, shard in enumerate(shards)
    ]
    for copy in copies:
        copy.start()
    return copies


def anchor_kernel(count, own, has_acc, bases, cols, *rest):
    acc_in, rest = (rest[0], rest[1:]) if has_acc else (None, rest)
    shards, (out, table, hot, sems) = rest[:count], rest[count:]
    copies = load_shards(shards, table, sems, own)
    q = cols.shape[0]
    ids = cols[:, 0:1]
    lane = lax.broadcasted_iota(jnp.int32, (q, own), 1)
    for j in range(count):
        hot[:, j * own : (j + 1) * own] = (ids - bases[j] == lane).astype(F32).astype(BF16)
    for copy in copies:
        copy.wait()
    found = jnp.dot(hot[...], table[...], preferred_element_type=F32).astype(BF16)
    out[...] = found + acc_in[...] if has_acc else found


def anchor_rows(bases, ids, shards, acc, shape):
    own = shards[0].shape[0]
    q, count = ids.shape[0], len(shards)
    operands = [bases, ids] + ([] if acc is None else [acc]) + list(shards)
    return pl.pallas_call(
        functools.partial(anchor_kernel, count, own, acc is not None),
        out_shape=jax.ShapeDtypeStruct((q, shape.total), BF16),
        in_specs=[SMEM, VMEM] + ([] if acc is None else [VMEM]) + [ANY] * count,
        out_specs=VMEM,
        scratch_shapes=[
            pltpu.VMEM((count * own, shape.total), BF16),
            pltpu.VMEM((q, count * own), BF16),
            pltpu.SemaphoreType.DMA((count,)),
        ],
        compiler_params=pltpu.CompilerParams(vmem_limit_bytes=2 * count * own * (shape.total + q) + 12 * MIB),
        cost_estimate=pl.CostEstimate(
            flops=2 * q * count * own * shape.total,
            bytes_accessed=2 * (count * own + 2 * q) * shape.total,
            transcendentals=0,
        ),
        name="anchor_rows",
    )(*operands)


def score_kernel(shape, own, n, chunk, mine, other, relation, relation_b, cols, *rest):
    shards, (t_out, s_out, stats, q_student, table, q_teacher, sems) = rest[:n], rest[n:]
    copies = load_shards(shards, table, sems, own)
    q = mine.shape[0]
    sw, wide = shape.sw, shape.wide
    rows = 128

    def build(i, _):
        at = pl.ds(pl.multiple_of(i * rows, rows), rows)
        g = (2 * cols[at, 2:3] - 1).astype(F32)
        a = mine[at, :].astype(F32) + other[at, :].astype(F32)
        r = relation[at, :].astype(F32) + relation_b[at, :].astype(F32)
        a_re, a_im = a[:, shape.re : shape.re + wide], a[:, shape.im : shape.im + wide]
        r_re, r_im = r[:, shape.re : shape.re + wide], r[:, shape.im : shape.im + wide]
        q_teacher[at, :wide] = (a_re * r_re - g * a_im * r_im).astype(BF16)
        q_teacher[at, wide:] = (a_im * r_re + g * a_re * r_im).astype(BF16)
        a_s, r_s = a[:, :sw], r[:, :sw]
        a_x, r_x = pltpu.roll(a_s, sw // 2, 1), pltpu.roll(r_s, sw // 2, 1)
        low = lax.broadcasted_iota(jnp.int32, (rows, sw), 1) < sw // 2
        re2, im2 = jnp.where(low, r_s, r_x), jnp.where(low, r_x, r_s)
        q_student[at, :] = (a_s * re2 + jnp.where(low, -g, g) * a_x * im2).astype(BF16)
        return 0

    lax.fori_loop(0, q // rows, build, 0)
    for copy in copies:
        copy.wait()

    dims = (((1,), (1,)), ((), ()))

    def score(c, carry):
        top_t, total_t, weighted, top_s, total_s = carry
        at = pl.ds(pl.multiple_of(c * chunk, chunk), chunk)
        t = lax.dot_general(table[at, sw:], q_teacher[...], dims, preferred_element_type=F32)
        s = lax.dot_general(table[at, :sw], q_student[...], dims, preferred_element_type=F32)
        t_out[at, :] = t
        s_out[at, :] = s
        new_t = jnp.maximum(top_t, jnp.max(t, axis=0, keepdims=True))
        new_s = jnp.maximum(top_s, jnp.max(s, axis=0, keepdims=True))
        scale_t, scale_s = jnp.exp(top_t - new_t), jnp.exp(top_s - new_s)
        e = jnp.exp(t - new_t)
        total_t = total_t * scale_t + jnp.sum(e, axis=0, keepdims=True)
        weighted = weighted * scale_t + jnp.sum(e * (t - s), axis=0, keepdims=True)
        total_s = total_s * scale_s + jnp.sum(jnp.exp(s - new_s), axis=0, keepdims=True)
        return new_t, total_t, weighted, new_s, total_s

    lowest = jnp.full((1, q), -jnp.inf, F32)
    nothing = jnp.zeros((1, q), F32)
    found = lax.fori_loop(0, n * own // chunk, score, (lowest, nothing, nothing, lowest, nothing), unroll=True)
    stats[...] = jnp.concatenate(list(found) + [nothing] * 3, axis=0)


def scores(mine, other, relation, relation_b, cols, shards, shape):
    n, own = len(shards), shards[0].shape[0]
    q = mine.shape[0]
    slab = n * own
    chunk = 512 if slab % 512 == 0 else own
    return pl.pallas_call(
        functools.partial(score_kernel, shape, own, n, chunk),
        out_shape=(
            jax.ShapeDtypeStruct((slab, q), F32),
            jax.ShapeDtypeStruct((slab, q), F32),
            jax.ShapeDtypeStruct((8, q), F32),
            jax.ShapeDtypeStruct((q, shape.sw), BF16),
        ),
        in_specs=[VMEM] * 5 + [ANY] * n,
        out_specs=(VMEM,) * 4,
        scratch_shapes=[
            pltpu.VMEM((slab, shape.total), BF16),
            pltpu.VMEM((q, 2 * shape.wide), BF16),
            pltpu.SemaphoreType.DMA((n,)),
        ],
        compiler_params=pltpu.CompilerParams(vmem_limit_bytes=8 * slab * q + 2 * slab * shape.total + 10 * MIB),
        cost_estimate=pl.CostEstimate(
            flops=2 * q * slab * shape.total, bytes_accessed=2 * slab * shape.total + 8 * slab * q, transcendentals=2 * slab * q
        ),
        name="scores",
    )(mine, other, relation, relation_b, cols, *shards)


def combine(a, b):
    top_t, top_s = jnp.maximum(a[0:1], b[0:1]), jnp.maximum(a[3:4], b[3:4])
    at, bt = jnp.exp(a[0:1] - top_t), jnp.exp(b[0:1] - top_t)
    as_, bs = jnp.exp(a[3:4] - top_s), jnp.exp(b[3:4] - top_s)
    total_t = a[1:2] * at + b[1:2] * bt
    weighted = a[2:3] * at + b[2:3] * bt
    total_s = a[4:5] * as_ + b[4:5] * bs
    return top_t, total_t, weighted, top_s, total_s


def grad_kernel(n, own, chunk, sw, order, t_in, s_in, mine, other, q_student, *rest):
    shards, (divergence, q_grad), outs = rest[:n], rest[n : n + 2], rest[n + 2 : -3]
    table, e_grad, sems = rest[-3:]
    copies = [
        pltpu.make_async_copy(shard.at[:, pl.ds(0, sw)], table.at[pl.ds(j * own, own)], sems.at[j])
        for j, shard in enumerate(shards)
    ]
    for copy in copies:
        copy.start()
    top_t, total_t, weighted, top_s, total_s = combine(mine[...], other[...])
    divergence[...] = weighted / total_t - top_t - jnp.log(total_t) + top_s + jnp.log(total_s)
    over_t, over_s = 1.0 / total_t, 1.0 / total_s
    for copy in copies:
        copy.wait()
    per = chunk // own

    def step(c, total):
        at = pl.ds(pl.multiple_of(c * chunk, chunk), chunk)
        prob_t = jnp.exp(t_in[at, :] - top_t) * over_t
        prob_s = jnp.exp(s_in[at, :] - top_s) * over_s
        weights = (prob_s - prob_t).astype(BF16)
        grad = jnp.dot(weights, q_student[...], preferred_element_type=F32).astype(BF16)
        for k in range(per):
            e_grad[order[c * per + k]] = grad[k * own : (k + 1) * own, :]
        return total + lax.dot_general(
            table[at, :], weights, (((0,), (0,)), ((), ())), preferred_element_type=F32
        )

    q = q_student.shape[0]
    total = lax.fori_loop(0, n * own // chunk, step, jnp.zeros((sw, q), F32), unroll=True)
    q_grad[...] = total.T
    count = n // len(outs)
    for d, out in enumerate(outs):
        out[...] = e_grad[d * count : (d + 1) * count]


def gradients(order, near, t, s, mine, other, q_student, shards):
    n, own = len(shards), shards[0].shape[0]
    q, sw = q_student.shape
    slab = n * own
    chunk = 512 if slab % 512 == 0 else own
    return pl.pallas_call(
        functools.partial(grad_kernel, n, own, chunk, sw),
        out_shape=(
            jax.ShapeDtypeStruct((1, q), F32),
            jax.ShapeDtypeStruct((q, sw), F32),
        )
        + (jax.ShapeDtypeStruct((n // near, own, sw), BF16),) * near,
        in_specs=[SMEM] + [VMEM] * 5 + [ANY] * n,
        out_specs=(VMEM,) * (2 + near),
        scratch_shapes=[
            pltpu.VMEM((slab, sw), BF16),
            pltpu.VMEM((n, own, sw), BF16),
            pltpu.SemaphoreType.DMA((n,)),
        ],
        compiler_params=pltpu.CompilerParams(vmem_limit_bytes=8 * slab * q + 10 * MIB),
        cost_estimate=pl.CostEstimate(
            flops=4 * q * slab * sw, bytes_accessed=8 * slab * q, transcendentals=2 * slab * q
        ),
        name="gradients",
    )(order, t, s, mine, other, q_student, *shards)


def add_kernel(count, *refs):
    terms, outs = refs[:count], refs[count:]
    for e, out in enumerate(outs):
        total = terms[0][e].astype(F32)
        for term in terms[1:]:
            total += term[e].astype(F32)
        out[...] = total.astype(out.dtype)


def add_blocks(terms):
    far, own, sw = terms[0].shape
    return pl.pallas_call(
        functools.partial(add_kernel, len(terms)),
        out_shape=(jax.ShapeDtypeStruct((own, sw), F32),)
        + (jax.ShapeDtypeStruct((own, sw), BF16),) * (far - 1),
        in_specs=[VMEM] * len(terms),
        out_specs=(VMEM,) * far,
        compiler_params=pltpu.CompilerParams(vmem_limit_bytes=8 * MIB),
        name="add_blocks",
    )(*terms)


def reduce_blocks(blocks, beside, n):
    near, far = len(blocks), n // len(blocks)
    terms = [blocks[0]]
    for d in range(1, near):
        terms.append(lax.ppermute(blocks[d], "query", [(i, i ^ d) for i in range(n)]))
    terms[-1], beside = lax.optimization_barrier((terms[-1], beside))
    sums = add_blocks(terms)
    total = sums[0]
    for e in range(1, far):
        pairs = [(h * near + r, (h ^ e if far & (far - 1) == 0 else (h + e) % far) * near + r) for h in range(far) for r in range(near)]
        total = total + lax.ppermute(sums[e], "query", pairs).astype(F32)
    return total, beside


def make(n, groups):
    place = places(n)
    steps, held = spread_steps(len(place), len(place[0]) == 2)
    table = owners(place, held, n)
    near = next(k for k in (4, 2, 1) if n % k == 0)
    me = np.arange(n)[:, None]
    far_move = (table // near) ^ (me // near) if n // near & (n // near - 1) == 0 else (table // near - me // near) % (n // near)
    position = ((table % near) ^ (me % near)) * (n // near) + far_move

    def per_device(
        anchor_ids,
        relation_ids,
        side_flags,
        teacher_entities,
        student_entities,
        teacher_relations,
        student_relations,
    ):
        own, tw = teacher_entities.shape
        shape = Shape(tw, student_entities.shape[1])
        owner, order = jnp.asarray(np.stack([table, position], axis=1))[lax.axis_index("query")]
        bases = (owner + lax.axis_index("entity") * n) * own
        cols = jnp.stack([anchor_ids, relation_ids, side_flags], axis=1)

        have = {(0, 0): pack(teacher_entities, student_entities, shape)}
        block = 768
        per_core = -(-teacher_relations.shape[0] // (2 * block))
        base = (lax.axis_index("entity") % 2 * per_core).astype(jnp.int32)[None]
        own_key = (0, 0)
        have[own_key], base = lax.optimization_barrier((have[own_key], base))
        anchors, counted = None, 0
        for number, step in enumerate(steps):
            got = {new: move(have[old], place, shift) for shift, old, new in step}
            beside = None
            if number == 0:
                relation = relation_rows(base, cols, teacher_relations, student_relations, per_core, block, shape)
                beside = relation
            elif number >= len(steps) // 2:
                names = held[counted : len(have)]
                anchors = anchor_rows(bases[counted:], cols, [have[h] for h in names], anchors, shape)
                counted = len(have)
                beside = anchors
            sent = [old for _, old, _ in steps[number + 1] if old in got] if number + 1 < len(steps) else []
            if sent and beside is not None:
                gate = sent[len(sent) // 2]
                got[gate], beside = lax.optimization_barrier((got[gate], beside))
                if number == 0:
                    relation = beside
                else:
                    anchors = beside
            if number == 0:
                relation_b = partner(relation, groups, 1)
            have.update(got)
        shards = [have[h] for h in held]
        mine = anchor_rows(bases[counted:], cols, shards[counted:], anchors, shape)
        far = 1
        while far < groups // 2:
            mine = mine + partner(mine, groups, far)
            far *= 2
        other = partner(mine, groups, far)
        t, s, stats, q_student = scores(mine, other, relation, relation_b, cols, shards, shape)
        far = 1
        while far < groups // 2:
            found = combine(stats, partner(stats, groups, far))
            stats = jnp.concatenate(list(found) + [jnp.zeros_like(found[0])] * 3, axis=0)
            far *= 2
        divergence, q_grad, *blocks = gradients(
            order, near, t, s, stats, partner(stats, groups, far), q_student, shards
        )
        far = 1
        while far < groups:
            q_grad = q_grad + partner(q_grad, groups, far)
            far *= 2
        entity_grad, q_grad = reduce_blocks(blocks, q_grad, n)
        return (divergence[0], entity_grad, q_grad)

    return per_device


def solution(mesh):
    in_specs = (
        P("query"),
        P("query"),
        P("query"),
        P(("entity", "query"), None),
        P(("entity", "query"), None),
        P(),
        P(),
    )
    out_specs = (P("query"), P(("entity", "query"), None), P("query", None))
    return jax.shard_map(
        make(mesh.shape["query"], mesh.shape["entity"]),
        mesh=mesh, in_specs=in_specs, out_specs=out_specs, check_vma=False,
    )
```

```python
import functools

import jax
import jax.numpy as jnp
import numpy as np
from jax import lax
from jax.experimental import pallas as pl
from jax.experimental.pallas import tpu as pltpu
from jax.sharding import PartitionSpec as P

F32 = jnp.float32
BF16 = jnp.bfloat16
VMEM = pl.BlockSpec(memory_space=pltpu.VMEM)
SMEM = pl.BlockSpec(memory_space=pltpu.SMEM)
ANY = pl.BlockSpec(memory_space=pl.ANY)
MIB = 1 << 20


def places(n):
    sides = 2 if n % 2 == 0 else 1
    m = n // sides
    order = list(range(m))
    if m % 2 == 0:
        order = [2 * z for z in range(m // 2)] + [2 * z + 1 for z in reversed(range(m // 2))]
    return [[order[p] * sides + x for x in range(sides)] for p in range(m)]


def spread_steps(m, across):
    held = [(0, 0)]
    steps = []
    while len(held) < m * (2 if across else 1):
        taken = []
        for shift in (1, -1, 0):
            if shift == 0 and not across:
                continue
            if shift:
                found = [((k, o), (k, (o + shift) % m)) for k, o in held]
            else:
                found = [((k, o), (1 - k, o)) for k, o in held]
            names = [t[2] for t in taken]
            found = [f for f in found if f[1] not in held and f[1] not in names]
            if found:
                best = min(found, key=lambda f: (f[1][0], -min(f[1][1], m - f[1][1]), f[1][1]))
                taken.append((shift,) + best)
        held += [t[2] for t in taken]
        steps.append(taken)
    return steps, held


def move(x, place, shift):
    m = len(place)
    pairs = []
    for p in range(m):
        for side in range(len(place[0])):
            source = place[(p + shift) % m][side] if shift else place[p][1 - side]
            pairs.append((source, place[p][side]))
    return lax.ppermute(x, "query", sorted(pairs))


def owners(place, held, n):
    owner = np.zeros((n, n), np.int32)
    for p in range(len(place)):
        for side in range(len(place[0])):
            for slot, (k, o) in enumerate(held):
                owner[place[p][side], slot] = place[(p + o) % len(place)][side ^ k]
    return owner


def partner(x, size, far):
    return lax.ppermute(x, "entity", [(i, i ^ far) for i in range(size)])


class Shape:
    def __init__(self, tw, sw):
        self.tw, self.sw = tw, sw
        self.half = tw // 2
        self.wide = -(-self.half // 128) * 128
        self.re, self.im = sw, sw + self.wide
        self.total = sw + 2 * self.wide


def put_row(out, student, teacher, shape):
    out[:, : shape.sw] = student.astype(BF16)
    pad = jnp.zeros((teacher.shape[0], shape.wide - shape.half), F32)
    for start, at in ((0, shape.re), (shape.half, shape.im)):
        piece = teacher[:, start : start + shape.half]
        out[:, at : at + shape.wide] = jnp.concatenate([piece, pad], axis=1).astype(BF16)


def pack_kernel(shape, teacher_t, student, anchor_ids, relation_ids, side_flags, out, cols):
    rows = jnp.concatenate([anchor_ids[...], relation_ids[...], side_flags[...]], axis=0).astype(F32)
    rows = jnp.concatenate([rows, jnp.zeros((5, rows.shape[1]), F32)], axis=0)
    cols[...] = rows.T.astype(jnp.int32)
    put_row(out, student[...].astype(F32), teacher_t[...].astype(F32).T, shape)


def pack(teacher, student, ids, shape):
    return pl.pallas_call(
        functools.partial(pack_kernel, shape),
        out_shape=(
            jax.ShapeDtypeStruct((teacher.shape[0], shape.total), BF16),
            jax.ShapeDtypeStruct((ids[0].shape[0], 8), jnp.int32),
        ),
        in_specs=[VMEM] * 5,
        out_specs=(VMEM, VMEM),
        compiler_params=pltpu.CompilerParams(vmem_limit_bytes=60 * MIB),
        name="pack_rows",
    )(teacher.T, student, *[x[None] for x in ids])


def relation_kernel(shape, rel, block, base, cols, table_t, student, out, acc, acc_s):
    step = pl.program_id(0)
    start = (base[0] + step) * block
    ids = cols[:, 1:2] - start
    hot = (ids == lax.broadcasted_iota(jnp.int32, (cols.shape[0], block), 1)).astype(F32).astype(BF16)

    def add(table, small):
        part = lax.dot_general(hot, table, (((1,), (1,)), ((), ())), preferred_element_type=F32)
        part_s = jnp.dot(hot, small, preferred_element_type=F32)

        @pl.when(step == 0)
        def _():
            acc[...] = part
            acc_s[...] = part_s

        @pl.when(step > 0)
        def _():
            acc[...] += part
            acc_s[...] += part_s

    @pl.when(start + block <= rel)
    def _():
        add(table_t[...], student[...])

    @pl.when(start + block > rel)
    def _():
        lanes = lax.broadcasted_iota(jnp.int32, table_t.shape, 1)
        rows = lax.broadcasted_iota(jnp.int32, student.shape, 0)
        add(
            jnp.where(lanes < rel - start, table_t[...], jnp.zeros_like(table_t)),
            jnp.where(rows < rel - start, student[...], jnp.zeros_like(student)),
        )

    @pl.when(step == pl.num_programs(0) - 1)
    def _():
        put_row(out, acc_s[...], acc[...], shape)


def relation_rows(base, cols, table, student, count, block, shape):
    rel, tw = table.shape
    q = cols.shape[0]
    final = -(-rel // block) - 1
    whole = lambda i, base: (0, 0)
    return pl.pallas_call(
        functools.partial(relation_kernel, shape, rel, block),
        out_shape=jax.ShapeDtypeStruct((q, shape.total), BF16),
        grid_spec=pltpu.PrefetchScalarGridSpec(
            num_scalar_prefetch=1,
            grid=(count,),
            in_specs=[
                pl.BlockSpec((q, cols.shape[1]), whole),
                pl.BlockSpec((tw, block), lambda i, base: (0, jnp.minimum(base[0] + i, final))),
                pl.BlockSpec((block, shape.sw), lambda i, base: (jnp.minimum(base[0] + i, final), 0)),
            ],
            out_specs=pl.BlockSpec((q, shape.total), whole),
            scratch_shapes=[pltpu.VMEM((q, tw), F32), pltpu.VMEM((q, shape.sw), F32)],
        ),
        compiler_params=pltpu.CompilerParams(vmem_limit_bytes=56 * MIB),
        cost_estimate=pl.CostEstimate(
            flops=2 * q * tw * block * count, bytes_accessed=2 * tw * block * count, transcendentals=0
        ),
        name="relation_rows",
    )(base, cols, table.T, student)


def load_shards(shards, table, sems, own):
    copies = [
        pltpu.make_async_copy(shard, table.at[pl.ds(j * own, own)], sems.at[j]) for j, shard in enumerate(shards)
    ]
    for copy in copies:
        copy.start()
    return copies


def anchor_kernel(count, own, has_acc, bases, cols, *rest):
    acc_in, rest = (rest[0], rest[1:]) if has_acc else (None, rest)
    shards, (out, table, hot, sems) = rest[:count], rest[count:]
    copies = load_shards(shards, table, sems, own)
    q = cols.shape[0]
    ids = cols[:, 0:1]
    lane = lax.broadcasted_iota(jnp.int32, (q, own), 1)
    for j in range(count):
        hot[:, j * own : (j + 1) * own] = (ids - bases[j] == lane).astype(F32).astype(BF16)
    for copy in copies:
        copy.wait()
    found = jnp.dot(hot[...], table[...], preferred_element_type=F32).astype(BF16)
    out[...] = found + acc_in[...] if has_acc else found


def anchor_rows(bases, ids, shards, acc, shape):
    own = shards[0].shape[0]
    q, count = ids.shape[0], len(shards)
    operands = [bases, ids] + ([] if acc is None else [acc]) + list(shards)
    return pl.pallas_call(
        functools.partial(anchor_kernel, count, own, acc is not None),
        out_shape=jax.ShapeDtypeStruct((q, shape.total), BF16),
        in_specs=[SMEM, VMEM] + ([] if acc is None else [VMEM]) + [ANY] * count,
        out_specs=VMEM,
        scratch_shapes=[
            pltpu.VMEM((count * own, shape.total), BF16),
            pltpu.VMEM((q, count * own), BF16),
            pltpu.SemaphoreType.DMA((count,)),
        ],
        compiler_params=pltpu.CompilerParams(vmem_limit_bytes=2 * count * own * (shape.total + q) + 12 * MIB),
        cost_estimate=pl.CostEstimate(
            flops=2 * q * count * own * shape.total,
            bytes_accessed=2 * (count * own + 2 * q) * shape.total,
            transcendentals=0,
        ),
        name="anchor_rows",
    )(*operands)


def score_kernel(shape, own, n, chunk, mine, other, relation, relation_b, cols, *rest):
    shards, (t_out, s_out, stats, q_student, table, q_teacher, sems) = rest[:n], rest[n:]
    copies = load_shards(shards, table, sems, own)
    q = mine.shape[0]
    sw, wide = shape.sw, shape.wide
    rows = 128

    def build(i, _):
        at = pl.ds(pl.multiple_of(i * rows, rows), rows)
        g = (2 * cols[at, 2:3] - 1).astype(F32)
        a = mine[at, :].astype(F32) + other[at, :].astype(F32)
        r = relation[at, :].astype(F32) + relation_b[at, :].astype(F32)
        a_re, a_im = a[:, shape.re : shape.re + wide], a[:, shape.im : shape.im + wide]
        r_re, r_im = r[:, shape.re : shape.re + wide], r[:, shape.im : shape.im + wide]
        q_teacher[at, :wide] = (a_re * r_re - g * a_im * r_im).astype(BF16)
        q_teacher[at, wide:] = (a_im * r_re + g * a_re * r_im).astype(BF16)
        a_s, r_s = a[:, :sw], r[:, :sw]
        a_x, r_x = pltpu.roll(a_s, sw // 2, 1), pltpu.roll(r_s, sw // 2, 1)
        low = lax.broadcasted_iota(jnp.int32, (rows, sw), 1) < sw // 2
        re2, im2 = jnp.where(low, r_s, r_x), jnp.where(low, r_x, r_s)
        q_student[at, :] = (a_s * re2 + jnp.where(low, -g, g) * a_x * im2).astype(BF16)
        return 0

    lax.fori_loop(0, q // rows, build, 0)
    for copy in copies:
        copy.wait()

    dims = (((1,), (1,)), ((), ()))

    def score(c, carry):
        top_t, total_t, weighted, top_s, total_s = carry
        at = pl.ds(pl.multiple_of(c * chunk, chunk), chunk)
        t = lax.dot_general(table[at, sw:], q_teacher[...], dims, preferred_element_type=F32)
        s = lax.dot_general(table[at, :sw], q_student[...], dims, preferred_element_type=F32)
        t_out[at, :] = t
        s_out[at, :] = s
        new_t = jnp.maximum(top_t, jnp.max(t, axis=0, keepdims=True))
        new_s = jnp.maximum(top_s, jnp.max(s, axis=0, keepdims=True))
        scale_t, scale_s = jnp.exp(top_t - new_t), jnp.exp(top_s - new_s)
        e = jnp.exp(t - new_t)
        total_t = total_t * scale_t + jnp.sum(e, axis=0, keepdims=True)
        weighted = weighted * scale_t + jnp.sum(e * (t - s), axis=0, keepdims=True)
        total_s = total_s * scale_s + jnp.sum(jnp.exp(s - new_s), axis=0, keepdims=True)
        return new_t, total_t, weighted, new_s, total_s

    lowest = jnp.full((1, q), -jnp.inf, F32)
    nothing = jnp.zeros((1, q), F32)
    found = lax.fori_loop(0, n * own // chunk, score, (lowest, nothing, nothing, lowest, nothing), unroll=True)
    stats[...] = jnp.concatenate(list(found) + [nothing] * 3, axis=0)


def scores(mine, other, relation, relation_b, cols, shards, shape):
    n, own = len(shards), shards[0].shape[0]
    q = mine.shape[0]
    slab = n * own
    chunk = 512 if slab % 512 == 0 else own
    return pl.pallas_call(
        functools.partial(score_kernel, shape, own, n, chunk),
        out_shape=(
            jax.ShapeDtypeStruct((slab, q), F32),
            jax.ShapeDtypeStruct((slab, q), F32),
            jax.ShapeDtypeStruct((8, q), F32),
            jax.ShapeDtypeStruct((q, shape.sw), BF16),
        ),
        in_specs=[VMEM] * 5 + [ANY] * n,
        out_specs=(VMEM,) * 4,
        scratch_shapes=[
            pltpu.VMEM((slab, shape.total), BF16),
            pltpu.VMEM((q, 2 * shape.wide), BF16),
            pltpu.SemaphoreType.DMA((n,)),
        ],
        compiler_params=pltpu.CompilerParams(vmem_limit_bytes=8 * slab * q + 2 * slab * shape.total + 10 * MIB),
        cost_estimate=pl.CostEstimate(
            flops=2 * q * slab * shape.total, bytes_accessed=2 * slab * shape.total + 8 * slab * q, transcendentals=2 * slab * q
        ),
        name="scores",
    )(mine, other, relation, relation_b, cols, *shards)


def combine(a, b):
    top_t, top_s = jnp.maximum(a[0:1], b[0:1]), jnp.maximum(a[3:4], b[3:4])
    at, bt = jnp.exp(a[0:1] - top_t), jnp.exp(b[0:1] - top_t)
    as_, bs = jnp.exp(a[3:4] - top_s), jnp.exp(b[3:4] - top_s)
    total_t = a[1:2] * at + b[1:2] * bt
    weighted = a[2:3] * at + b[2:3] * bt
    total_s = a[4:5] * as_ + b[4:5] * bs
    return top_t, total_t, weighted, top_s, total_s


def grad_kernel(n, own, chunk, sw, order, t_in, s_in, mine, other, q_student, *rest):
    shards, (divergence, q_grad), outs = rest[:n], rest[n : n + 2], rest[n + 2 : -3]
    table, e_grad, sems = rest[-3:]
    copies = [
        pltpu.make_async_copy(shard.at[:, pl.ds(0, sw)], table.at[pl.ds(j * own, own)], sems.at[j])
        for j, shard in enumerate(shards)
    ]
    for copy in copies:
        copy.start()
    top_t, total_t, weighted, top_s, total_s = combine(mine[...], other[...])
    divergence[...] = weighted / total_t - top_t - jnp.log(total_t) + top_s + jnp.log(total_s)
    over_t, over_s = 1.0 / total_t, 1.0 / total_s
    for copy in copies:
        copy.wait()
    per = chunk // own

    def step(c, total):
        at = pl.ds(pl.multiple_of(c * chunk, chunk), chunk)
        prob_t = jnp.exp(t_in[at, :] - top_t) * over_t
        prob_s = jnp.exp(s_in[at, :] - top_s) * over_s
        weights = (prob_s - prob_t).astype(BF16)
        grad = jnp.dot(weights, q_student[...], preferred_element_type=F32).astype(BF16)
        for k in range(per):
            e_grad[order[c * per + k]] = grad[k * own : (k + 1) * own, :]
        return total + lax.dot_general(
            table[at, :], weights, (((0,), (0,)), ((), ())), preferred_element_type=F32
        )

    q = q_student.shape[0]
    total = lax.fori_loop(0, n * own // chunk, step, jnp.zeros((sw, q), F32), unroll=True)
    q_grad[...] = total.T
    count = n // len(outs)
    for d, out in enumerate(outs):
        out[...] = e_grad[d * count : (d + 1) * count]


def gradients(order, near, t, s, mine, other, q_student, shards):
    n, own = len(shards), shards[0].shape[0]
    q, sw = q_student.shape
    slab = n * own
    chunk = 512 if slab % 512 == 0 else own
    return pl.pallas_call(
        functools.partial(grad_kernel, n, own, chunk, sw),
        out_shape=(
            jax.ShapeDtypeStruct((1, q), F32),
            jax.ShapeDtypeStruct((q, sw), F32),
        )
        + (jax.ShapeDtypeStruct((n // near, own, sw), BF16),) * near,
        in_specs=[SMEM] + [VMEM] * 5 + [ANY] * n,
        out_specs=(VMEM,) * (2 + near),
        scratch_shapes=[
            pltpu.VMEM((slab, sw), BF16),
            pltpu.VMEM((n, own, sw), BF16),
            pltpu.SemaphoreType.DMA((n,)),
        ],
        compiler_params=pltpu.CompilerParams(vmem_limit_bytes=8 * slab * q + 10 * MIB),
        cost_estimate=pl.CostEstimate(
            flops=4 * q * slab * sw, bytes_accessed=8 * slab * q, transcendentals=2 * slab * q
        ),
        name="gradients",
    )(order, t, s, mine, other, q_student, *shards)


def add_kernel(count, *refs):
    terms, outs = refs[:count], refs[count:]
    for e, out in enumerate(outs):
        total = terms[0][e].astype(F32)
        for term in terms[1:]:
            total += term[e].astype(F32)
        out[...] = total.astype(out.dtype)


def add_blocks(terms):
    far, own, sw = terms[0].shape
    return pl.pallas_call(
        functools.partial(add_kernel, len(terms)),
        out_shape=(jax.ShapeDtypeStruct((own, sw), F32),)
        + (jax.ShapeDtypeStruct((own, sw), BF16),) * (far - 1),
        in_specs=[VMEM] * len(terms),
        out_specs=(VMEM,) * far,
        compiler_params=pltpu.CompilerParams(vmem_limit_bytes=8 * MIB),
        name="add_blocks",
    )(*terms)


def reduce_blocks(blocks, beside, n):
    near, far = len(blocks), n // len(blocks)
    terms = [blocks[0]]
    for d in range(1, near):
        terms.append(lax.ppermute(blocks[d], "query", [(i, i ^ d) for i in range(n)]))
    terms[-1], beside = lax.optimization_barrier((terms[-1], beside))
    sums = add_blocks(terms)
    total = sums[0]
    for e in range(1, far):
        pairs = [(h * near + r, (h + e) % far * near + r) for h in range(far) for r in range(near)]
        total = total + lax.ppermute(sums[e], "query", pairs).astype(F32)
    return total, beside


def make(n, groups):
    place = places(n)
    steps, held = spread_steps(len(place), len(place[0]) == 2)
    table = owners(place, held, n)
    near = next(k for k in (4, 2, 1) if n % k == 0)
    me = np.arange(n)[:, None]
    position = ((table % near) ^ (me % near)) * (n // near) + (table // near - me // near) % (n // near)

    def per_device(
        anchor_ids,
        relation_ids,
        side_flags,
        teacher_entities,
        student_entities,
        teacher_relations,
        student_relations,
    ):
        own, tw = teacher_entities.shape
        shape = Shape(tw, student_entities.shape[1])
        owner, order = jnp.asarray(np.stack([table, position], axis=1))[lax.axis_index("query")]
        bases = (owner + lax.axis_index("entity") * n) * own
        packed, cols = pack(
            teacher_entities, student_entities, (anchor_ids, relation_ids, side_flags), shape
        )
        have = {(0, 0): packed}
        block = 768
        per_core = -(-teacher_relations.shape[0] // (2 * block))
        base = (lax.axis_index("entity") % 2 * per_core).astype(jnp.int32)[None]
        own_key = (0, 0)
        have[own_key], base = lax.optimization_barrier((have[own_key], base))
        anchors, counted = None, 0
        for number, step in enumerate(steps):
            got = {new: move(have[old], place, shift) for shift, old, new in step}
            if number == 0:
                relation = relation_rows(base, cols, teacher_relations, student_relations, per_core, block, shape)
                got, relation = lax.optimization_barrier((got, relation))
                relation_b = partner(relation, groups, 1)
            if number == len(steps) - 1:
                counted = len(have)
                anchors = anchor_rows(bases, cols, [have[h] for h in held[:counted]], None, shape)
            have.update(got)
        shards = [have[h] for h in held]
        mine = anchor_rows(bases[counted:], cols, shards[counted:], anchors, shape)
        far = 1
        while far < groups // 2:
            mine = mine + partner(mine, groups, far)
            far *= 2
        other = partner(mine, groups, far)
        t, s, stats, q_student = scores(mine, other, relation, relation_b, cols, shards, shape)
        far = 1
        while far < groups // 2:
            found = combine(stats, partner(stats, groups, far))
            stats = jnp.concatenate(list(found) + [jnp.zeros_like(found[0])] * 3, axis=0)
            far *= 2
        divergence, q_grad, *blocks = gradients(
            order, near, t, s, stats, partner(stats, groups, far), q_student, shards
        )
        far = 1
        while far < groups:
            q_grad = q_grad + partner(q_grad, groups, far)
            far *= 2
        entity_grad, q_grad = reduce_blocks(blocks, q_grad, n)
        return (divergence[0], entity_grad, q_grad)

    return per_device


def solution(mesh):
    in_specs = (
        P("query"),
        P("query"),
        P("query"),
        P(("entity", "query"), None),
        P(("entity", "query"), None),
        P(),
        P(),
    )
    out_specs = (P("query"), P(("entity", "query"), None), P("query", None))
    return jax.shard_map(
        make(mesh.shape["query"], mesh.shape["entity"]),
        mesh=mesh, in_specs=in_specs, out_specs=out_specs, check_vma=False,
    )
```

```python
import functools

import jax
import jax.numpy as jnp
import numpy as np
from jax import lax
from jax.experimental import pallas as pl
from jax.experimental.pallas import tpu as pltpu
from jax.sharding import PartitionSpec as P

F32 = jnp.float32
BF16 = jnp.bfloat16
VMEM = pl.BlockSpec(memory_space=pltpu.VMEM)
SMEM = pl.BlockSpec(memory_space=pltpu.SMEM)
ANY = pl.BlockSpec(memory_space=pl.ANY)
MIB = 1 << 20


def places(n):
    sides = 2 if n % 2 == 0 else 1
    m = n // sides
    order = list(range(m))
    if m % 2 == 0:
        order = [2 * z for z in range(m // 2)] + [2 * z + 1 for z in reversed(range(m // 2))]
    return [[order[p] * sides + x for x in range(sides)] for p in range(m)]


def spread_steps(m, across):
    held = [(0, 0)]
    steps = []
    while len(held) < m * (2 if across else 1):
        taken = []
        for shift in (1, -1, 0):
            if shift == 0 and not across:
                continue
            if shift:
                found = [((k, o), (k, (o + shift) % m)) for k, o in held]
            else:
                found = [((k, o), (1 - k, o)) for k, o in held]
            names = [t[2] for t in taken]
            found = [f for f in found if f[1] not in held and f[1] not in names]
            if found:
                best = min(found, key=lambda f: (f[1][0], -min(f[1][1], m - f[1][1]), f[1][1]))
                taken.append((shift,) + best)
        held += [t[2] for t in taken]
        steps.append(taken)
    return steps, held


def move(x, place, shift):
    m = len(place)
    pairs = []
    for p in range(m):
        for side in range(len(place[0])):
            source = place[(p + shift) % m][side] if shift else place[p][1 - side]
            pairs.append((source, place[p][side]))
    return lax.ppermute(x, "query", sorted(pairs))


def owners(place, held, n):
    owner = np.zeros((n, n), np.int32)
    for p in range(len(place)):
        for side in range(len(place[0])):
            for slot, (k, o) in enumerate(held):
                owner[place[p][side], slot] = place[(p + o) % len(place)][side ^ k]
    return owner


def partner(x, size, far):
    return lax.ppermute(x, "entity", [(i, i ^ far) for i in range(size)])


class Shape:
    def __init__(self, tw, sw):
        self.tw, self.sw = tw, sw
        self.half = tw // 2
        self.wide = -(-self.half // 128) * 128
        self.re, self.im = sw, sw + self.wide
        self.total = sw + 2 * self.wide


def put_row(out, student, teacher, shape):
    out[:, : shape.sw] = student.astype(BF16)
    pad = jnp.zeros((teacher.shape[0], shape.wide - shape.half), F32)
    for start, at in ((0, shape.re), (shape.half, shape.im)):
        piece = teacher[:, start : start + shape.half]
        out[:, at : at + shape.wide] = jnp.concatenate([piece, pad], axis=1).astype(BF16)


def pack_kernel(shape, teacher_t, student, anchor_ids, relation_ids, side_flags, out, cols):
    rows = jnp.concatenate([anchor_ids[...], relation_ids[...], side_flags[...]], axis=0).astype(F32)
    rows = jnp.concatenate([rows, jnp.zeros((5, rows.shape[1]), F32)], axis=0)
    cols[...] = rows.T.astype(jnp.int32)
    put_row(out, student[...].astype(F32), teacher_t[...].astype(F32).T, shape)


def pack(teacher, student, ids, shape):
    return pl.pallas_call(
        functools.partial(pack_kernel, shape),
        out_shape=(
            jax.ShapeDtypeStruct((teacher.shape[0], shape.total), BF16),
            jax.ShapeDtypeStruct((ids[0].shape[0], 8), jnp.int32),
        ),
        in_specs=[VMEM] * 5,
        out_specs=(VMEM, VMEM),
        compiler_params=pltpu.CompilerParams(vmem_limit_bytes=60 * MIB),
        name="pack_rows",
    )(teacher.T, student, *[x[None] for x in ids])


def relation_kernel(shape, rel, block, cut, base, cols, table_t, student, out):
    start = base[0] * block
    ids = cols[:, 1:2] - start
    hot = (ids == lax.broadcasted_iota(jnp.int32, (cols.shape[0], block), 1)).astype(F32).astype(BF16)
    tail = block - cut
    lanes = lax.broadcasted_iota(jnp.int32, (shape.tw, tail), 1) + cut
    rows = lax.broadcasted_iota(jnp.int32, (tail, shape.sw), 0) + cut
    table = jnp.where(lanes < rel - start, table_t[:, cut:], jnp.zeros((shape.tw, tail), BF16))
    small = jnp.where(rows < rel - start, student[cut:, :], jnp.zeros((tail, shape.sw), BF16))
    dims = (((1,), (1,)), ((), ()))
    found = lax.dot_general(hot[:, cut:], table, dims, preferred_element_type=F32)
    found_s = jnp.dot(hot[:, cut:], small, preferred_element_type=F32)
    if cut:
        found += lax.dot_general(hot[:, :cut], table_t[:, :cut], dims, preferred_element_type=F32)
        found_s += jnp.dot(hot[:, :cut], student[:cut, :], preferred_element_type=F32)
    put_row(out, found_s, found, shape)


def relation_rows(base, cols, table, student, block, shape):
    rel, tw = table.shape
    q = cols.shape[0]
    cut = max(0, rel - rel // block * block) // 128 * 128
    whole = lambda i, base: (0, 0)
    return pl.pallas_call(
        functools.partial(relation_kernel, shape, rel, block, cut),
        out_shape=jax.ShapeDtypeStruct((q, shape.total), BF16),
        grid_spec=pltpu.PrefetchScalarGridSpec(
            num_scalar_prefetch=1,
            grid=(1,),
            in_specs=[
                pl.BlockSpec((q, cols.shape[1]), whole),
                pl.BlockSpec((tw, block), lambda i, base: (0, base[0])),
                pl.BlockSpec((block, shape.sw), lambda i, base: (base[0], 0)),
            ],
            out_specs=pl.BlockSpec((q, shape.total), whole),
        ),
        compiler_params=pltpu.CompilerParams(vmem_limit_bytes=56 * MIB),
        cost_estimate=pl.CostEstimate(
            flops=2 * q * tw * block, bytes_accessed=2 * tw * block, transcendentals=0
        ),
        name="relation_rows",
    )(base, cols, table.T, student)


def load_shards(shards, table, sems, own):
    copies = [
        pltpu.make_async_copy(shard, table.at[pl.ds(j * own, own)], sems.at[j]) for j, shard in enumerate(shards)
    ]
    for copy in copies:
        copy.start()
    return copies


def anchor_kernel(count, own, has_acc, bases, cols, *rest):
    acc_in, rest = (rest[0], rest[1:]) if has_acc else (None, rest)
    shards, (out, table, hot, sems) = rest[:count], rest[count:]
    copies = load_shards(shards, table, sems, own)
    q = cols.shape[0]
    ids = cols[:, 0:1]
    lane = lax.broadcasted_iota(jnp.int32, (q, own), 1)
    for j in range(count):
        hot[:, j * own : (j + 1) * own] = (ids - bases[j] == lane).astype(F32).astype(BF16)
    for copy in copies:
        copy.wait()
    found = jnp.dot(hot[...], table[...], preferred_element_type=F32).astype(BF16)
    out[...] = found + acc_in[...] if has_acc else found


def anchor_rows(bases, ids, shards, acc, shape):
    own = shards[0].shape[0]
    q, count = ids.shape[0], len(shards)
    operands = [bases, ids] + ([] if acc is None else [acc]) + list(shards)
    return pl.pallas_call(
        functools.partial(anchor_kernel, count, own, acc is not None),
        out_shape=jax.ShapeDtypeStruct((q, shape.total), BF16),
        in_specs=[SMEM, VMEM] + ([] if acc is None else [VMEM]) + [ANY] * count,
        out_specs=VMEM,
        scratch_shapes=[
            pltpu.VMEM((count * own, shape.total), BF16),
            pltpu.VMEM((q, count * own), BF16),
            pltpu.SemaphoreType.DMA((count,)),
        ],
        compiler_params=pltpu.CompilerParams(vmem_limit_bytes=2 * count * own * (shape.total + q) + 12 * MIB),
        cost_estimate=pl.CostEstimate(
            flops=2 * q * count * own * shape.total,
            bytes_accessed=2 * (count * own + 2 * q) * shape.total,
            transcendentals=0,
        ),
        name="anchor_rows",
    )(*operands)


def score_kernel(shape, own, n, chunk, mine, other, relation, relation_b, cols, *rest):
    shards, (t_out, s_out, stats, q_student, table, q_teacher, sems) = rest[:n], rest[n:]
    copies = load_shards(shards, table, sems, own)
    q = mine.shape[0]
    sw, wide = shape.sw, shape.wide
    rows = 128

    def build(i, _):
        at = pl.ds(pl.multiple_of(i * rows, rows), rows)
        g = (2 * cols[at, 2:3] - 1).astype(F32)
        a = mine[at, :].astype(F32) + other[at, :].astype(F32)
        r = relation[at, :].astype(F32) + relation_b[at, :].astype(F32)
        a_re, a_im = a[:, shape.re : shape.re + wide], a[:, shape.im : shape.im + wide]
        r_re, r_im = r[:, shape.re : shape.re + wide], r[:, shape.im : shape.im + wide]
        q_teacher[at, :wide] = (a_re * r_re - g * a_im * r_im).astype(BF16)
        q_teacher[at, wide:] = (a_im * r_re + g * a_re * r_im).astype(BF16)
        a_s, r_s = a[:, :sw], r[:, :sw]
        a_x, r_x = pltpu.roll(a_s, sw // 2, 1), pltpu.roll(r_s, sw // 2, 1)
        low = lax.broadcasted_iota(jnp.int32, (rows, sw), 1) < sw // 2
        re2, im2 = jnp.where(low, r_s, r_x), jnp.where(low, r_x, r_s)
        q_student[at, :] = (a_s * re2 + jnp.where(low, -g, g) * a_x * im2).astype(BF16)
        return 0

    lax.fori_loop(0, q // rows, build, 0)
    for copy in copies:
        copy.wait()

    dims = (((1,), (1,)), ((), ()))

    def score(c, carry):
        top_t, total_t, weighted, top_s, total_s = carry
        at = pl.ds(pl.multiple_of(c * chunk, chunk), chunk)
        t = lax.dot_general(table[at, sw:], q_teacher[...], dims, preferred_element_type=F32)
        s = lax.dot_general(table[at, :sw], q_student[...], dims, preferred_element_type=F32)
        t_out[at, :] = t
        s_out[at, :] = s
        new_t = jnp.maximum(top_t, jnp.max(t, axis=0, keepdims=True))
        new_s = jnp.maximum(top_s, jnp.max(s, axis=0, keepdims=True))
        scale_t, scale_s = jnp.exp(top_t - new_t), jnp.exp(top_s - new_s)
        e = jnp.exp(t - new_t)
        total_t = total_t * scale_t + jnp.sum(e, axis=0, keepdims=True)
        weighted = weighted * scale_t + jnp.sum(e * (t - s), axis=0, keepdims=True)
        total_s = total_s * scale_s + jnp.sum(jnp.exp(s - new_s), axis=0, keepdims=True)
        return new_t, total_t, weighted, new_s, total_s

    lowest = jnp.full((1, q), -jnp.inf, F32)
    nothing = jnp.zeros((1, q), F32)
    found = lax.fori_loop(0, n * own // chunk, score, (lowest, nothing, nothing, lowest, nothing), unroll=True)
    stats[...] = jnp.concatenate(list(found) + [nothing] * 3, axis=0)


def scores(mine, other, relation, relation_b, cols, shards, shape):
    n, own = len(shards), shards[0].shape[0]
    q = mine.shape[0]
    slab = n * own
    chunk = 512 if slab % 512 == 0 else own
    return pl.pallas_call(
        functools.partial(score_kernel, shape, own, n, chunk),
        out_shape=(
            jax.ShapeDtypeStruct((slab, q), F32),
            jax.ShapeDtypeStruct((slab, q), F32),
            jax.ShapeDtypeStruct((8, q), F32),
            jax.ShapeDtypeStruct((q, shape.sw), BF16),
        ),
        in_specs=[VMEM] * 5 + [ANY] * n,
        out_specs=(VMEM,) * 4,
        scratch_shapes=[
            pltpu.VMEM((slab, shape.total), BF16),
            pltpu.VMEM((q, 2 * shape.wide), BF16),
            pltpu.SemaphoreType.DMA((n,)),
        ],
        compiler_params=pltpu.CompilerParams(vmem_limit_bytes=8 * slab * q + 2 * slab * shape.total + 10 * MIB),
        cost_estimate=pl.CostEstimate(
            flops=2 * q * slab * shape.total, bytes_accessed=2 * slab * shape.total + 8 * slab * q, transcendentals=2 * slab * q
        ),
        name="scores",
    )(mine, other, relation, relation_b, cols, *shards)


def combine(a, b):
    top_t, top_s = jnp.maximum(a[0:1], b[0:1]), jnp.maximum(a[3:4], b[3:4])
    at, bt = jnp.exp(a[0:1] - top_t), jnp.exp(b[0:1] - top_t)
    as_, bs = jnp.exp(a[3:4] - top_s), jnp.exp(b[3:4] - top_s)
    total_t = a[1:2] * at + b[1:2] * bt
    weighted = a[2:3] * at + b[2:3] * bt
    total_s = a[4:5] * as_ + b[4:5] * bs
    return top_t, total_t, weighted, top_s, total_s


def grad_kernel(n, own, chunk, sw, order, t_in, s_in, mine, other, q_student, *rest):
    shards, (divergence, q_grad), outs = rest[:n], rest[n : n + 2], rest[n + 2 : -3]
    table, e_grad, sems = rest[-3:]
    copies = [
        pltpu.make_async_copy(shard.at[:, pl.ds(0, sw)], table.at[pl.ds(j * own, own)], sems.at[j])
        for j, shard in enumerate(shards)
    ]
    for copy in copies:
        copy.start()
    top_t, total_t, weighted, top_s, total_s = combine(mine[...], other[...])
    divergence[...] = weighted / total_t - top_t - jnp.log(total_t) + top_s + jnp.log(total_s)
    over_t, over_s = 1.0 / total_t, 1.0 / total_s
    for copy in copies:
        copy.wait()
    per = chunk // own

    def step(c, total):
        at = pl.ds(pl.multiple_of(c * chunk, chunk), chunk)
        prob_t = jnp.exp(t_in[at, :] - top_t) * over_t
        prob_s = jnp.exp(s_in[at, :] - top_s) * over_s
        weights = (prob_s - prob_t).astype(BF16)
        grad = jnp.dot(weights, q_student[...], preferred_element_type=F32).astype(BF16)
        for k in range(per):
            e_grad[order[c * per + k]] = grad[k * own : (k + 1) * own, :]
        return total + lax.dot_general(
            table[at, :], weights, (((0,), (0,)), ((), ())), preferred_element_type=F32
        )

    q = q_student.shape[0]
    total = lax.fori_loop(0, n * own // chunk, step, jnp.zeros((sw, q), F32), unroll=True)
    q_grad[...] = total.T
    count = n // len(outs)
    for d, out in enumerate(outs):
        out[...] = e_grad[d * count : (d + 1) * count]


def gradients(order, near, t, s, mine, other, q_student, shards):
    n, own = len(shards), shards[0].shape[0]
    q, sw = q_student.shape
    slab = n * own
    chunk = 512 if slab % 512 == 0 else own
    return pl.pallas_call(
        functools.partial(grad_kernel, n, own, chunk, sw),
        out_shape=(
            jax.ShapeDtypeStruct((1, q), F32),
            jax.ShapeDtypeStruct((q, sw), F32),
        )
        + (jax.ShapeDtypeStruct((n // near, own, sw), BF16),) * near,
        in_specs=[SMEM] + [VMEM] * 5 + [ANY] * n,
        out_specs=(VMEM,) * (2 + near),
        scratch_shapes=[
            pltpu.VMEM((slab, sw), BF16),
            pltpu.VMEM((n, own, sw), BF16),
            pltpu.SemaphoreType.DMA((n,)),
        ],
        compiler_params=pltpu.CompilerParams(vmem_limit_bytes=8 * slab * q + 10 * MIB),
        cost_estimate=pl.CostEstimate(
            flops=4 * q * slab * sw, bytes_accessed=8 * slab * q, transcendentals=2 * slab * q
        ),
        name="gradients",
    )(order, t, s, mine, other, q_student, *shards)


def add_kernel(count, *refs):
    terms, outs = refs[:count], refs[count:]
    for e, out in enumerate(outs):
        total = terms[0][e].astype(F32)
        for term in terms[1:]:
            total += term[e].astype(F32)
        out[...] = total.astype(out.dtype)


def add_blocks(terms):
    far, own, sw = terms[0].shape
    return pl.pallas_call(
        functools.partial(add_kernel, len(terms)),
        out_shape=(jax.ShapeDtypeStruct((own, sw), F32),)
        + (jax.ShapeDtypeStruct((own, sw), BF16),) * (far - 1),
        in_specs=[VMEM] * len(terms),
        out_specs=(VMEM,) * far,
        compiler_params=pltpu.CompilerParams(vmem_limit_bytes=8 * MIB),
        name="add_blocks",
    )(*terms)


def reduce_blocks(blocks, beside, n):
    near, far = len(blocks), n // len(blocks)
    terms = [blocks[0]]
    for d in range(1, near):
        terms.append(lax.ppermute(blocks[d], "query", [(i, i ^ d) for i in range(n)]))
    terms[-1], beside = lax.optimization_barrier((terms[-1], beside))
    sums = add_blocks(terms)
    total = sums[0]
    for e in range(1, far):
        pairs = [(h * near + r, (h + e) % far * near + r) for h in range(far) for r in range(near)]
        total = total + lax.ppermute(sums[e], "query", pairs).astype(F32)
    return total, beside


def make(n, groups):
    place = places(n)
    steps, held = spread_steps(len(place), len(place[0]) == 2)
    table = owners(place, held, n)
    near = next(k for k in (4, 2, 1) if n % k == 0)
    me = np.arange(n)[:, None]
    position = ((table % near) ^ (me % near)) * (n // near) + (table // near - me // near) % (n // near)

    def per_device(
        anchor_ids,
        relation_ids,
        side_flags,
        teacher_entities,
        student_entities,
        teacher_relations,
        student_relations,
    ):
        own, tw = teacher_entities.shape
        shape = Shape(tw, student_entities.shape[1])
        owner, order = jnp.asarray(np.stack([table, position], axis=1))[lax.axis_index("query")]
        bases = (owner + lax.axis_index("entity") * n) * own
        packed, cols = pack(
            teacher_entities, student_entities, (anchor_ids, relation_ids, side_flags), shape
        )
        have = {(0, 0): packed}
        block = -(-teacher_relations.shape[0] // 512) * 256
        base = (lax.axis_index("entity") % 2).astype(jnp.int32)[None]
        own_key = (0, 0)
        have[own_key], base = lax.optimization_barrier((have[own_key], base))
        anchors, counted = None, 0
        kept, last = {}, {}
        for number, step in enumerate(steps):
            got = {}
            for shift, old, new in step:
                operand = have[old]
                if shift in last and last[shift] != old:
                    before = last[shift]
                    operand, kept[before] = lax.optimization_barrier((operand, have[before]))
                got[new] = move(operand, place, shift)
                last[shift] = new
            if number == 0:
                relation = relation_rows(base, cols, teacher_relations, student_relations, block, shape)
                got, relation = lax.optimization_barrier((got, relation))
                relation_b = partner(relation, groups, 1)
            if number == len(steps) - 1:
                counted = len(have)
                names = held[:counted]
                anchors = anchor_rows(bases, cols, [kept.get(h, have[h]) for h in names], None, shape)
            have.update(got)
        have.update(kept)
        shards = [have[h] for h in held]
        mine = anchor_rows(bases[counted:], cols, shards[counted:], anchors, shape)
        far = 1
        while far < groups // 2:
            mine = mine + partner(mine, groups, far)
            far *= 2
        other = partner(mine, groups, far)
        t, s, stats, q_student = scores(mine, other, relation, relation_b, cols, shards, shape)
        far = 1
        while far < groups // 2:
            found = combine(stats, partner(stats, groups, far))
            stats = jnp.concatenate(list(found) + [jnp.zeros_like(found[0])] * 3, axis=0)
            far *= 2
        divergence, q_grad, *blocks = gradients(
            order, near, t, s, stats, partner(stats, groups, far), q_student, shards
        )
        far = 1
        while far < groups:
            q_grad = q_grad + partner(q_grad, groups, far)
            far *= 2
        entity_grad, q_grad = reduce_blocks(blocks, q_grad, n)
        return (divergence[0], entity_grad, q_grad)

    return per_device


def solution(mesh):
    in_specs = (
        P("query"),
        P("query"),
        P("query"),
        P(("entity", "query"), None),
        P(("entity", "query"), None),
        P(),
        P(),
    )
    out_specs = (P("query"), P(("entity", "query"), None), P("query", None))
    return jax.shard_map(
        make(mesh.shape["query"], mesh.shape["entity"]),
        mesh=mesh, in_specs=in_specs, out_specs=out_specs, check_vma=False,
    )
```

```python
import functools

import jax
import jax.numpy as jnp
import numpy as np
from jax import lax
from jax.experimental import pallas as pl
from jax.experimental.pallas import tpu as pltpu
from jax.sharding import PartitionSpec as P

F32 = jnp.float32
BF16 = jnp.bfloat16
VMEM = pl.BlockSpec(memory_space=pltpu.VMEM)
SMEM = pl.BlockSpec(memory_space=pltpu.SMEM)
MIB = 1 << 20


def places(n):
    sides = 2 if n % 2 == 0 else 1
    m = n // sides
    order = list(range(m))
    if m % 2 == 0:
        order = [2 * z for z in range(m // 2)] + [2 * z + 1 for z in reversed(range(m // 2))]
    return [[order[p] * sides + x for x in range(sides)] for p in range(m)]


def spread_steps(m, across):
    held = [(0, 0)]
    steps = []
    while len(held) < m * (2 if across else 1):
        taken = []
        for shift in (1, -1, 0):
            if shift == 0 and not across:
                continue
            if shift:
                found = [((k, o), (k, (o + shift) % m)) for k, o in held]
            else:
                found = [((k, o), (1 - k, o)) for k, o in held]
            names = [t[2] for t in taken]
            found = [f for f in found if f[1] not in held and f[1] not in names]
            if found:
                best = min(found, key=lambda f: (f[1][0], -min(f[1][1], m - f[1][1]), f[1][1]))
                taken.append((shift,) + best)
        held += [t[2] for t in taken]
        steps.append(taken)
    return steps, held


def move(x, place, shift):
    m = len(place)
    pairs = []
    for p in range(m):
        for side in range(len(place[0])):
            source = place[(p + shift) % m][side] if shift else place[p][1 - side]
            pairs.append((source, place[p][side]))
    return lax.ppermute(x, "query", sorted(pairs))


def owners(place, held, n):
    owner = np.zeros((n, n), np.int32)
    for p in range(len(place)):
        for side in range(len(place[0])):
            for slot, (k, o) in enumerate(held):
                owner[place[p][side], slot] = place[(p + o) % len(place)][side ^ k]
    return owner


def partner(x, size, far):
    return lax.ppermute(x, "entity", [(i, i ^ far) for i in range(size)])


class Shape:
    def __init__(self, tw, sw):
        self.tw, self.sw = tw, sw
        self.half = tw // 2
        self.wide = -(-self.half // 128) * 128
        self.re, self.im = sw, sw + self.wide
        self.total = sw + 2 * self.wide


def put_row(out, student, teacher, shape):
    out[:, : shape.sw] = student.astype(BF16)
    pad = jnp.zeros((teacher.shape[0], shape.wide - shape.half), F32)
    for start, at in ((0, shape.re), (shape.half, shape.im)):
        piece = teacher[:, start : start + shape.half]
        out[:, at : at + shape.wide] = jnp.concatenate([piece, pad], axis=1).astype(BF16)


def pack_kernel(shape, teacher_t, student, anchor_ids, relation_ids, side_flags, out, cols):
    rows = jnp.concatenate([anchor_ids[...], relation_ids[...], side_flags[...]], axis=0).astype(F32)
    rows = jnp.concatenate([rows, jnp.zeros((5, rows.shape[1]), F32)], axis=0)
    cols[...] = rows.T.astype(jnp.int32)
    put_row(out, student[...].astype(F32), teacher_t[...].astype(F32).T, shape)


def pack(teacher, student, ids, shape):
    return pl.pallas_call(
        functools.partial(pack_kernel, shape),
        out_shape=(
            jax.ShapeDtypeStruct((teacher.shape[0], shape.total), BF16),
            jax.ShapeDtypeStruct((ids[0].shape[0], 8), jnp.int32),
        ),
        in_specs=[VMEM] * 5,
        out_specs=(VMEM, VMEM),
        compiler_params=pltpu.CompilerParams(vmem_limit_bytes=60 * MIB),
        name="pack_rows",
    )(teacher.T, student, *[x[None] for x in ids])


def relation_kernel(shape, rel, block, cut, base, cols, table_t, student, out):
    start = base[0] * block
    ids = cols[:, 1:2] - start
    hot = (ids == lax.broadcasted_iota(jnp.int32, (cols.shape[0], block), 1)).astype(F32).astype(BF16)
    tail = block - cut
    lanes = lax.broadcasted_iota(jnp.int32, (shape.tw, tail), 1) + cut
    rows = lax.broadcasted_iota(jnp.int32, (tail, shape.sw), 0) + cut
    table = jnp.where(lanes < rel - start, table_t[:, cut:], jnp.zeros((shape.tw, tail), BF16))
    small = jnp.where(rows < rel - start, student[cut:, :], jnp.zeros((tail, shape.sw), BF16))
    dims = (((1,), (1,)), ((), ()))
    found = lax.dot_general(hot[:, cut:], table, dims, preferred_element_type=F32)
    found_s = jnp.dot(hot[:, cut:], small, preferred_element_type=F32)
    if cut:
        found += lax.dot_general(hot[:, :cut], table_t[:, :cut], dims, preferred_element_type=F32)
        found_s += jnp.dot(hot[:, :cut], student[:cut, :], preferred_element_type=F32)
    put_row(out, found_s, found, shape)


def relation_rows(base, cols, table, student, block, shape):
    rel, tw = table.shape
    q = cols.shape[0]
    cut = max(0, rel - rel // block * block) // 128 * 128
    whole = lambda i, base: (0, 0)
    return pl.pallas_call(
        functools.partial(relation_kernel, shape, rel, block, cut),
        out_shape=jax.ShapeDtypeStruct((q, shape.total), BF16),
        grid_spec=pltpu.PrefetchScalarGridSpec(
            num_scalar_prefetch=1,
            grid=(1,),
            in_specs=[
                pl.BlockSpec((q, cols.shape[1]), whole),
                pl.BlockSpec((tw, block), lambda i, base: (0, base[0])),
                pl.BlockSpec((block, shape.sw), lambda i, base: (base[0], 0)),
            ],
            out_specs=pl.BlockSpec((q, shape.total), whole),
        ),
        compiler_params=pltpu.CompilerParams(vmem_limit_bytes=56 * MIB),
        cost_estimate=pl.CostEstimate(
            flops=2 * q * tw * block, bytes_accessed=2 * tw * block, transcendentals=0
        ),
        name="relation_rows",
    )(base, cols, table.T, student)


def joined(shards, columns):
    return jnp.concatenate([shard[:, columns] for shard in shards], axis=0)


def anchor_kernel(count, own, has_acc, bases, cols, *rest):
    acc_in, rest = (rest[0], rest[1:]) if has_acc else (None, rest)
    shards, out = rest[:count], rest[count]
    ids = cols[:, 0:1]
    lane = lax.broadcasted_iota(jnp.int32, (cols.shape[0], own), 1)
    group = max(1, 512 // own)
    total = None
    for first in range(0, count, group):
        last = min(count, first + group)
        hot = jnp.concatenate([(ids - bases[j] == lane).astype(F32).astype(BF16) for j in range(first, last)], axis=1)
        found = jnp.dot(hot, joined(shards[first:last], slice(None)), preferred_element_type=F32)
        total = found if total is None else total + found
    total = total.astype(BF16)
    out[...] = total + acc_in[...] if has_acc else total


def anchor_rows(bases, cols, shards, acc, shape):
    own = shards[0].shape[0]
    q, count = cols.shape[0], len(shards)
    operands = [bases, cols] + ([] if acc is None else [acc]) + list(shards)
    return pl.pallas_call(
        functools.partial(anchor_kernel, count, own, acc is not None),
        out_shape=jax.ShapeDtypeStruct((q, shape.total), BF16),
        in_specs=[SMEM, VMEM] + ([] if acc is None else [VMEM]) + [VMEM] * count,
        out_specs=VMEM,
        compiler_params=pltpu.CompilerParams(vmem_limit_bytes=2 * count * own * (shape.total + q) + 12 * MIB),
        cost_estimate=pl.CostEstimate(
            flops=2 * q * count * own * shape.total,
            bytes_accessed=2 * (count * own + 2 * q) * shape.total,
            transcendentals=0,
        ),
        name="anchor_rows",
    )(*operands)


def score_kernel(shape, own, n, chunk, mine, other, relation, relation_b, cols, *rest):
    shards, (t_out, s_out, stats, q_student, q_teacher) = rest[:n], rest[n:]
    q = mine.shape[0]
    sw, wide = shape.sw, shape.wide
    rows = 128

    def build(i, _):
        at = pl.ds(pl.multiple_of(i * rows, rows), rows)
        g = (2 * cols[at, 2:3] - 1).astype(F32)
        a = mine[at, :].astype(F32) + other[at, :].astype(F32)
        r = relation[at, :].astype(F32) + relation_b[at, :].astype(F32)
        a_re, a_im = a[:, shape.re : shape.re + wide], a[:, shape.im : shape.im + wide]
        r_re, r_im = r[:, shape.re : shape.re + wide], r[:, shape.im : shape.im + wide]
        q_teacher[at, :wide] = (a_re * r_re - g * a_im * r_im).astype(BF16)
        q_teacher[at, wide:] = (a_im * r_re + g * a_re * r_im).astype(BF16)
        a_s, r_s = a[:, :sw], r[:, :sw]
        a_x, r_x = pltpu.roll(a_s, sw // 2, 1), pltpu.roll(r_s, sw // 2, 1)
        low = lax.broadcasted_iota(jnp.int32, (rows, sw), 1) < sw // 2
        re2, im2 = jnp.where(low, r_s, r_x), jnp.where(low, r_x, r_s)
        q_student[at, :] = (a_s * re2 + jnp.where(low, -g, g) * a_x * im2).astype(BF16)
        return 0

    lax.fori_loop(0, q // rows, build, 0)
    dims = (((1,), (1,)), ((), ()))

    def score(c, carry):
        top_t, total_t, weighted, top_s, total_s = carry
        at = slice(c * chunk, (c + 1) * chunk)
        group = shards[c * chunk // own : (c + 1) * chunk // own]
        t = lax.dot_general(joined(group, slice(sw, None)), q_teacher[...], dims, preferred_element_type=F32)
        s = lax.dot_general(joined(group, slice(0, sw)), q_student[...], dims, preferred_element_type=F32)
        t_out[at, :] = t
        s_out[at, :] = s
        new_t = jnp.maximum(top_t, jnp.max(t, axis=0, keepdims=True))
        new_s = jnp.maximum(top_s, jnp.max(s, axis=0, keepdims=True))
        scale_t, scale_s = jnp.exp(top_t - new_t), jnp.exp(top_s - new_s)
        e = jnp.exp(t - new_t)
        total_t = total_t * scale_t + jnp.sum(e, axis=0, keepdims=True)
        weighted = weighted * scale_t + jnp.sum(e * (t - s), axis=0, keepdims=True)
        total_s = total_s * scale_s + jnp.sum(jnp.exp(s - new_s), axis=0, keepdims=True)
        return new_t, total_t, weighted, new_s, total_s

    lowest = jnp.full((1, q), -jnp.inf, F32)
    nothing = jnp.zeros((1, q), F32)
    found = (lowest, nothing, nothing, lowest, nothing)
    for c in range(n * own // chunk):
        found = score(c, found)
    stats[...] = jnp.concatenate(list(found) + [nothing] * 3, axis=0)


def scores(mine, other, relation, relation_b, cols, shards, shape):
    n, own = len(shards), shards[0].shape[0]
    q = mine.shape[0]
    slab = n * own
    chunk = 512 if slab % 512 == 0 else own
    return pl.pallas_call(
        functools.partial(score_kernel, shape, own, n, chunk),
        out_shape=(
            jax.ShapeDtypeStruct((slab, q), F32),
            jax.ShapeDtypeStruct((slab, q), F32),
            jax.ShapeDtypeStruct((8, q), F32),
            jax.ShapeDtypeStruct((q, shape.sw), BF16),
        ),
        in_specs=[VMEM] * (5 + n),
        out_specs=(VMEM,) * 4,
        scratch_shapes=[pltpu.VMEM((q, 2 * shape.wide), BF16)],
        compiler_params=pltpu.CompilerParams(vmem_limit_bytes=8 * slab * q + 2 * slab * shape.total + 10 * MIB),
        cost_estimate=pl.CostEstimate(
            flops=2 * q * slab * shape.total, bytes_accessed=2 * slab * shape.total + 8 * slab * q, transcendentals=2 * slab * q
        ),
        name="scores",
    )(mine, other, relation, relation_b, cols, *shards)


def combine(a, b):
    top_t, top_s = jnp.maximum(a[0:1], b[0:1]), jnp.maximum(a[3:4], b[3:4])
    at, bt = jnp.exp(a[0:1] - top_t), jnp.exp(b[0:1] - top_t)
    as_, bs = jnp.exp(a[3:4] - top_s), jnp.exp(b[3:4] - top_s)
    total_t = a[1:2] * at + b[1:2] * bt
    weighted = a[2:3] * at + b[2:3] * bt
    total_s = a[4:5] * as_ + b[4:5] * bs
    return top_t, total_t, weighted, top_s, total_s


def grad_kernel(n, own, chunk, sw, order, t_in, s_in, mine, other, q_student, *rest):
    shards, (divergence, q_grad), outs = rest[:n], rest[n : n + 2], rest[n + 2 : -1]
    e_grad = rest[-1]
    top_t, total_t, weighted, top_s, total_s = combine(mine[...], other[...])
    divergence[...] = weighted / total_t - top_t - jnp.log(total_t) + top_s + jnp.log(total_s)
    over_t, over_s = 1.0 / total_t, 1.0 / total_s
    per = chunk // own

    def step(c, total):
        at = slice(c * chunk, (c + 1) * chunk)
        prob_t = jnp.exp(t_in[at, :] - top_t) * over_t
        prob_s = jnp.exp(s_in[at, :] - top_s) * over_s
        weights = (prob_s - prob_t).astype(BF16)
        grad = jnp.dot(weights, q_student[...], preferred_element_type=F32).astype(BF16)
        for k in range(per):
            e_grad[order[c * per + k]] = grad[k * own : (k + 1) * own, :]
        return total + lax.dot_general(
            joined(shards[c * per : (c + 1) * per], slice(0, sw)),
            weights,
            (((0,), (0,)), ((), ())),
            preferred_element_type=F32,
        )

    q = q_student.shape[0]
    total = jnp.zeros((sw, q), F32)
    for c in range(n * own // chunk):
        total = step(c, total)
    q_grad[...] = total.T
    count = n // len(outs)
    for d, out in enumerate(outs):
        out[...] = e_grad[d * count : (d + 1) * count]


def gradients(order, near, t, s, mine, other, q_student, shards):
    n, own = len(shards), shards[0].shape[0]
    q, sw = q_student.shape
    slab = n * own
    shape_total = shards[0].shape[1]
    chunk = 512 if slab % 512 == 0 else own
    return pl.pallas_call(
        functools.partial(grad_kernel, n, own, chunk, sw),
        out_shape=(
            jax.ShapeDtypeStruct((1, q), F32),
            jax.ShapeDtypeStruct((q, sw), F32),
        )
        + (jax.ShapeDtypeStruct((n // near, own, sw), BF16),) * near,
        in_specs=[SMEM] + [VMEM] * (5 + n),
        out_specs=(VMEM,) * (2 + near),
        scratch_shapes=[pltpu.VMEM((n, own, sw), BF16)],
        compiler_params=pltpu.CompilerParams(vmem_limit_bytes=8 * slab * q + 2 * slab * shape_total + 10 * MIB),
        cost_estimate=pl.CostEstimate(
            flops=4 * q * slab * sw, bytes_accessed=8 * slab * q, transcendentals=2 * slab * q
        ),
        name="gradients",
    )(order, t, s, mine, other, q_student, *shards)


def add_kernel(count, *refs):
    terms, outs = refs[:count], refs[count:]
    for e, out in enumerate(outs):
        total = terms[0][e].astype(F32)
        for term in terms[1:]:
            total += term[e].astype(F32)
        out[...] = total.astype(out.dtype)


def add_blocks(terms):
    far, own, sw = terms[0].shape
    return pl.pallas_call(
        functools.partial(add_kernel, len(terms)),
        out_shape=(jax.ShapeDtypeStruct((own, sw), F32),)
        + (jax.ShapeDtypeStruct((own, sw), BF16),) * (far - 1),
        in_specs=[VMEM] * len(terms),
        out_specs=(VMEM,) * far,
        compiler_params=pltpu.CompilerParams(vmem_limit_bytes=8 * MIB),
        name="add_blocks",
    )(*terms)


def reduce_blocks(blocks, beside, n):
    near, far = len(blocks), n // len(blocks)
    terms = [blocks[0]]
    for d in range(1, near):
        terms.append(lax.ppermute(blocks[d], "query", [(i, i ^ d) for i in range(n)]))
    terms[-1], beside = lax.optimization_barrier((terms[-1], beside))
    sums = add_blocks(terms)
    total = sums[0]
    for e in range(1, far):
        pairs = [(h * near + r, (h + e) % far * near + r) for h in range(far) for r in range(near)]
        total = total + lax.ppermute(sums[e], "query", pairs).astype(F32)
    return total, beside


def make(n, groups):
    place = places(n)
    steps, held = spread_steps(len(place), len(place[0]) == 2)
    table = owners(place, held, n)
    near = next(k for k in (4, 2, 1) if n % k == 0)
    me = np.arange(n)[:, None]
    position = ((table % near) ^ (me % near)) * (n // near) + (table // near - me // near) % (n // near)

    def per_device(
        anchor_ids,
        relation_ids,
        side_flags,
        teacher_entities,
        student_entities,
        teacher_relations,
        student_relations,
    ):
        own, tw = teacher_entities.shape
        shape = Shape(tw, student_entities.shape[1])
        owner, order = jnp.asarray(np.stack([table, position], axis=1))[lax.axis_index("query")]
        bases = (owner + lax.axis_index("entity") * n) * own
        packed, cols = pack(
            teacher_entities, student_entities, (anchor_ids, relation_ids, side_flags), shape
        )
        have = {(0, 0): packed}
        block = -(-teacher_relations.shape[0] // 512) * 256
        base = (lax.axis_index("entity") % 2).astype(jnp.int32)[None]
        own_key = (0, 0)
        have[own_key], base = lax.optimization_barrier((have[own_key], base))
        anchors, counted = None, 0
        kept, last = {}, {}
        for number, step in enumerate(steps):
            got = {}
            for shift, old, new in step:
                operand = have[old]
                if shift in last and last[shift] != old:
                    before = last[shift]
                    operand, kept[before] = lax.optimization_barrier((operand, have[before]))
                got[new] = move(operand, place, shift)
                last[shift] = new
            if number == 0:
                relation = relation_rows(base, cols, teacher_relations, student_relations, block, shape)
                got, relation = lax.optimization_barrier((got, relation))
                relation_b = partner(relation, groups, 1)
            if number == len(steps) - 1:
                counted = len(have)
                names = held[:counted]
                anchors = anchor_rows(bases, cols, [kept.get(h, have[h]) for h in names], None, shape)
            have.update(got)
        have.update(kept)
        shards = [have[h] for h in held]
        mine = anchor_rows(bases[counted:], cols, shards[counted:], anchors, shape)
        far = 1
        while far < groups // 2:
            mine = mine + partner(mine, groups, far)
            far *= 2
        other = partner(mine, groups, far)
        t, s, stats, q_student = scores(mine, other, relation, relation_b, cols, shards, shape)
        far = 1
        while far < groups // 2:
            found = combine(stats, partner(stats, groups, far))
            stats = jnp.concatenate(list(found) + [jnp.zeros_like(found[0])] * 3, axis=0)
            far *= 2
        divergence, q_grad, *blocks = gradients(
            order, near, t, s, stats, partner(stats, groups, far), q_student, shards
        )
        far = 1
        while far < groups:
            q_grad = q_grad + partner(q_grad, groups, far)
            far *= 2
        entity_grad, q_grad = reduce_blocks(blocks, q_grad, n)
        return (divergence[0], entity_grad, q_grad)

    return per_device


def solution(mesh):
    in_specs = (
        P("query"),
        P("query"),
        P("query"),
        P(("entity", "query"), None),
        P(("entity", "query"), None),
        P(),
        P(),
    )
    out_specs = (P("query"), P(("entity", "query"), None), P("query", None))
    return jax.shard_map(
        make(mesh.shape["query"], mesh.shape["entity"]),
        mesh=mesh, in_specs=in_specs, out_specs=out_specs, check_vma=False,
    )
```

```python
import functools

import jax
import jax.numpy as jnp
import numpy as np
from jax import lax
from jax.experimental import pallas as pl
from jax.experimental.pallas import tpu as pltpu
from jax.sharding import PartitionSpec as P

F32 = jnp.float32
BF16 = jnp.bfloat16
VMEM = pl.BlockSpec(memory_space=pltpu.VMEM)
SMEM = pl.BlockSpec(memory_space=pltpu.SMEM)
MIB = 1 << 20


def places(n):
    sides = 2 if n % 2 == 0 else 1
    m = n // sides
    order = list(range(m))
    if m % 2 == 0:
        order = [2 * z for z in range(m // 2)] + [2 * z + 1 for z in reversed(range(m // 2))]
    return [[order[p] * sides + x for x in range(sides)] for p in range(m)]


def spread_steps(m, across):
    held = [(0, 0)]
    steps = []
    while len(held) < m * (2 if across else 1):
        taken = []
        for shift in (1, -1, 0):
            if shift == 0 and not across:
                continue
            if shift:
                found = [((k, o), (k, (o + shift) % m)) for k, o in held]
            else:
                found = [((k, o), (1 - k, o)) for k, o in held]
            names = [t[2] for t in taken]
            found = [f for f in found if f[1] not in held and f[1] not in names]
            if found:
                best = min(found, key=lambda f: (f[1][0], -min(f[1][1], m - f[1][1]), f[1][1]))
                taken.append((shift,) + best)
        held += [t[2] for t in taken]
        steps.append(taken)
    return steps, held


def move(x, place, shift):
    m = len(place)
    pairs = []
    for p in range(m):
        for side in range(len(place[0])):
            source = place[(p + shift) % m][side] if shift else place[p][1 - side]
            pairs.append((source, place[p][side]))
    return lax.ppermute(x, "query", sorted(pairs))


def owners(place, held, n):
    owner = np.zeros((n, n), np.int32)
    for p in range(len(place)):
        for side in range(len(place[0])):
            for slot, (k, o) in enumerate(held):
                owner[place[p][side], slot] = place[(p + o) % len(place)][side ^ k]
    return owner


def partner(x, size, far):
    return lax.ppermute(x, "entity", [(i, i ^ far) for i in range(size)])


class Shape:
    def __init__(self, tw, sw):
        self.tw, self.sw = tw, sw
        self.half = tw // 2
        self.wide = -(-self.half // 128) * 128
        self.re, self.im = sw, sw + self.wide
        self.total = sw + 2 * self.wide


def put_row(out, student, teacher, shape):
    out[:, : shape.sw] = student.astype(BF16)
    pad = jnp.zeros((teacher.shape[0], shape.wide - shape.half), F32)
    for start, at in ((0, shape.re), (shape.half, shape.im)):
        piece = teacher[:, start : start + shape.half]
        out[:, at : at + shape.wide] = jnp.concatenate([piece, pad], axis=1).astype(BF16)


def pack_kernel(shape, teacher_t, student, anchor_ids, relation_ids, side_flags, out, cols):
    rows = jnp.concatenate([anchor_ids[...], relation_ids[...], side_flags[...]], axis=0).astype(F32)
    rows = jnp.concatenate([rows, jnp.zeros((5, rows.shape[1]), F32)], axis=0)
    cols[...] = rows.T.astype(jnp.int32)
    put_row(out, student[...].astype(F32), teacher_t[...].astype(F32).T, shape)


def pack(teacher, student, ids, shape):
    return pl.pallas_call(
        functools.partial(pack_kernel, shape),
        out_shape=(
            jax.ShapeDtypeStruct((teacher.shape[0], shape.total), BF16),
            jax.ShapeDtypeStruct((ids[0].shape[0], 8), jnp.int32),
        ),
        in_specs=[VMEM] * 5,
        out_specs=(VMEM, VMEM),
        compiler_params=pltpu.CompilerParams(vmem_limit_bytes=60 * MIB),
        name="pack_rows",
    )(teacher.T, student, *[x[None] for x in ids])


def relation_kernel(shape, rel, block, cut, base, cols, table_t, student, out):
    start = base[0] * block
    ids = cols[:, 1:2] - start
    hot = (ids == lax.broadcasted_iota(jnp.int32, (cols.shape[0], block), 1)).astype(F32).astype(BF16)
    tail = block - cut
    lanes = lax.broadcasted_iota(jnp.int32, (shape.tw, tail), 1) + cut
    rows = lax.broadcasted_iota(jnp.int32, (tail, shape.sw), 0) + cut
    table = jnp.where(lanes < rel - start, table_t[:, cut:], jnp.zeros((shape.tw, tail), BF16))
    small = jnp.where(rows < rel - start, student[cut:, :], jnp.zeros((tail, shape.sw), BF16))
    dims = (((1,), (1,)), ((), ()))
    found = lax.dot_general(hot[:, cut:], table, dims, preferred_element_type=F32)
    found_s = jnp.dot(hot[:, cut:], small, preferred_element_type=F32)
    if cut:
        found += lax.dot_general(hot[:, :cut], table_t[:, :cut], dims, preferred_element_type=F32)
        found_s += jnp.dot(hot[:, :cut], student[:cut, :], preferred_element_type=F32)
    put_row(out, found_s, found, shape)


def relation_rows(base, cols, table, student, block, shape):
    rel, tw = table.shape
    q = cols.shape[0]
    cut = max(0, rel - rel // block * block) // 128 * 128
    whole = lambda i, base: (0, 0)
    return pl.pallas_call(
        functools.partial(relation_kernel, shape, rel, block, cut),
        out_shape=jax.ShapeDtypeStruct((q, shape.total), BF16),
        grid_spec=pltpu.PrefetchScalarGridSpec(
            num_scalar_prefetch=1,
            grid=(1,),
            in_specs=[
                pl.BlockSpec((q, cols.shape[1]), whole),
                pl.BlockSpec((tw, block), lambda i, base: (0, base[0])),
                pl.BlockSpec((block, shape.sw), lambda i, base: (base[0], 0)),
            ],
            out_specs=pl.BlockSpec((q, shape.total), whole),
        ),
        compiler_params=pltpu.CompilerParams(vmem_limit_bytes=56 * MIB),
        cost_estimate=pl.CostEstimate(
            flops=2 * q * tw * block, bytes_accessed=2 * tw * block, transcendentals=0
        ),
        name="relation_rows",
    )(base, cols, table.T, student)


def joined(shards, columns):
    return jnp.concatenate([shard[:, columns] for shard in shards], axis=0)


def anchor_kernel(spots, own, bases, cols, *rest):
    count = len(spots)
    shards, accs, out = rest[:count], rest[count:-1], rest[-1]
    ids = cols[:, 0:1]
    lane = lax.broadcasted_iota(jnp.int32, (cols.shape[0], own), 1)
    group = max(1, 512 // own)
    total = None
    for first in range(0, count, group):
        last = min(count, first + group)
        hot = jnp.concatenate([(ids - bases[spots[j]] == lane).astype(F32).astype(BF16) for j in range(first, last)], axis=1)
        found = jnp.dot(hot, joined(shards[first:last], slice(None)), preferred_element_type=F32)
        total = found if total is None else total + found
    total = total.astype(BF16)
    for acc in accs:
        total = total + acc[...]
    out[...] = total


def anchor_rows(bases, spots, cols, shards, accs, shape):
    own = shards[0].shape[0]
    q, count = cols.shape[0], len(shards)
    operands = [bases, cols] + list(shards) + list(accs)
    return pl.pallas_call(
        functools.partial(anchor_kernel, spots, own),
        out_shape=jax.ShapeDtypeStruct((q, shape.total), BF16),
        in_specs=[SMEM] + [VMEM] * (len(operands) - 1),
        out_specs=VMEM,
        compiler_params=pltpu.CompilerParams(vmem_limit_bytes=2 * count * own * (shape.total + q) + 12 * MIB),
        cost_estimate=pl.CostEstimate(
            flops=2 * q * count * own * shape.total,
            bytes_accessed=2 * (count * own + 2 * q) * shape.total,
            transcendentals=0,
        ),
        name="anchor_rows",
    )(*operands)


def score_kernel(shape, own, n, chunk, anchor, other, relation, cols, *rest):
    shards, (t_out, s_out, tops, stats, q_student, q_teacher) = rest[:n], rest[n:]
    q = anchor.shape[0]
    sw, wide = shape.sw, shape.wide
    rows = 128

    def build(i, _):
        at = pl.ds(pl.multiple_of(i * rows, rows), rows)
        g = (2 * cols[at, 2:3] - 1).astype(F32)
        a = anchor[at, :].astype(F32) + other[at, :].astype(F32)
        r = relation[at, :].astype(F32)
        a_re, a_im = a[:, shape.re : shape.re + wide], a[:, shape.im : shape.im + wide]
        r_re, r_im = r[:, shape.re : shape.re + wide], r[:, shape.im : shape.im + wide]
        q_teacher[at, :wide] = (a_re * r_re - g * a_im * r_im).astype(BF16)
        q_teacher[at, wide:] = (a_im * r_re + g * a_re * r_im).astype(BF16)
        a_s, r_s = a[:, :sw], r[:, :sw]
        a_x, r_x = pltpu.roll(a_s, sw // 2, 1), pltpu.roll(r_s, sw // 2, 1)
        low = lax.broadcasted_iota(jnp.int32, (rows, sw), 1) < sw // 2
        re2, im2 = jnp.where(low, r_s, r_x), jnp.where(low, r_x, r_s)
        q_student[at, :] = (a_s * re2 + jnp.where(low, -g, g) * a_x * im2).astype(BF16)
        return 0

    lax.fori_loop(0, q // rows, build, 0)
    dims = (((1,), (1,)), ((), ()))

    def score(c, carry):
        top_t, total_t, weighted, top_s, total_s = carry
        at = slice(c * chunk, (c + 1) * chunk)
        group = shards[c * chunk // own : (c + 1) * chunk // own]
        t = lax.dot_general(joined(group, slice(sw, None)), q_teacher[...], dims, preferred_element_type=F32)
        s = lax.dot_general(joined(group, slice(0, sw)), q_student[...], dims, preferred_element_type=F32)
        new_t = jnp.maximum(top_t, jnp.max(t, axis=0, keepdims=True))
        new_s = jnp.maximum(top_s, jnp.max(s, axis=0, keepdims=True))
        scale_t, scale_s = jnp.exp(top_t - new_t), jnp.exp(top_s - new_s)
        e = jnp.exp(t - new_t)
        f = jnp.exp(s - new_s)
        t_out[at, :] = e
        s_out[at, :] = f
        tops[2 * c : 2 * c + 1, :] = new_t
        tops[2 * c + 1 : 2 * c + 2, :] = new_s
        total_t = total_t * scale_t + jnp.sum(e, axis=0, keepdims=True)
        weighted = weighted * scale_t + jnp.sum(e * (t - s), axis=0, keepdims=True)
        total_s = total_s * scale_s + jnp.sum(f, axis=0, keepdims=True)
        return new_t, total_t, weighted, new_s, total_s

    lowest = jnp.full((1, q), -jnp.inf, F32)
    nothing = jnp.zeros((1, q), F32)
    found = (lowest, nothing, nothing, lowest, nothing)
    for c in range(n * own // chunk):
        found = score(c, found)
    stats[...] = jnp.concatenate(list(found) + [nothing] * 3, axis=0)


def scores(anchor, other, relation, cols, shards, shape):
    n, own = len(shards), shards[0].shape[0]
    q = anchor.shape[0]
    slab = n * own
    chunk = 512 if slab % 512 == 0 else own
    return pl.pallas_call(
        functools.partial(score_kernel, shape, own, n, chunk),
        out_shape=(
            jax.ShapeDtypeStruct((slab, q), F32),
            jax.ShapeDtypeStruct((slab, q), F32),
            jax.ShapeDtypeStruct((2 * slab // chunk, q), F32),
            jax.ShapeDtypeStruct((8, q), F32),
            jax.ShapeDtypeStruct((q, shape.sw), BF16),
        ),
        in_specs=[VMEM] * (4 + n),
        out_specs=(VMEM,) * 5,
        scratch_shapes=[pltpu.VMEM((q, 2 * shape.wide), BF16)],
        compiler_params=pltpu.CompilerParams(vmem_limit_bytes=8 * slab * q + 2 * slab * shape.total + 10 * MIB),
        cost_estimate=pl.CostEstimate(
            flops=2 * q * slab * shape.total, bytes_accessed=2 * slab * shape.total + 8 * slab * q, transcendentals=2 * slab * q
        ),
        name="scores",
    )(anchor, other, relation, cols, *shards)


def combine(a, b):
    top_t, top_s = jnp.maximum(a[0:1], b[0:1]), jnp.maximum(a[3:4], b[3:4])
    at, bt = jnp.exp(a[0:1] - top_t), jnp.exp(b[0:1] - top_t)
    as_, bs = jnp.exp(a[3:4] - top_s), jnp.exp(b[3:4] - top_s)
    total_t = a[1:2] * at + b[1:2] * bt
    weighted = a[2:3] * at + b[2:3] * bt
    total_s = a[4:5] * as_ + b[4:5] * bs
    return top_t, total_t, weighted, top_s, total_s


def grad_kernel(n, own, chunk, sw, order, t_in, s_in, tops, mine, other, q_student, *rest):
    shards, (divergence, q_grad), outs = rest[:n], rest[n : n + 2], rest[n + 2 : -1]
    e_grad = rest[-1]
    top_t, total_t, weighted, top_s, total_s = combine(mine[...], other[...])
    divergence[...] = weighted / total_t - top_t - jnp.log(total_t) + top_s + jnp.log(total_s)
    over_t, over_s = 1.0 / total_t, 1.0 / total_s
    per = chunk // own

    def step(c, total):
        at = slice(c * chunk, (c + 1) * chunk)
        scale_t = jnp.exp(tops[2 * c : 2 * c + 1, :] - top_t) * over_t
        scale_s = jnp.exp(tops[2 * c + 1 : 2 * c + 2, :] - top_s) * over_s
        weights = (s_in[at, :] * scale_s - t_in[at, :] * scale_t).astype(BF16)
        grad = jnp.dot(weights, q_student[...], preferred_element_type=F32).astype(BF16)
        for k in range(per):
            e_grad[order[c * per + k]] = grad[k * own : (k + 1) * own, :]
        return total + lax.dot_general(
            joined(shards[c * per : (c + 1) * per], slice(0, sw)),
            weights,
            (((0,), (0,)), ((), ())),
            preferred_element_type=F32,
        )

    q = q_student.shape[0]
    total = jnp.zeros((sw, q), F32)
    for c in range(n * own // chunk):
        total = step(c, total)
    q_grad[...] = total.T
    count = n // len(outs)
    for d, out in enumerate(outs):
        out[...] = e_grad[d * count : (d + 1) * count]


def gradients(order, near, t, s, tops, mine, other, q_student, shards):
    n, own = len(shards), shards[0].shape[0]
    q, sw = q_student.shape
    slab = n * own
    shape_total = shards[0].shape[1]
    chunk = 512 if slab % 512 == 0 else own
    return pl.pallas_call(
        functools.partial(grad_kernel, n, own, chunk, sw),
        out_shape=(
            jax.ShapeDtypeStruct((1, q), F32),
            jax.ShapeDtypeStruct((q, sw), F32),
        )
        + (jax.ShapeDtypeStruct((n // near, own, sw), BF16),) * near,
        in_specs=[SMEM] + [VMEM] * (6 + n),
        out_specs=(VMEM,) * (2 + near),
        scratch_shapes=[pltpu.VMEM((n, own, sw), BF16)],
        compiler_params=pltpu.CompilerParams(vmem_limit_bytes=8 * slab * q + 2 * slab * shape_total + 10 * MIB),
        cost_estimate=pl.CostEstimate(
            flops=4 * q * slab * sw, bytes_accessed=8 * slab * q, transcendentals=2 * slab * q
        ),
        name="gradients",
    )(order, t, s, tops, mine, other, q_student, *shards)


def add_kernel(count, *refs):
    terms, outs = refs[:count], refs[count:]
    for e, out in enumerate(outs):
        total = terms[0][e].astype(F32)
        for term in terms[1:]:
            total += term[e].astype(F32)
        out[...] = total.astype(out.dtype)


def add_blocks(terms):
    far, own, sw = terms[0].shape
    return pl.pallas_call(
        functools.partial(add_kernel, len(terms)),
        out_shape=(jax.ShapeDtypeStruct((own, sw), F32),)
        + (jax.ShapeDtypeStruct((own, sw), BF16),) * (far - 1),
        in_specs=[VMEM] * len(terms),
        out_specs=(VMEM,) * far,
        compiler_params=pltpu.CompilerParams(vmem_limit_bytes=8 * MIB),
        name="add_blocks",
    )(*terms)


def reduce_blocks(blocks, beside, n):
    near, far = len(blocks), n // len(blocks)
    terms = [blocks[0]]
    for d in range(1, near):
        terms.append(lax.ppermute(blocks[d], "query", [(i, i ^ d) for i in range(n)]))
    terms[-1], beside = lax.optimization_barrier((terms[-1], beside))
    sums = add_blocks(terms)
    total = sums[0]
    for e in range(1, far):
        pairs = [(h * near + r, (h + e) % far * near + r) for h in range(far) for r in range(near)]
        total = total + lax.ppermute(sums[e], "query", pairs).astype(F32)
    return total, beside


def make(n, groups):
    place = places(n)
    steps, held = spread_steps(len(place), len(place[0]) == 2)
    table = owners(place, held, n)
    near = next(k for k in (4, 2, 1) if n % k == 0)
    me = np.arange(n)[:, None]
    position = ((table % near) ^ (me % near)) * (n // near) + (table // near - me // near) % (n // near)

    def per_device(
        anchor_ids,
        relation_ids,
        side_flags,
        teacher_entities,
        student_entities,
        teacher_relations,
        student_relations,
    ):
        own, tw = teacher_entities.shape
        shape = Shape(tw, student_entities.shape[1])
        owner, order = jnp.asarray(np.stack([table, position], axis=1))[lax.axis_index("query")]
        bases = (owner + lax.axis_index("entity") * n) * own
        packed, cols = pack(
            teacher_entities, student_entities, (anchor_ids, relation_ids, side_flags), shape
        )
        have = {(0, 0): packed}
        block = -(-teacher_relations.shape[0] // 512) * 256
        base = (lax.axis_index("entity") % 2).astype(jnp.int32)[None]
        own_key = (0, 0)
        have[own_key], base = lax.optimization_barrier((have[own_key], base))
        anchors, counted = None, 0
        kept, last = {}, {}
        for number, step in enumerate(steps):
            got = {}
            for shift, old, new in step:
                operand = have[old]
                if shift in last and last[shift] != old:
                    before = last[shift]
                    operand, kept[before] = lax.optimization_barrier((operand, have[before]))
                got[new] = move(operand, place, shift)
                last[shift] = new
            if number == 0:
                relation = relation_rows(base, cols, teacher_relations, student_relations, block, shape)
                got, relation = lax.optimization_barrier((got, relation))
                relation = relation + partner(relation, groups, 1)
            if number == len(steps) - 1:
                counted = len(have)
                names = held[:counted]
                anchors = anchor_rows(bases, range(counted), cols, [kept.get(h, have[h]) for h in names], [], shape)
            have.update(got)
        have.update(kept)
        shards = [have[h] for h in held]
        anchor = anchor_rows(bases, range(counted, n), cols, shards[counted:], [anchors], shape)
        far = 1
        while far < groups // 2:
            anchor = anchor + partner(anchor, groups, far)
            far *= 2
        other = partner(anchor, groups, far)
        expo_t, expo_s, tops, stats, q_student = scores(anchor, other, relation, cols, shards, shape)
        far = 1
        while far < groups // 2:
            found = combine(stats, partner(stats, groups, far))
            stats = jnp.concatenate(list(found) + [jnp.zeros_like(found[0])] * 3, axis=0)
            far *= 2
        divergence, q_grad, *blocks = gradients(
            order, near, expo_t, expo_s, tops, stats, partner(stats, groups, far), q_student, shards
        )
        far = 1
        while far < groups:
            q_grad = q_grad + partner(q_grad, groups, far)
            far *= 2
        entity_grad, q_grad = reduce_blocks(blocks, q_grad, n)
        return (divergence[0], entity_grad, q_grad)

    return per_device


def solution(mesh):
    in_specs = (
        P("query"),
        P("query"),
        P("query"),
        P(("entity", "query"), None),
        P(("entity", "query"), None),
        P(),
        P(),
    )
    out_specs = (P("query"), P(("entity", "query"), None), P("query", None))
    return jax.shard_map(
        make(mesh.shape["query"], mesh.shape["entity"]),
        mesh=mesh, in_specs=in_specs, out_specs=out_specs, check_vma=False,
    )
```

```python
import functools

import jax
import jax.numpy as jnp
import numpy as np
from jax import lax
from jax.experimental import pallas as pl
from jax.experimental.pallas import tpu as pltpu
from jax.sharding import PartitionSpec as P

F32 = jnp.float32
BF16 = jnp.bfloat16
VMEM = pl.BlockSpec(memory_space=pltpu.VMEM)
SMEM = pl.BlockSpec(memory_space=pltpu.SMEM)
MIB = 1 << 20


def places(n):
    sides = 2 if n % 2 == 0 else 1
    m = n // sides
    order = list(range(m))
    if m % 2 == 0:
        order = [2 * z for z in range(m // 2)] + [2 * z + 1 for z in reversed(range(m // 2))]
    return [[order[p] * sides + x for x in range(sides)] for p in range(m)]


def spread_steps(m, across):
    held = [(0, 0)]
    steps = []
    while len(held) < m * (2 if across else 1):
        taken = []
        for shift in (1, -1, 0):
            if shift == 0 and not across:
                continue
            if shift:
                found = [((k, o), (k, (o + shift) % m)) for k, o in held]
            else:
                found = [((k, o), (1 - k, o)) for k, o in held]
            names = [t[2] for t in taken]
            found = [f for f in found if f[1] not in held and f[1] not in names]
            if found:
                best = min(found, key=lambda f: (f[1][0], -min(f[1][1], m - f[1][1]), f[1][1]))
                taken.append((shift,) + best)
        held += [t[2] for t in taken]
        steps.append(taken)
    return steps, held


def move(x, place, shift):
    m = len(place)
    pairs = []
    for p in range(m):
        for side in range(len(place[0])):
            source = place[(p + shift) % m][side] if shift else place[p][1 - side]
            pairs.append((source, place[p][side]))
    return lax.ppermute(x, "query", sorted(pairs))


def owners(place, held, n):
    owner = np.zeros((n, n), np.int32)
    for p in range(len(place)):
        for side in range(len(place[0])):
            for slot, (k, o) in enumerate(held):
                owner[place[p][side], slot] = place[(p + o) % len(place)][side ^ k]
    return owner


def partner(x, size, far):
    return lax.ppermute(x, "entity", [(i, i ^ far) for i in range(size)])


class Shape:
    def __init__(self, tw, sw):
        self.tw, self.sw = tw, sw
        self.half = tw // 2
        self.wide = -(-self.half // 128) * 128
        self.re, self.im = sw, sw + self.wide
        self.total = sw + 2 * self.wide


def put_row(out, student, teacher, shape):
    out[:, : shape.sw] = student.astype(BF16)
    pad = jnp.zeros((teacher.shape[0], shape.wide - shape.half), F32)
    for start, at in ((0, shape.re), (shape.half, shape.im)):
        piece = teacher[:, start : start + shape.half]
        out[:, at : at + shape.wide] = jnp.concatenate([piece, pad], axis=1).astype(BF16)


def pack_kernel(shape, teacher_t, student, anchor_ids, relation_ids, side_flags, out, cols):
    rows = jnp.concatenate([anchor_ids[...], relation_ids[...], side_flags[...]], axis=0).astype(F32)
    rows = jnp.concatenate([rows, jnp.zeros((5, rows.shape[1]), F32)], axis=0)
    cols[...] = rows.T.astype(jnp.int32)
    put_row(out, student[...].astype(F32), teacher_t[...].astype(F32).T, shape)


def pack(teacher, student, ids, shape):
    return pl.pallas_call(
        functools.partial(pack_kernel, shape),
        out_shape=(
            jax.ShapeDtypeStruct((teacher.shape[0], shape.total), BF16),
            jax.ShapeDtypeStruct((ids[0].shape[0], 8), jnp.int32),
        ),
        in_specs=[VMEM] * 5,
        out_specs=(VMEM, VMEM),
        compiler_params=pltpu.CompilerParams(vmem_limit_bytes=60 * MIB),
        name="pack_rows",
    )(teacher.T, student, *[x[None] for x in ids])


def relation_kernel(shape, rel, block, cut, base, cols, table_t, student, out):
    start = base[0] * block
    ids = cols[:, 1:2] - start
    hot = (ids == lax.broadcasted_iota(jnp.int32, (cols.shape[0], block), 1)).astype(F32).astype(BF16)
    tail = block - cut
    lanes = lax.broadcasted_iota(jnp.int32, (shape.tw, tail), 1) + cut
    rows = lax.broadcasted_iota(jnp.int32, (tail, shape.sw), 0) + cut
    table = jnp.where(lanes < rel - start, table_t[:, cut:], jnp.zeros((shape.tw, tail), BF16))
    small = jnp.where(rows < rel - start, student[cut:, :], jnp.zeros((tail, shape.sw), BF16))
    dims = (((1,), (1,)), ((), ()))
    found = lax.dot_general(hot[:, cut:], table, dims, preferred_element_type=F32)
    found_s = jnp.dot(hot[:, cut:], small, preferred_element_type=F32)
    if cut:
        found += lax.dot_general(hot[:, :cut], table_t[:, :cut], dims, preferred_element_type=F32)
        found_s += jnp.dot(hot[:, :cut], student[:cut, :], preferred_element_type=F32)
    put_row(out, found_s, found, shape)


def relation_rows(base, cols, table, student, block, shape):
    rel, tw = table.shape
    q = cols.shape[0]
    cut = max(0, rel - rel // block * block) // 128 * 128
    whole = lambda i, base: (0, 0)
    return pl.pallas_call(
        functools.partial(relation_kernel, shape, rel, block, cut),
        out_shape=jax.ShapeDtypeStruct((q, shape.total), BF16),
        grid_spec=pltpu.PrefetchScalarGridSpec(
            num_scalar_prefetch=1,
            grid=(1,),
            in_specs=[
                pl.BlockSpec((q, cols.shape[1]), whole),
                pl.BlockSpec((tw, block), lambda i, base: (0, base[0])),
                pl.BlockSpec((block, shape.sw), lambda i, base: (base[0], 0)),
            ],
            out_specs=pl.BlockSpec((q, shape.total), whole),
        ),
        compiler_params=pltpu.CompilerParams(vmem_limit_bytes=56 * MIB),
        cost_estimate=pl.CostEstimate(
            flops=2 * q * tw * block, bytes_accessed=2 * tw * block, transcendentals=0
        ),
        name="relation_rows",
    )(base, cols, table.T, student)


def joined(shards, columns):
    return jnp.concatenate([shard[:, columns] for shard in shards], axis=0)


def anchor_kernel(spots, own, bases, cols, *rest):
    count = len(spots)
    shards, accs, out = rest[:count], rest[count:-1], rest[-1]
    ids = cols[:, 0:1]
    lane = lax.broadcasted_iota(jnp.int32, (cols.shape[0], own), 1)
    group = max(1, 512 // own)
    total = None
    for first in range(0, count, group):
        last = min(count, first + group)
        hot = jnp.concatenate([(ids - bases[spots[j]] == lane).astype(F32).astype(BF16) for j in range(first, last)], axis=1)
        found = jnp.dot(hot, joined(shards[first:last], slice(None)), preferred_element_type=F32)
        total = found if total is None else total + found
    total = total.astype(BF16)
    for acc in accs:
        total = total + acc[...]
    out[...] = total


def anchor_rows(bases, spots, cols, shards, accs, shape):
    own = shards[0].shape[0]
    q, count = cols.shape[0], len(shards)
    operands = [bases, cols] + list(shards) + list(accs)
    return pl.pallas_call(
        functools.partial(anchor_kernel, spots, own),
        out_shape=jax.ShapeDtypeStruct((q, shape.total), BF16),
        in_specs=[SMEM] + [VMEM] * (len(operands) - 1),
        out_specs=VMEM,
        compiler_params=pltpu.CompilerParams(vmem_limit_bytes=2 * count * own * (shape.total + q) + 12 * MIB),
        cost_estimate=pl.CostEstimate(
            flops=2 * q * count * own * shape.total,
            bytes_accessed=2 * (count * own + 2 * q) * shape.total,
            transcendentals=0,
        ),
        name="anchor_rows",
    )(*operands)


def score_kernel(shape, own, n, chunk, anchor, other, relation, cols, *rest):
    shards, (t_out, s_out, stats, q_student, q_teacher) = rest[:n], rest[n:]
    q = anchor.shape[0]
    sw, wide = shape.sw, shape.wide
    rows = 128

    def build(i, _):
        at = pl.ds(pl.multiple_of(i * rows, rows), rows)
        g = (2 * cols[at, 2:3] - 1).astype(F32)
        a = anchor[at, :].astype(F32) + other[at, :].astype(F32)
        r = relation[at, :].astype(F32)
        a_re, a_im = a[:, shape.re : shape.re + wide], a[:, shape.im : shape.im + wide]
        r_re, r_im = r[:, shape.re : shape.re + wide], r[:, shape.im : shape.im + wide]
        q_teacher[at, :wide] = (a_re * r_re - g * a_im * r_im).astype(BF16)
        q_teacher[at, wide:] = (a_im * r_re + g * a_re * r_im).astype(BF16)
        a_s, r_s = a[:, :sw], r[:, :sw]
        a_x, r_x = pltpu.roll(a_s, sw // 2, 1), pltpu.roll(r_s, sw // 2, 1)
        low = lax.broadcasted_iota(jnp.int32, (rows, sw), 1) < sw // 2
        re2, im2 = jnp.where(low, r_s, r_x), jnp.where(low, r_x, r_s)
        q_student[at, :] = (a_s * re2 + jnp.where(low, -g, g) * a_x * im2).astype(BF16)
        return 0

    lax.fori_loop(0, q // rows, build, 0)
    dims = (((1,), (1,)), ((), ()))

    def products(c):
        group = shards[c * chunk // own : (c + 1) * chunk // own]
        t = lax.dot_general(joined(group, slice(sw, None)), q_teacher[...], dims, preferred_element_type=F32)
        s = lax.dot_general(joined(group, slice(0, sw)), q_student[...], dims, preferred_element_type=F32)
        return t, s

    def score(c, t, s, carry):
        top_t, total_t, weighted, top_s, total_s = carry
        t_out[c * chunk : (c + 1) * chunk, :] = t
        s_out[c * chunk : (c + 1) * chunk, :] = s
        new_t = jnp.maximum(top_t, jnp.max(t, axis=0, keepdims=True))
        new_s = jnp.maximum(top_s, jnp.max(s, axis=0, keepdims=True))
        scale_t, scale_s = jnp.exp(top_t - new_t), jnp.exp(top_s - new_s)
        e = jnp.exp(t - new_t)
        total_t = total_t * scale_t + jnp.sum(e, axis=0, keepdims=True)
        weighted = weighted * scale_t + jnp.sum(e * (t - s), axis=0, keepdims=True)
        total_s = total_s * scale_s + jnp.sum(jnp.exp(s - new_s), axis=0, keepdims=True)
        return new_t, total_t, weighted, new_s, total_s

    lowest = jnp.full((1, q), -jnp.inf, F32)
    nothing = jnp.zeros((1, q), F32)
    found = (lowest, nothing, nothing, lowest, nothing)
    count = n * own // chunk
    t, s = products(0)
    for c in range(count):
        later = products(c + 1) if c + 1 < count else None
        found = score(c, t, s, found)
        t, s = later or (None, None)
    stats[...] = jnp.concatenate(list(found) + [nothing] * 3, axis=0)


def scores(anchor, other, relation, cols, shards, shape):
    n, own = len(shards), shards[0].shape[0]
    q = anchor.shape[0]
    slab = n * own
    chunk = 512 if slab % 512 == 0 else own
    return pl.pallas_call(
        functools.partial(score_kernel, shape, own, n, chunk),
        out_shape=(
            jax.ShapeDtypeStruct((slab, q), F32),
            jax.ShapeDtypeStruct((slab, q), F32),
            jax.ShapeDtypeStruct((8, q), F32),
            jax.ShapeDtypeStruct((q, shape.sw), BF16),
        ),
        in_specs=[VMEM] * (4 + n),
        out_specs=(VMEM,) * 4,
        scratch_shapes=[pltpu.VMEM((q, 2 * shape.wide), BF16)],
        compiler_params=pltpu.CompilerParams(vmem_limit_bytes=8 * slab * q + 2 * slab * shape.total + 10 * MIB),
        cost_estimate=pl.CostEstimate(
            flops=2 * q * slab * shape.total, bytes_accessed=2 * slab * shape.total + 8 * slab * q, transcendentals=2 * slab * q
        ),
        name="scores",
    )(anchor, other, relation, cols, *shards)


def combine(a, b):
    top_t, top_s = jnp.maximum(a[0:1], b[0:1]), jnp.maximum(a[3:4], b[3:4])
    at, bt = jnp.exp(a[0:1] - top_t), jnp.exp(b[0:1] - top_t)
    as_, bs = jnp.exp(a[3:4] - top_s), jnp.exp(b[3:4] - top_s)
    total_t = a[1:2] * at + b[1:2] * bt
    weighted = a[2:3] * at + b[2:3] * bt
    total_s = a[4:5] * as_ + b[4:5] * bs
    return top_t, total_t, weighted, top_s, total_s


def grad_kernel(n, own, chunk, sw, order, t_in, s_in, mine, other, q_student, *rest):
    shards, (divergence, q_grad), outs = rest[:n], rest[n : n + 2], rest[n + 2 : -1]
    e_grad = rest[-1]
    top_t, total_t, weighted, top_s, total_s = combine(mine[...], other[...])
    divergence[...] = weighted / total_t - top_t - jnp.log(total_t) + top_s + jnp.log(total_s)
    over_t, over_s = 1.0 / total_t, 1.0 / total_s
    per = chunk // own

    def weigh(c):
        at = slice(c * chunk, (c + 1) * chunk)
        prob_t = jnp.exp(t_in[at, :] - top_t) * over_t
        prob_s = jnp.exp(s_in[at, :] - top_s) * over_s
        return (prob_s - prob_t).astype(BF16)

    def step(c, weights, total):
        grad = jnp.dot(weights, q_student[...], preferred_element_type=F32).astype(BF16)
        for k in range(per):
            e_grad[order[c * per + k]] = grad[k * own : (k + 1) * own, :]
        return total + lax.dot_general(
            joined(shards[c * per : (c + 1) * per], slice(0, sw)),
            weights,
            (((0,), (0,)), ((), ())),
            preferred_element_type=F32,
        )

    q = q_student.shape[0]
    total = jnp.zeros((sw, q), F32)
    count = n * own // chunk
    weights = weigh(0)
    for c in range(count):
        later = weigh(c + 1) if c + 1 < count else None
        total = step(c, weights, total)
        weights = later
    q_grad[...] = total.T
    far = n // len(outs)
    for d, out in enumerate(outs):
        out[...] = e_grad[d * far : (d + 1) * far]


def gradients(order, near, t, s, mine, other, q_student, shards):
    n, own = len(shards), shards[0].shape[0]
    q, sw = q_student.shape
    slab = n * own
    shape_total = shards[0].shape[1]
    chunk = 512 if slab % 512 == 0 else own
    return pl.pallas_call(
        functools.partial(grad_kernel, n, own, chunk, sw),
        out_shape=(
            jax.ShapeDtypeStruct((1, q), F32),
            jax.ShapeDtypeStruct((q, sw), F32),
        )
        + (jax.ShapeDtypeStruct((n // near, own, sw), BF16),) * near,
        in_specs=[SMEM] + [VMEM] * (5 + n),
        out_specs=(VMEM,) * (2 + near),
        scratch_shapes=[pltpu.VMEM((n, own, sw), BF16)],
        compiler_params=pltpu.CompilerParams(vmem_limit_bytes=8 * slab * q + 2 * slab * shape_total + 10 * MIB),
        cost_estimate=pl.CostEstimate(
            flops=4 * q * slab * sw, bytes_accessed=8 * slab * q, transcendentals=2 * slab * q
        ),
        name="gradients",
    )(order, t, s, mine, other, q_student, *shards)


def add_kernel(count, *refs):
    terms, outs = refs[:count], refs[count:]
    for e, out in enumerate(outs):
        total = terms[0][e].astype(F32)
        for term in terms[1:]:
            total += term[e].astype(F32)
        out[...] = total.astype(out.dtype)


def add_blocks(terms):
    far, own, sw = terms[0].shape
    return pl.pallas_call(
        functools.partial(add_kernel, len(terms)),
        out_shape=(jax.ShapeDtypeStruct((own, sw), F32),)
        + (jax.ShapeDtypeStruct((own, sw), BF16),) * (far - 1),
        in_specs=[VMEM] * len(terms),
        out_specs=(VMEM,) * far,
        compiler_params=pltpu.CompilerParams(vmem_limit_bytes=8 * MIB),
        name="add_blocks",
    )(*terms)


def reduce_blocks(blocks, beside, n):
    near, far = len(blocks), n // len(blocks)
    terms = [blocks[0]]
    for d in range(1, near):
        terms.append(lax.ppermute(blocks[d], "query", [(i, i ^ d) for i in range(n)]))
    terms[-1], beside = lax.optimization_barrier((terms[-1], beside))
    sums = add_blocks(terms)
    total = sums[0]
    for e in range(1, far):
        pairs = [(h * near + r, (h + e) % far * near + r) for h in range(far) for r in range(near)]
        total = total + lax.ppermute(sums[e], "query", pairs).astype(F32)
    return total, beside


def make(n, groups):
    place = places(n)
    steps, held = spread_steps(len(place), len(place[0]) == 2)
    table = owners(place, held, n)
    near = next(k for k in (4, 2, 1) if n % k == 0)
    me = np.arange(n)[:, None]
    position = ((table % near) ^ (me % near)) * (n // near) + (table // near - me // near) % (n // near)

    def per_device(
        anchor_ids,
        relation_ids,
        side_flags,
        teacher_entities,
        student_entities,
        teacher_relations,
        student_relations,
    ):
        own, tw = teacher_entities.shape
        shape = Shape(tw, student_entities.shape[1])
        owner, order = jnp.asarray(np.stack([table, position], axis=1))[lax.axis_index("query")]
        bases = (owner + lax.axis_index("entity") * n) * own
        packed, cols = pack(
            teacher_entities, student_entities, (anchor_ids, relation_ids, side_flags), shape
        )
        have = {(0, 0): packed}
        block = -(-teacher_relations.shape[0] // 512) * 256
        base = (lax.axis_index("entity") % 2).astype(jnp.int32)[None]
        own_key = (0, 0)
        have[own_key], base = lax.optimization_barrier((have[own_key], base))
        anchors, counted = None, 0
        kept, last = {}, {}
        for number, step in enumerate(steps):
            got = {}
            for shift, old, new in step:
                operand = have[old]
                if shift in last and last[shift] != old:
                    before = last[shift]
                    operand, kept[before] = lax.optimization_barrier((operand, have[before]))
                got[new] = move(operand, place, shift)
                last[shift] = new
            if number == 0:
                relation = relation_rows(base, cols, teacher_relations, student_relations, block, shape)
                got, relation = lax.optimization_barrier((got, relation))
                relation = relation + partner(relation, groups, 1)
            if number == len(steps) - 1:
                counted = len(have)
                names = held[:counted]
                anchors = anchor_rows(bases, range(counted), cols, [kept.get(h, have[h]) for h in names], [], shape)
            have.update(got)
        have.update(kept)
        shards = [have[h] for h in held]
        anchor = anchor_rows(bases, range(counted, n), cols, shards[counted:], [anchors], shape)
        far = 1
        while far < groups // 2:
            anchor = anchor + partner(anchor, groups, far)
            far *= 2
        other = partner(anchor, groups, far)
        t, s, stats, q_student = scores(anchor, other, relation, cols, shards, shape)
        far = 1
        while far < groups // 2:
            found = combine(stats, partner(stats, groups, far))
            stats = jnp.concatenate(list(found) + [jnp.zeros_like(found[0])] * 3, axis=0)
            far *= 2
        divergence, q_grad, *blocks = gradients(
            order, near, t, s, stats, partner(stats, groups, far), q_student, shards
        )
        far = 1
        while far < groups:
            q_grad = q_grad + partner(q_grad, groups, far)
            far *= 2
        entity_grad, q_grad = reduce_blocks(blocks, q_grad, n)
        return (divergence[0], entity_grad, q_grad)

    return per_device


def solution(mesh):
    in_specs = (
        P("query"),
        P("query"),
        P("query"),
        P(("entity", "query"), None),
        P(("entity", "query"), None),
        P(),
        P(),
    )
    out_specs = (P("query"), P(("entity", "query"), None), P("query", None))
    return jax.shard_map(
        make(mesh.shape["query"], mesh.shape["entity"]),
        mesh=mesh, in_specs=in_specs, out_specs=out_specs, check_vma=False,
    )
```

```python
import functools

import jax
import jax.numpy as jnp
import numpy as np
from jax import lax
from jax.experimental import pallas as pl
from jax.experimental.pallas import tpu as pltpu
from jax.sharding import PartitionSpec as P

F32 = jnp.float32
BF16 = jnp.bfloat16
VMEM = pl.BlockSpec(memory_space=pltpu.VMEM)
SMEM = pl.BlockSpec(memory_space=pltpu.SMEM)
MIB = 1 << 20


def places(n):
    sides = 2 if n % 2 == 0 else 1
    m = n // sides
    order = list(range(m))
    if m % 2 == 0:
        order = [2 * z for z in range(m // 2)] + [2 * z + 1 for z in reversed(range(m // 2))]
    return [[order[p] * sides + x for x in range(sides)] for p in range(m)]


def spread_steps(m, across):
    held = [(0, 0)]
    steps = []
    while len(held) < m * (2 if across else 1):
        taken = []
        for shift in (1, -1, 0):
            if shift == 0 and not across:
                continue
            if shift:
                found = [((k, o), (k, (o + shift) % m)) for k, o in held]
            else:
                found = [((k, o), (1 - k, o)) for k, o in held]
            names = [t[2] for t in taken]
            found = [f for f in found if f[1] not in held and f[1] not in names]
            if found:
                best = min(found, key=lambda f: (f[1][0], -min(f[1][1], m - f[1][1]), f[1][1]))
                taken.append((shift,) + best)
        held += [t[2] for t in taken]
        steps.append(taken)
    return steps, held


def move(x, place, shift):
    m = len(place)
    pairs = []
    for p in range(m):
        for side in range(len(place[0])):
            source = place[(p + shift) % m][side] if shift else place[p][1 - side]
            pairs.append((source, place[p][side]))
    return lax.ppermute(x, "query", sorted(pairs))


def owners(place, held, n):
    owner = np.zeros((n, n), np.int32)
    for p in range(len(place)):
        for side in range(len(place[0])):
            for slot, (k, o) in enumerate(held):
                owner[place[p][side], slot] = place[(p + o) % len(place)][side ^ k]
    return owner


def partner(x, size, far):
    return lax.ppermute(x, "entity", [(i, i ^ far) for i in range(size)])


class Shape:
    def __init__(self, tw, sw):
        self.tw, self.sw = tw, sw
        self.half = tw // 2
        self.wide = -(-self.half // 128) * 128
        self.re, self.im = sw, sw + self.wide
        self.total = sw + 2 * self.wide


def put_row(out, student, teacher, shape):
    out[:, : shape.sw] = student.astype(BF16)
    pad = jnp.zeros((teacher.shape[0], shape.wide - shape.half), F32)
    for start, at in ((0, shape.re), (shape.half, shape.im)):
        piece = teacher[:, start : start + shape.half]
        out[:, at : at + shape.wide] = jnp.concatenate([piece, pad], axis=1).astype(BF16)


def pack_kernel(shape, teacher_t, student, anchor_ids, relation_ids, side_flags, out, cols):
    rows = jnp.concatenate([anchor_ids[...], relation_ids[...], side_flags[...]], axis=0).astype(F32)
    rows = jnp.concatenate([rows, jnp.zeros((5, rows.shape[1]), F32)], axis=0)
    cols[...] = rows.T.astype(jnp.int32)
    put_row(out, student[...].astype(F32), teacher_t[...].astype(F32).T, shape)


def pack(teacher, student, ids, shape):
    return pl.pallas_call(
        functools.partial(pack_kernel, shape),
        out_shape=(
            jax.ShapeDtypeStruct((teacher.shape[0], shape.total), BF16),
            jax.ShapeDtypeStruct((ids[0].shape[0], 8), jnp.int32),
        ),
        in_specs=[VMEM] * 5,
        out_specs=(VMEM, VMEM),
        compiler_params=pltpu.CompilerParams(vmem_limit_bytes=60 * MIB),
        name="pack_rows",
    )(teacher.T, student, *[x[None] for x in ids])


def relation_kernel(shape, rel, block, cut, base, cols, table_t, student, out):
    start = base[0] * block
    ids = cols[:, 1:2] - start
    hot = (ids == lax.broadcasted_iota(jnp.int32, (cols.shape[0], block), 1)).astype(F32).astype(BF16)
    tail = block - cut
    lanes = lax.broadcasted_iota(jnp.int32, (shape.tw, tail), 1) + cut
    rows = lax.broadcasted_iota(jnp.int32, (tail, shape.sw), 0) + cut
    table = jnp.where(lanes < rel - start, table_t[:, cut:], jnp.zeros((shape.tw, tail), BF16))
    small = jnp.where(rows < rel - start, student[cut:, :], jnp.zeros((tail, shape.sw), BF16))
    dims = (((1,), (1,)), ((), ()))
    found = lax.dot_general(hot[:, cut:], table, dims, preferred_element_type=F32)
    found_s = jnp.dot(hot[:, cut:], small, preferred_element_type=F32)
    if cut:
        found += lax.dot_general(hot[:, :cut], table_t[:, :cut], dims, preferred_element_type=F32)
        found_s += jnp.dot(hot[:, :cut], student[:cut, :], preferred_element_type=F32)
    put_row(out, found_s, found, shape)


def relation_rows(base, cols, table, student, block, shape):
    rel, tw = table.shape
    q = cols.shape[0]
    cut = max(0, rel - rel // block * block) // 128 * 128
    whole = lambda i, base: (0, 0)
    return pl.pallas_call(
        functools.partial(relation_kernel, shape, rel, block, cut),
        out_shape=jax.ShapeDtypeStruct((q, shape.total), BF16),
        grid_spec=pltpu.PrefetchScalarGridSpec(
            num_scalar_prefetch=1,
            grid=(1,),
            in_specs=[
                pl.BlockSpec((q, cols.shape[1]), whole),
                pl.BlockSpec((tw, block), lambda i, base: (0, base[0])),
                pl.BlockSpec((block, shape.sw), lambda i, base: (base[0], 0)),
            ],
            out_specs=pl.BlockSpec((q, shape.total), whole),
        ),
        compiler_params=pltpu.CompilerParams(vmem_limit_bytes=56 * MIB),
        cost_estimate=pl.CostEstimate(
            flops=2 * q * tw * block, bytes_accessed=2 * tw * block, transcendentals=0
        ),
        name="relation_rows",
    )(base, cols, table.T, student)


def joined(shards, columns):
    return jnp.concatenate([shard[:, columns] for shard in shards], axis=0)


def anchor_kernel(spots, own, bases, cols, *rest):
    count = len(spots)
    shards, accs, out = rest[:count], rest[count:-1], rest[-1]
    ids = cols[:, 0:1]
    lane = lax.broadcasted_iota(jnp.int32, (cols.shape[0], own), 1)
    group = max(1, 512 // own)
    total = None
    for first in range(0, count, group):
        last = min(count, first + group)
        hot = jnp.concatenate([(ids - bases[spots[j]] == lane).astype(F32).astype(BF16) for j in range(first, last)], axis=1)
        found = jnp.dot(hot, joined(shards[first:last], slice(None)), preferred_element_type=F32)
        total = found if total is None else total + found
    total = total.astype(BF16)
    for acc in accs:
        total = total + acc[...]
    out[...] = total


def anchor_rows(bases, spots, cols, shards, accs, shape):
    own = shards[0].shape[0]
    q, count = cols.shape[0], len(shards)
    operands = [bases, cols] + list(shards) + list(accs)
    return pl.pallas_call(
        functools.partial(anchor_kernel, spots, own),
        out_shape=jax.ShapeDtypeStruct((q, shape.total), BF16),
        in_specs=[SMEM] + [VMEM] * (len(operands) - 1),
        out_specs=VMEM,
        compiler_params=pltpu.CompilerParams(vmem_limit_bytes=2 * count * own * (shape.total + q) + 12 * MIB),
        cost_estimate=pl.CostEstimate(
            flops=2 * q * count * own * shape.total,
            bytes_accessed=2 * (count * own + 2 * q) * shape.total,
            transcendentals=0,
        ),
        name="anchor_rows",
    )(*operands)


def score_kernel(shape, own, n, chunk, anchor, other, relation, cols, *rest):
    shards, (t_out, s_out, stats, q_student, q_teacher) = rest[:n], rest[n:]
    q = anchor.shape[0]
    sw, wide = shape.sw, shape.wide
    rows = 128

    def build(i, _):
        at = pl.ds(pl.multiple_of(i * rows, rows), rows)
        g = (2 * cols[at, 2:3] - 1).astype(F32)
        a = anchor[at, :].astype(F32) + other[at, :].astype(F32)
        r = relation[at, :].astype(F32)
        a_re, a_im = a[:, shape.re : shape.re + wide], a[:, shape.im : shape.im + wide]
        r_re, r_im = r[:, shape.re : shape.re + wide], r[:, shape.im : shape.im + wide]
        q_teacher[at, :wide] = (a_re * r_re - g * a_im * r_im).astype(BF16)
        q_teacher[at, wide:] = (a_im * r_re + g * a_re * r_im).astype(BF16)
        a_s, r_s = a[:, :sw], r[:, :sw]
        a_x, r_x = pltpu.roll(a_s, sw // 2, 1), pltpu.roll(r_s, sw // 2, 1)
        low = lax.broadcasted_iota(jnp.int32, (rows, sw), 1) < sw // 2
        re2, im2 = jnp.where(low, r_s, r_x), jnp.where(low, r_x, r_s)
        q_student[at, :] = (a_s * re2 + jnp.where(low, -g, g) * a_x * im2).astype(BF16)
        return 0

    lax.fori_loop(0, q // rows, build, 0)
    dims = (((1,), (1,)), ((), ()))

    def score(c, carry):
        top_t, total_t, weighted, top_s, total_s = carry
        at = slice(c * chunk, (c + 1) * chunk)
        group = shards[c * chunk // own : (c + 1) * chunk // own]
        t = lax.dot_general(joined(group, slice(sw, None)), q_teacher[...], dims, preferred_element_type=F32)
        s = lax.dot_general(joined(group, slice(0, sw)), q_student[...], dims, preferred_element_type=F32)
        t_out[at, :] = t
        s_out[at, :] = s
        new_t = jnp.maximum(top_t, jnp.max(t, axis=0, keepdims=True))
        new_s = jnp.maximum(top_s, jnp.max(s, axis=0, keepdims=True))
        scale_t, scale_s = jnp.exp(top_t - new_t), jnp.exp(top_s - new_s)
        e = jnp.exp(t - new_t)
        total_t = total_t * scale_t + jnp.sum(e, axis=0, keepdims=True)
        weighted = weighted * scale_t + jnp.sum(e * (t - s), axis=0, keepdims=True)
        total_s = total_s * scale_s + jnp.sum(jnp.exp(s - new_s), axis=0, keepdims=True)
        return new_t, total_t, weighted, new_s, total_s

    lowest = jnp.full((1, q), -jnp.inf, F32)
    nothing = jnp.zeros((1, q), F32)
    found = (lowest, nothing, nothing, lowest, nothing)
    for c in range(n * own // chunk):
        found = score(c, found)
    stats[...] = jnp.concatenate(list(found) + [nothing] * 3, axis=0)


def scores(anchor, other, relation, cols, shards, shape):
    n, own = len(shards), shards[0].shape[0]
    q = anchor.shape[0]
    slab = n * own
    chunk = 512 if slab % 512 == 0 else own
    return pl.pallas_call(
        functools.partial(score_kernel, shape, own, n, chunk),
        out_shape=(
            jax.ShapeDtypeStruct((slab, q), F32),
            jax.ShapeDtypeStruct((slab, q), F32),
            jax.ShapeDtypeStruct((8, q), F32),
            jax.ShapeDtypeStruct((q, shape.sw), BF16),
        ),
        in_specs=[VMEM] * (4 + n),
        out_specs=(VMEM,) * 4,
        scratch_shapes=[pltpu.VMEM((q, 2 * shape.wide), BF16)],
        compiler_params=pltpu.CompilerParams(vmem_limit_bytes=8 * slab * q + 2 * slab * shape.total + 10 * MIB),
        cost_estimate=pl.CostEstimate(
            flops=2 * q * slab * shape.total, bytes_accessed=2 * slab * shape.total + 8 * slab * q, transcendentals=2 * slab * q
        ),
        name="scores",
    )(anchor, other, relation, cols, *shards)


def combine(a, b):
    top_t, top_s = jnp.maximum(a[0:1], b[0:1]), jnp.maximum(a[3:4], b[3:4])
    at, bt = jnp.exp(a[0:1] - top_t), jnp.exp(b[0:1] - top_t)
    as_, bs = jnp.exp(a[3:4] - top_s), jnp.exp(b[3:4] - top_s)
    total_t = a[1:2] * at + b[1:2] * bt
    weighted = a[2:3] * at + b[2:3] * bt
    total_s = a[4:5] * as_ + b[4:5] * bs
    return top_t, total_t, weighted, top_s, total_s


def grad_kernel(n, own, chunk, sw, order, t_in, s_in, mine, other, q_student, *rest):
    shards, (divergence, q_grad), outs = rest[:n], rest[n : n + 2], rest[n + 2 : -1]
    e_grad = rest[-1]
    top_t, total_t, weighted, top_s, total_s = combine(mine[...], other[...])
    divergence[...] = weighted / total_t - top_t - jnp.log(total_t) + top_s + jnp.log(total_s)
    over_t, over_s = 1.0 / total_t, 1.0 / total_s
    per = chunk // own

    def step(c, total):
        at = slice(c * chunk, (c + 1) * chunk)
        prob_t = jnp.exp(t_in[at, :] - top_t) * over_t
        prob_s = jnp.exp(s_in[at, :] - top_s) * over_s
        weights = (prob_s - prob_t).astype(BF16)
        grad = jnp.dot(weights, q_student[...], preferred_element_type=F32).astype(BF16)
        for k in range(per):
            e_grad[order[c * per + k]] = grad[k * own : (k + 1) * own, :]
        return total + lax.dot_general(
            joined(shards[c * per : (c + 1) * per], slice(0, sw)),
            weights,
            (((0,), (0,)), ((), ())),
            preferred_element_type=F32,
        )

    q = q_student.shape[0]
    total = jnp.zeros((sw, q), F32)
    for c in range(n * own // chunk):
        total = step(c, total)
    q_grad[...] = total.T
    far = n // len(outs)
    for d, out in enumerate(outs):
        out[...] = e_grad[d * far : (d + 1) * far]


def gradients(order, near, t, s, mine, other, q_student, shards):
    n, own = len(shards), shards[0].shape[0]
    q, sw = q_student.shape
    slab = n * own
    shape_total = shards[0].shape[1]
    chunk = 512 if slab % 512 == 0 else own
    return pl.pallas_call(
        functools.partial(grad_kernel, n, own, chunk, sw),
        out_shape=(
            jax.ShapeDtypeStruct((1, q), F32),
            jax.ShapeDtypeStruct((q, sw), F32),
        )
        + (jax.ShapeDtypeStruct((n // near, own, sw), BF16),) * near,
        in_specs=[SMEM] + [VMEM] * (5 + n),
        out_specs=(VMEM,) * (2 + near),
        scratch_shapes=[pltpu.VMEM((n, own, sw), BF16)],
        compiler_params=pltpu.CompilerParams(vmem_limit_bytes=8 * slab * q + 2 * slab * shape_total + 10 * MIB),
        cost_estimate=pl.CostEstimate(
            flops=4 * q * slab * sw, bytes_accessed=8 * slab * q, transcendentals=2 * slab * q
        ),
        name="gradients",
    )(order, t, s, mine, other, q_student, *shards)


def fold_kernel(count, *refs):
    terms, outs = refs[:count], refs[count:]
    for i in range(terms[0].shape[0]):
        total = terms[0][i].astype(F32)
        for term in terms[1:]:
            total += term[i].astype(F32)
        out = outs[i % len(outs)]
        if len(outs) == 1:
            out[...] = total
        else:
            out[i // 2] = total.astype(out.dtype)


def fold(terms):
    count, own, sw = terms[0].shape
    if count == 1:
        out_shape = (jax.ShapeDtypeStruct((own, sw), F32),)
    else:
        out_shape = tuple(jax.ShapeDtypeStruct((count // 2, own, sw), dtype) for dtype in (F32, BF16))
    return pl.pallas_call(
        functools.partial(fold_kernel, len(terms)),
        out_shape=out_shape,
        in_specs=[VMEM] * len(terms),
        out_specs=(VMEM,) * len(out_shape),
        compiler_params=pltpu.CompilerParams(vmem_limit_bytes=8 * MIB),
        name="fold_blocks",
    )(*terms)


def reduce_blocks(blocks, beside, n):
    near = len(blocks)
    terms = [blocks[0]]
    for d in range(1, near):
        terms.append(lax.ppermute(blocks[d], "query", [(i, i ^ d) for i in range(n)]))
    terms[-1], beside = lax.optimization_barrier((terms[-1], beside))
    found = fold(terms)
    away = near
    while len(found) == 2:
        keep, send = found
        found = fold([keep, lax.ppermute(send, "query", [(i, i ^ away) for i in range(n)])])
        away *= 2
    return found[0], beside


def make(n, groups):
    place = places(n)
    steps, held = spread_steps(len(place), len(place[0]) == 2)
    table = owners(place, held, n)
    assert n & (n - 1) == 0
    near = min(4, n)
    me = np.arange(n)[:, None]
    position = ((table % near) ^ (me % near)) * (n // near) + (table // near ^ me // near)

    def per_device(
        anchor_ids,
        relation_ids,
        side_flags,
        teacher_entities,
        student_entities,
        teacher_relations,
        student_relations,
    ):
        own, tw = teacher_entities.shape
        shape = Shape(tw, student_entities.shape[1])
        owner, order = jnp.asarray(np.stack([table, position], axis=1))[lax.axis_index("query")]
        bases = (owner + lax.axis_index("entity") * n) * own
        packed, cols = pack(
            teacher_entities, student_entities, (anchor_ids, relation_ids, side_flags), shape
        )
        have = {(0, 0): packed}
        block = -(-teacher_relations.shape[0] // 512) * 256
        base = (lax.axis_index("entity") % 2).astype(jnp.int32)[None]
        own_key = (0, 0)
        have[own_key], base = lax.optimization_barrier((have[own_key], base))
        anchors, counted = None, 0
        kept, last = {}, {}
        for number, step in enumerate(steps):
            got = {}
            for shift, old, new in step:
                operand = have[old]
                if shift in last and last[shift] != old:
                    before = last[shift]
                    operand, kept[before] = lax.optimization_barrier((operand, have[before]))
                got[new] = move(operand, place, shift)
                last[shift] = new
            if number == 0:
                relation = relation_rows(base, cols, teacher_relations, student_relations, block, shape)
                got, relation = lax.optimization_barrier((got, relation))
                relation = relation + partner(relation, groups, 1)
            if number == len(steps) - 1:
                counted = len(have)
                names = held[:counted]
                anchors = anchor_rows(bases, range(counted), cols, [kept.get(h, have[h]) for h in names], [], shape)
            have.update(got)
        have.update(kept)
        shards = [have[h] for h in held]
        anchor = anchor_rows(bases, range(counted, n), cols, shards[counted:], [anchors], shape)
        far = 1
        while far < groups // 2:
            anchor = anchor + partner(anchor, groups, far)
            far *= 2
        other = partner(anchor, groups, far)
        t, s, stats, q_student = scores(anchor, other, relation, cols, shards, shape)
        far = 1
        while far < groups // 2:
            found = combine(stats, partner(stats, groups, far))
            stats = jnp.concatenate(list(found) + [jnp.zeros_like(found[0])] * 3, axis=0)
            far *= 2
        divergence, q_grad, *blocks = gradients(
            order, near, t, s, stats, partner(stats, groups, far), q_student, shards
        )
        far = 1
        while far < groups:
            q_grad = q_grad + partner(q_grad, groups, far)
            far *= 2
        entity_grad, q_grad = reduce_blocks(blocks, q_grad, n)
        return (divergence[0], entity_grad, q_grad)

    return per_device


def solution(mesh):
    in_specs = (
        P("query"),
        P("query"),
        P("query"),
        P(("entity", "query"), None),
        P(("entity", "query"), None),
        P(),
        P(),
    )
    out_specs = (P("query"), P(("entity", "query"), None), P("query", None))
    return jax.shard_map(
        make(mesh.shape["query"], mesh.shape["entity"]),
        mesh=mesh, in_specs=in_specs, out_specs=out_specs, check_vma=False,
    )
```

```python
import functools

import jax
import jax.numpy as jnp
import numpy as np
from jax import lax
from jax.experimental import pallas as pl
from jax.experimental.pallas import tpu as pltpu
from jax.sharding import PartitionSpec as P

F32 = jnp.float32
BF16 = jnp.bfloat16
VMEM = pl.BlockSpec(memory_space=pltpu.VMEM)
SMEM = pl.BlockSpec(memory_space=pltpu.SMEM)
MIB = 1 << 20


def places(n):
    sides = 2 if n % 2 == 0 else 1
    m = n // sides
    order = list(range(m))
    if m % 2 == 0:
        order = [2 * z for z in range(m // 2)] + [2 * z + 1 for z in reversed(range(m // 2))]
    return [[order[p] * sides + x for x in range(sides)] for p in range(m)]


def spread_steps(m, across):
    held = [(0, 0)]
    steps = []
    while len(held) < m * (2 if across else 1):
        taken = []
        for shift in (1, -1, 0):
            if shift == 0 and not across:
                continue
            if shift:
                found = [((k, o), (k, (o + shift) % m)) for k, o in held]
            else:
                found = [((k, o), (1 - k, o)) for k, o in held]
            names = [t[2] for t in taken]
            found = [f for f in found if f[1] not in held and f[1] not in names]
            if found:
                best = min(found, key=lambda f: (f[1][0], -min(f[1][1], m - f[1][1]), f[1][1]))
                taken.append((shift,) + best)
        held += [t[2] for t in taken]
        steps.append(taken)
    return steps, held


def move(x, place, shift):
    m = len(place)
    pairs = []
    for p in range(m):
        for side in range(len(place[0])):
            source = place[(p + shift) % m][side] if shift else place[p][1 - side]
            pairs.append((source, place[p][side]))
    return lax.ppermute(x, "query", sorted(pairs))


def owners(place, held, n):
    owner = np.zeros((n, n), np.int32)
    for p in range(len(place)):
        for side in range(len(place[0])):
            for slot, (k, o) in enumerate(held):
                owner[place[p][side], slot] = place[(p + o) % len(place)][side ^ k]
    return owner


def partner(x, size, far):
    return lax.ppermute(x, "entity", [(i, i ^ far) for i in range(size)])


class Shape:
    def __init__(self, tw, sw):
        self.tw, self.sw = tw, sw
        self.half = tw // 2
        self.wide = -(-self.half // 128) * 128
        self.re, self.im = sw, sw + self.wide
        self.total = sw + 2 * self.wide


def put_row(out, student, teacher, shape):
    out[:, : shape.sw] = student.astype(BF16)
    pad = jnp.zeros((teacher.shape[0], shape.wide - shape.half), F32)
    for start, at in ((0, shape.re), (shape.half, shape.im)):
        piece = teacher[:, start : start + shape.half]
        out[:, at : at + shape.wide] = jnp.concatenate([piece, pad], axis=1).astype(BF16)


def pack_kernel(shape, teacher_t, student, anchor_ids, relation_ids, side_flags, out, cols):
    rows = jnp.concatenate([anchor_ids[...], relation_ids[...], side_flags[...]], axis=0).astype(F32)
    rows = jnp.concatenate([rows, jnp.zeros((5, rows.shape[1]), F32)], axis=0)
    cols[...] = rows.T.astype(jnp.int32)
    put_row(out, student[...].astype(F32), teacher_t[...].astype(F32).T, shape)


def pack(teacher, student, ids, shape):
    return pl.pallas_call(
        functools.partial(pack_kernel, shape),
        out_shape=(
            jax.ShapeDtypeStruct((teacher.shape[0], shape.total), BF16),
            jax.ShapeDtypeStruct((ids[0].shape[0], 8), jnp.int32),
        ),
        in_specs=[VMEM] * 5,
        out_specs=(VMEM, VMEM),
        compiler_params=pltpu.CompilerParams(vmem_limit_bytes=60 * MIB),
        name="pack_rows",
    )(teacher.T, student, *[x[None] for x in ids])


def relation_kernel(shape, rel, block, cut, base, cols, table_t, student, out):
    start = base[0] * block
    ids = cols[:, 1:2] - start
    hot = (ids == lax.broadcasted_iota(jnp.int32, (cols.shape[0], block), 1)).astype(F32).astype(BF16)
    tail = block - cut
    lanes = lax.broadcasted_iota(jnp.int32, (shape.tw, tail), 1) + cut
    rows = lax.broadcasted_iota(jnp.int32, (tail, shape.sw), 0) + cut
    table = jnp.where(lanes < rel - start, table_t[:, cut:], jnp.zeros((shape.tw, tail), BF16))
    small = jnp.where(rows < rel - start, student[cut:, :], jnp.zeros((tail, shape.sw), BF16))
    dims = (((1,), (1,)), ((), ()))
    found = lax.dot_general(hot[:, cut:], table, dims, preferred_element_type=F32)
    found_s = jnp.dot(hot[:, cut:], small, preferred_element_type=F32)
    if cut:
        found += lax.dot_general(hot[:, :cut], table_t[:, :cut], dims, preferred_element_type=F32)
        found_s += jnp.dot(hot[:, :cut], student[:cut, :], preferred_element_type=F32)
    put_row(out, found_s, found, shape)


def relation_rows(base, cols, table, student, block, shape):
    rel, tw = table.shape
    q = cols.shape[0]
    cut = max(0, rel - rel // block * block) // 128 * 128
    whole = lambda i, base: (0, 0)
    return pl.pallas_call(
        functools.partial(relation_kernel, shape, rel, block, cut),
        out_shape=jax.ShapeDtypeStruct((q, shape.total), BF16),
        grid_spec=pltpu.PrefetchScalarGridSpec(
            num_scalar_prefetch=1,
            grid=(1,),
            in_specs=[
                pl.BlockSpec((q, cols.shape[1]), whole),
                pl.BlockSpec((tw, block), lambda i, base: (0, base[0])),
                pl.BlockSpec((block, shape.sw), lambda i, base: (base[0], 0)),
            ],
            out_specs=pl.BlockSpec((q, shape.total), whole),
        ),
        compiler_params=pltpu.CompilerParams(vmem_limit_bytes=56 * MIB),
        cost_estimate=pl.CostEstimate(
            flops=2 * q * tw * block, bytes_accessed=2 * tw * block, transcendentals=0
        ),
        name="relation_rows",
    )(base, cols, table.T, student)


def joined(shards, columns):
    return jnp.concatenate([shard[:, columns] for shard in shards], axis=0)


def anchor_kernel(count, first_slot, own, has_acc, bases, cols, *rest):
    acc_in, rest = (rest[0], rest[1:]) if has_acc else (None, rest)
    shards, out = rest[:count], rest[count]
    ids = cols[:, 0:1]
    lane = lax.broadcasted_iota(jnp.int32, (cols.shape[0], own), 1)
    group = max(1, 512 // own)
    total = None
    for first in range(0, count, group):
        last = min(count, first + group)
        hot = jnp.concatenate([(ids - bases[first_slot + j] == lane).astype(F32).astype(BF16) for j in range(first, last)], axis=1)
        found = jnp.dot(hot, joined(shards[first:last], slice(None)), preferred_element_type=F32)
        total = found if total is None else total + found
    total = total.astype(BF16)
    out[...] = total + acc_in[...] if has_acc else total


def anchor_rows(bases, first_slot, cols, shards, acc, shape):
    own = shards[0].shape[0]
    q, count = cols.shape[0], len(shards)
    operands = [bases, cols] + ([] if acc is None else [acc]) + list(shards)
    return pl.pallas_call(
        functools.partial(anchor_kernel, count, first_slot, own, acc is not None),
        out_shape=jax.ShapeDtypeStruct((q, shape.total), BF16),
        in_specs=[SMEM, VMEM] + ([] if acc is None else [VMEM]) + [VMEM] * count,
        out_specs=VMEM,
        compiler_params=pltpu.CompilerParams(vmem_limit_bytes=2 * count * own * (shape.total + q) + 12 * MIB),
        cost_estimate=pl.CostEstimate(
            flops=2 * q * count * own * shape.total,
            bytes_accessed=2 * (count * own + 2 * q) * shape.total,
            transcendentals=0,
        ),
        name="anchor_rows",
    )(*operands)


def score_kernel(shape, own, n, chunk, mine, other, relation, relation_b, cols, *rest):
    shards, (t_out, s_out, stats, q_student, q_teacher) = rest[:n], rest[n:]
    q = mine.shape[0]
    sw, wide = shape.sw, shape.wide
    rows = 128

    def build(i, _):
        at = pl.ds(pl.multiple_of(i * rows, rows), rows)
        g = (2 * cols[at, 2:3] - 1).astype(F32)
        a = mine[at, :].astype(F32) + other[at, :].astype(F32)
        r = relation[at, :].astype(F32) + relation_b[at, :].astype(F32)
        a_re, a_im = a[:, shape.re : shape.re + wide], a[:, shape.im : shape.im + wide]
        r_re, r_im = r[:, shape.re : shape.re + wide], r[:, shape.im : shape.im + wide]
        q_teacher[at, :wide] = (a_re * r_re - g * a_im * r_im).astype(BF16)
        q_teacher[at, wide:] = (a_im * r_re + g * a_re * r_im).astype(BF16)
        a_s, r_s = a[:, :sw], r[:, :sw]
        a_x, r_x = pltpu.roll(a_s, sw // 2, 1), pltpu.roll(r_s, sw // 2, 1)
        low = lax.broadcasted_iota(jnp.int32, (rows, sw), 1) < sw // 2
        re2, im2 = jnp.where(low, r_s, r_x), jnp.where(low, r_x, r_s)
        q_student[at, :] = (a_s * re2 + jnp.where(low, -g, g) * a_x * im2).astype(BF16)
        return 0

    lax.fori_loop(0, q // rows, build, 0)
    dims = (((1,), (1,)), ((), ()))

    def score(c, carry):
        top_t, total_t, weighted, top_s, total_s = carry
        at = slice(c * chunk, (c + 1) * chunk)
        group = shards[c * chunk // own : (c + 1) * chunk // own]
        t = lax.dot_general(joined(group, slice(sw, None)), q_teacher[...], dims, preferred_element_type=F32)
        s = lax.dot_general(joined(group, slice(0, sw)), q_student[...], dims, preferred_element_type=F32)
        t_out[at, :] = t
        s_out[at, :] = s
        new_t = jnp.maximum(top_t, jnp.max(t, axis=0, keepdims=True))
        new_s = jnp.maximum(top_s, jnp.max(s, axis=0, keepdims=True))
        scale_t, scale_s = jnp.exp(top_t - new_t), jnp.exp(top_s - new_s)
        e = jnp.exp(t - new_t)
        total_t = total_t * scale_t + jnp.sum(e, axis=0, keepdims=True)
        weighted = weighted * scale_t + jnp.sum(e * (t - s), axis=0, keepdims=True)
        total_s = total_s * scale_s + jnp.sum(jnp.exp(s - new_s), axis=0, keepdims=True)
        return new_t, total_t, weighted, new_s, total_s

    lowest = jnp.full((1, q), -jnp.inf, F32)
    nothing = jnp.zeros((1, q), F32)
    found = (lowest, nothing, nothing, lowest, nothing)
    for c in range(n * own // chunk):
        found = score(c, found)
    stats[...] = jnp.concatenate(list(found) + [nothing] * 3, axis=0)


def scores(mine, other, relation, relation_b, cols, shards, shape):
    n, own = len(shards), shards[0].shape[0]
    q = mine.shape[0]
    slab = n * own
    chunk = 512 if slab % 512 == 0 else own
    return pl.pallas_call(
        functools.partial(score_kernel, shape, own, n, chunk),
        out_shape=(
            jax.ShapeDtypeStruct((slab, q), F32),
            jax.ShapeDtypeStruct((slab, q), F32),
            jax.ShapeDtypeStruct((8, q), F32),
            jax.ShapeDtypeStruct((q, shape.sw), BF16),
        ),
        in_specs=[VMEM] * (5 + n),
        out_specs=(VMEM,) * 4,
        scratch_shapes=[pltpu.VMEM((q, 2 * shape.wide), BF16)],
        compiler_params=pltpu.CompilerParams(vmem_limit_bytes=8 * slab * q + 2 * slab * shape.total + 10 * MIB),
        cost_estimate=pl.CostEstimate(
            flops=2 * q * slab * shape.total, bytes_accessed=2 * slab * shape.total + 8 * slab * q, transcendentals=2 * slab * q
        ),
        name="scores",
    )(mine, other, relation, relation_b, cols, *shards)


def combine(a, b):
    top_t, top_s = jnp.maximum(a[0:1], b[0:1]), jnp.maximum(a[3:4], b[3:4])
    at, bt = jnp.exp(a[0:1] - top_t), jnp.exp(b[0:1] - top_t)
    as_, bs = jnp.exp(a[3:4] - top_s), jnp.exp(b[3:4] - top_s)
    total_t = a[1:2] * at + b[1:2] * bt
    weighted = a[2:3] * at + b[2:3] * bt
    total_s = a[4:5] * as_ + b[4:5] * bs
    return top_t, total_t, weighted, top_s, total_s


def grad_kernel(n, own, chunk, sw, order, t_in, s_in, mine, other, q_student, *rest):
    shards, (divergence, q_grad), outs = rest[:n], rest[n : n + 2], rest[n + 2 : -1]
    e_grad = rest[-1]
    top_t, total_t, weighted, top_s, total_s = combine(mine[...], other[...])
    divergence[...] = weighted / total_t - top_t - jnp.log(total_t) + top_s + jnp.log(total_s)
    over_t, over_s = 1.0 / total_t, 1.0 / total_s
    per = chunk // own

    def step(c, total):
        at = slice(c * chunk, (c + 1) * chunk)
        prob_t = jnp.exp(t_in[at, :] - top_t) * over_t
        prob_s = jnp.exp(s_in[at, :] - top_s) * over_s
        weights = (prob_s - prob_t).astype(BF16)
        grad = jnp.dot(weights, q_student[...], preferred_element_type=F32).astype(BF16)
        for k in range(per):
            e_grad[order[c * per + k]] = grad[k * own : (k + 1) * own, :]
        return total + lax.dot_general(
            joined(shards[c * per : (c + 1) * per], slice(0, sw)),
            weights,
            (((0,), (0,)), ((), ())),
            preferred_element_type=F32,
        )

    q = q_student.shape[0]
    total = jnp.zeros((sw, q), F32)
    for c in range(n * own // chunk):
        total = step(c, total)
    q_grad[...] = total.T
    count = n // len(outs)
    for d, out in enumerate(outs):
        out[...] = e_grad[d * count : (d + 1) * count]


def gradients(order, near, t, s, mine, other, q_student, shards):
    n, own = len(shards), shards[0].shape[0]
    q, sw = q_student.shape
    slab = n * own
    shape_total = shards[0].shape[1]
    chunk = 512 if slab % 512 == 0 else own
    return pl.pallas_call(
        functools.partial(grad_kernel, n, own, chunk, sw),
        out_shape=(
            jax.ShapeDtypeStruct((1, q), F32),
            jax.ShapeDtypeStruct((q, sw), F32),
        )
        + (jax.ShapeDtypeStruct((n // near, own, sw), BF16),) * near,
        in_specs=[SMEM] + [VMEM] * (5 + n),
        out_specs=(VMEM,) * (2 + near),
        scratch_shapes=[pltpu.VMEM((n, own, sw), BF16)],
        compiler_params=pltpu.CompilerParams(vmem_limit_bytes=8 * slab * q + 2 * slab * shape_total + 10 * MIB),
        cost_estimate=pl.CostEstimate(
            flops=4 * q * slab * sw, bytes_accessed=8 * slab * q, transcendentals=2 * slab * q
        ),
        name="gradients",
    )(order, t, s, mine, other, q_student, *shards)


def add_kernel(count, *refs):
    terms, outs = refs[:count], refs[count:]
    for e, out in enumerate(outs):
        total = terms[0][e].astype(F32)
        for term in terms[1:]:
            total += term[e].astype(F32)
        out[...] = total.astype(out.dtype)


def add_blocks(terms):
    far, own, sw = terms[0].shape
    return pl.pallas_call(
        functools.partial(add_kernel, len(terms)),
        out_shape=(jax.ShapeDtypeStruct((own, sw), F32),)
        + (jax.ShapeDtypeStruct((own, sw), BF16),) * (far - 1),
        in_specs=[VMEM] * len(terms),
        out_specs=(VMEM,) * far,
        compiler_params=pltpu.CompilerParams(vmem_limit_bytes=8 * MIB),
        name="add_blocks",
    )(*terms)


def reduce_blocks(blocks, beside, n):
    near, far = len(blocks), n // len(blocks)
    terms = [blocks[0]]
    for d in range(1, near):
        terms.append(lax.ppermute(blocks[d], "query", [(i, i ^ d) for i in range(n)]))
    terms[-1], beside = lax.optimization_barrier((terms[-1], beside))
    sums = add_blocks(terms)
    total = sums[0]
    for e in range(1, far):
        pairs = [(h * near + r, (h + e) % far * near + r) for h in range(far) for r in range(near)]
        total = total + lax.ppermute(sums[e], "query", pairs).astype(F32)
    return total, beside


def make(n, groups):
    place = places(n)
    steps, held = spread_steps(len(place), len(place[0]) == 2)
    table = owners(place, held, n)
    near = next(k for k in (4, 2, 1) if n % k == 0)
    me = np.arange(n)[:, None]
    position = ((table % near) ^ (me % near)) * (n // near) + (table // near - me // near) % (n // near)

    def per_device(
        anchor_ids,
        relation_ids,
        side_flags,
        teacher_entities,
        student_entities,
        teacher_relations,
        student_relations,
    ):
        own, tw = teacher_entities.shape
        shape = Shape(tw, student_entities.shape[1])
        owner, order = jnp.asarray(np.stack([table, position], axis=1))[lax.axis_index("query")]
        bases = (owner + lax.axis_index("entity") * n) * own
        packed, cols = pack(
            teacher_entities, student_entities, (anchor_ids, relation_ids, side_flags), shape
        )
        have = {(0, 0): packed}
        block = -(-teacher_relations.shape[0] // 512) * 256
        base = (lax.axis_index("entity") % 2).astype(jnp.int32)[None]
        own_key = (0, 0)
        have[own_key], base = lax.optimization_barrier((have[own_key], base))
        anchors, counted = None, 0
        kept, last = {}, {}
        for number, step in enumerate(steps):
            got = {}
            for shift, old, new in step:
                operand = have[old]
                if shift in last and last[shift] != old:
                    before = last[shift]
                    operand, kept[before] = lax.optimization_barrier((operand, have[before]))
                got[new] = move(operand, place, shift)
                last[shift] = new
            if number == 0:
                relation = relation_rows(base, cols, teacher_relations, student_relations, block, shape)
                got, relation = lax.optimization_barrier((got, relation))
                relation_b = partner(relation, groups, 1)
            if number == len(steps) - 1:
                counted = len(have)
                names = held[:counted]
                anchors = anchor_rows(bases, 0, cols, [kept.get(h, have[h]) for h in names], None, shape)
            have.update(got)
        have.update(kept)
        shards = [have[h] for h in held]
        mine = anchor_rows(bases, counted, cols, shards[counted:], anchors, shape)
        far = 1
        while far < groups // 2:
            mine = mine + partner(mine, groups, far)
            far *= 2
        other = partner(mine, groups, far)
        t, s, stats, q_student = scores(mine, other, relation, relation_b, cols, shards, shape)
        far = 1
        while far < groups // 2:
            found = combine(stats, partner(stats, groups, far))
            stats = jnp.concatenate(list(found) + [jnp.zeros_like(found[0])] * 3, axis=0)
            far *= 2
        divergence, q_grad, *blocks = gradients(
            order, near, t, s, stats, partner(stats, groups, far), q_student, shards
        )
        far = 1
        while far < groups:
            q_grad = q_grad + partner(q_grad, groups, far)
            far *= 2
        entity_grad, q_grad = reduce_blocks(blocks, q_grad, n)
        return (divergence[0], entity_grad, q_grad)

    return per_device


def solution(mesh):
    in_specs = (
        P("query"),
        P("query"),
        P("query"),
        P(("entity", "query"), None),
        P(("entity", "query"), None),
        P(),
        P(),
    )
    out_specs = (P("query"), P(("entity", "query"), None), P("query", None))
    return jax.shard_map(
        make(mesh.shape["query"], mesh.shape["entity"]),
        mesh=mesh, in_specs=in_specs, out_specs=out_specs, check_vma=False,
    )
```

```python
import functools

import jax
import jax.numpy as jnp
import numpy as np
from jax import lax
from jax.experimental import pallas as pl
from jax.experimental.pallas import tpu as pltpu
from jax.sharding import PartitionSpec as P

F32 = jnp.float32
BF16 = jnp.bfloat16
VMEM = pl.BlockSpec(memory_space=pltpu.VMEM)
SMEM = pl.BlockSpec(memory_space=pltpu.SMEM)
MIB = 1 << 20


def places(n):
    sides = 2 if n % 2 == 0 else 1
    m = n // sides
    order = list(range(m))
    if m % 2 == 0:
        order = [2 * z for z in range(m // 2)] + [2 * z + 1 for z in reversed(range(m // 2))]
    return [[order[p] * sides + x for x in range(sides)] for p in range(m)]


def spread_steps(m, across):
    held = [(0, 0)]
    steps = []
    while len(held) < m * (2 if across else 1):
        taken = []
        for shift in (1, -1, 0):
            if shift == 0 and not across:
                continue
            if shift:
                found = [((k, o), (k, (o + shift) % m)) for k, o in held]
            else:
                found = [((k, o), (1 - k, o)) for k, o in held]
            names = [t[2] for t in taken]
            found = [f for f in found if f[1] not in held and f[1] not in names]
            if found:
                best = min(found, key=lambda f: (f[1][0], -min(f[1][1], m - f[1][1]), f[1][1]))
                taken.append((shift,) + best)
        held += [t[2] for t in taken]
        steps.append(taken)
    return steps, held


def move(x, place, shift):
    m = len(place)
    pairs = []
    for p in range(m):
        for side in range(len(place[0])):
            source = place[(p + shift) % m][side] if shift else place[p][1 - side]
            pairs.append((source, place[p][side]))
    return lax.ppermute(x, "query", sorted(pairs))


def owners(place, held, n):
    owner = np.zeros((n, n), np.int32)
    for p in range(len(place)):
        for side in range(len(place[0])):
            for slot, (k, o) in enumerate(held):
                owner[place[p][side], slot] = place[(p + o) % len(place)][side ^ k]
    return owner


def partner(x, size, far):
    return lax.ppermute(x, "entity", [(i, i ^ far) for i in range(size)])


class Shape:
    def __init__(self, tw, sw):
        self.tw, self.sw = tw, sw
        self.half = tw // 2
        self.wide = -(-self.half // 128) * 128
        self.re, self.im = sw, sw + self.wide
        self.total = sw + 2 * self.wide


def put_row(out, student, teacher, shape):
    out[:, : shape.sw] = student.astype(BF16)
    pad = jnp.zeros((teacher.shape[0], shape.wide - shape.half), F32)
    for start, at in ((0, shape.re), (shape.half, shape.im)):
        piece = teacher[:, start : start + shape.half]
        out[:, at : at + shape.wide] = jnp.concatenate([piece, pad], axis=1).astype(BF16)


def pack_kernel(shape, teacher_t, student, anchor_ids, relation_ids, side_flags, out, cols):
    rows = jnp.concatenate([anchor_ids[...], relation_ids[...], side_flags[...]], axis=0).astype(F32)
    rows = jnp.concatenate([rows, jnp.zeros((5, rows.shape[1]), F32)], axis=0)
    cols[...] = rows.T.astype(jnp.int32)
    put_row(out, student[...].astype(F32), teacher_t[...].astype(F32).T, shape)


def pack(teacher, student, ids, shape):
    return pl.pallas_call(
        functools.partial(pack_kernel, shape),
        out_shape=(
            jax.ShapeDtypeStruct((teacher.shape[0], shape.total), BF16),
            jax.ShapeDtypeStruct((ids[0].shape[0], 8), jnp.int32),
        ),
        in_specs=[VMEM] * 5,
        out_specs=(VMEM, VMEM),
        compiler_params=pltpu.CompilerParams(vmem_limit_bytes=60 * MIB),
        name="pack_rows",
    )(teacher.T, student, *[x[None] for x in ids])


def relation_kernel(shape, rel, block, cut, base, cols, table_t, student, out):
    start = base[0] * block
    ids = cols[:, 1:2] - start
    hot = (ids == lax.broadcasted_iota(jnp.int32, (cols.shape[0], block), 1)).astype(F32).astype(BF16)
    tail = block - cut
    lanes = lax.broadcasted_iota(jnp.int32, (shape.tw, tail), 1) + cut
    rows = lax.broadcasted_iota(jnp.int32, (tail, shape.sw), 0) + cut
    table = jnp.where(lanes < rel - start, table_t[:, cut:], jnp.zeros((shape.tw, tail), BF16))
    small = jnp.where(rows < rel - start, student[cut:, :], jnp.zeros((tail, shape.sw), BF16))
    dims = (((1,), (1,)), ((), ()))
    found = lax.dot_general(hot[:, cut:], table, dims, preferred_element_type=F32)
    found_s = jnp.dot(hot[:, cut:], small, preferred_element_type=F32)
    if cut:
        found += lax.dot_general(hot[:, :cut], table_t[:, :cut], dims, preferred_element_type=F32)
        found_s += jnp.dot(hot[:, :cut], student[:cut, :], preferred_element_type=F32)
    put_row(out, found_s, found, shape)


def relation_rows(base, cols, table, student, block, shape):
    rel, tw = table.shape
    q = cols.shape[0]
    cut = max(0, rel - rel // block * block) // 128 * 128
    whole = lambda i, base: (0, 0)
    return pl.pallas_call(
        functools.partial(relation_kernel, shape, rel, block, cut),
        out_shape=jax.ShapeDtypeStruct((q, shape.total), BF16),
        grid_spec=pltpu.PrefetchScalarGridSpec(
            num_scalar_prefetch=1,
            grid=(1,),
            in_specs=[
                pl.BlockSpec((q, cols.shape[1]), whole),
                pl.BlockSpec((tw, block), lambda i, base: (0, base[0])),
                pl.BlockSpec((block, shape.sw), lambda i, base: (base[0], 0)),
            ],
            out_specs=pl.BlockSpec((q, shape.total), whole),
        ),
        compiler_params=pltpu.CompilerParams(vmem_limit_bytes=56 * MIB),
        cost_estimate=pl.CostEstimate(
            flops=2 * q * tw * block, bytes_accessed=2 * tw * block, transcendentals=0
        ),
        name="relation_rows",
    )(base, cols, table.T, student)


def joined(shards, columns):
    return jnp.concatenate([shard[:, columns] for shard in shards], axis=0)


def anchor_kernel(count, first_slot, own, has_acc, me, core, owner, cols, *rest):
    acc_in, rest = (rest[0], rest[1:]) if has_acc else (None, rest)
    shards, out = rest[:count], rest[count]
    slab = owner.shape[1] * own
    ids = cols[:, 0:1] - core[0] * slab
    lane = lax.broadcasted_iota(jnp.int32, (cols.shape[0], own), 1)
    group = max(1, 512 // own)
    total = None
    for first in range(0, count, group):
        last = min(count, first + group)
        starts = [owner[me[0], first_slot + j] * own for j in range(first, last)]
        hot = jnp.concatenate([(ids - start == lane).astype(F32).astype(BF16) for start in starts], axis=1)
        found = jnp.dot(hot, joined(shards[first:last], slice(None)), preferred_element_type=F32)
        total = found if total is None else total + found
    total = total.astype(BF16)
    out[...] = total + acc_in[...] if has_acc else total


def anchor_rows(spot, first_slot, cols, shards, acc, shape):
    own = shards[0].shape[0]
    q, count = cols.shape[0], len(shards)
    operands = [*spot, cols] + ([] if acc is None else [acc]) + list(shards)
    return pl.pallas_call(
        functools.partial(anchor_kernel, count, first_slot, own, acc is not None),
        out_shape=jax.ShapeDtypeStruct((q, shape.total), BF16),
        in_specs=[SMEM] * 3 + [VMEM] * (len(operands) - 3),
        out_specs=VMEM,
        compiler_params=pltpu.CompilerParams(vmem_limit_bytes=2 * count * own * (shape.total + q) + 12 * MIB),
        cost_estimate=pl.CostEstimate(
            flops=2 * q * count * own * shape.total,
            bytes_accessed=2 * (count * own + 2 * q) * shape.total,
            transcendentals=0,
        ),
        name="anchor_rows",
    )(*operands)


def score_kernel(shape, own, n, chunk, mine, other, relation, relation_b, cols, *rest):
    shards, (t_out, s_out, stats, q_student, q_teacher) = rest[:n], rest[n:]
    q = mine.shape[0]
    sw, wide = shape.sw, shape.wide
    rows = 128

    def build(i, _):
        at = pl.ds(pl.multiple_of(i * rows, rows), rows)
        g = (2 * cols[at, 2:3] - 1).astype(F32)
        a = mine[at, :].astype(F32) + other[at, :].astype(F32)
        r = relation[at, :].astype(F32) + relation_b[at, :].astype(F32)
        a_re, a_im = a[:, shape.re : shape.re + wide], a[:, shape.im : shape.im + wide]
        r_re, r_im = r[:, shape.re : shape.re + wide], r[:, shape.im : shape.im + wide]
        q_teacher[at, :wide] = (a_re * r_re - g * a_im * r_im).astype(BF16)
        q_teacher[at, wide:] = (a_im * r_re + g * a_re * r_im).astype(BF16)
        a_s, r_s = a[:, :sw], r[:, :sw]
        a_x, r_x = pltpu.roll(a_s, sw // 2, 1), pltpu.roll(r_s, sw // 2, 1)
        low = lax.broadcasted_iota(jnp.int32, (rows, sw), 1) < sw // 2
        re2, im2 = jnp.where(low, r_s, r_x), jnp.where(low, r_x, r_s)
        q_student[at, :] = (a_s * re2 + jnp.where(low, -g, g) * a_x * im2).astype(BF16)
        return 0

    lax.fori_loop(0, q // rows, build, 0)
    dims = (((1,), (1,)), ((), ()))

    def score(c, carry):
        top_t, total_t, weighted, top_s, total_s = carry
        at = slice(c * chunk, (c + 1) * chunk)
        group = shards[c * chunk // own : (c + 1) * chunk // own]
        t = lax.dot_general(joined(group, slice(sw, None)), q_teacher[...], dims, preferred_element_type=F32)
        s = lax.dot_general(joined(group, slice(0, sw)), q_student[...], dims, preferred_element_type=F32)
        t_out[at, :] = t
        s_out[at, :] = s
        new_t = jnp.maximum(top_t, jnp.max(t, axis=0, keepdims=True))
        new_s = jnp.maximum(top_s, jnp.max(s, axis=0, keepdims=True))
        scale_t, scale_s = jnp.exp(top_t - new_t), jnp.exp(top_s - new_s)
        e = jnp.exp(t - new_t)
        total_t = total_t * scale_t + jnp.sum(e, axis=0, keepdims=True)
        weighted = weighted * scale_t + jnp.sum(e * (t - s), axis=0, keepdims=True)
        total_s = total_s * scale_s + jnp.sum(jnp.exp(s - new_s), axis=0, keepdims=True)
        return new_t, total_t, weighted, new_s, total_s

    lowest = jnp.full((1, q), -jnp.inf, F32)
    nothing = jnp.zeros((1, q), F32)
    found = (lowest, nothing, nothing, lowest, nothing)
    for c in range(n * own // chunk):
        found = score(c, found)
    stats[...] = jnp.concatenate(list(found) + [nothing] * 3, axis=0)


def scores(mine, other, relation, relation_b, cols, shards, shape):
    n, own = len(shards), shards[0].shape[0]
    q = mine.shape[0]
    slab = n * own
    chunk = 512 if slab % 512 == 0 else own
    return pl.pallas_call(
        functools.partial(score_kernel, shape, own, n, chunk),
        out_shape=(
            jax.ShapeDtypeStruct((slab, q), F32),
            jax.ShapeDtypeStruct((slab, q), F32),
            jax.ShapeDtypeStruct((8, q), F32),
            jax.ShapeDtypeStruct((q, shape.sw), BF16),
        ),
        in_specs=[VMEM] * (5 + n),
        out_specs=(VMEM,) * 4,
        scratch_shapes=[pltpu.VMEM((q, 2 * shape.wide), BF16)],
        compiler_params=pltpu.CompilerParams(vmem_limit_bytes=8 * slab * q + 2 * slab * shape.total + 10 * MIB),
        cost_estimate=pl.CostEstimate(
            flops=2 * q * slab * shape.total, bytes_accessed=2 * slab * shape.total + 8 * slab * q, transcendentals=2 * slab * q
        ),
        name="scores",
    )(mine, other, relation, relation_b, cols, *shards)


def combine(a, b):
    top_t, top_s = jnp.maximum(a[0:1], b[0:1]), jnp.maximum(a[3:4], b[3:4])
    at, bt = jnp.exp(a[0:1] - top_t), jnp.exp(b[0:1] - top_t)
    as_, bs = jnp.exp(a[3:4] - top_s), jnp.exp(b[3:4] - top_s)
    total_t = a[1:2] * at + b[1:2] * bt
    weighted = a[2:3] * at + b[2:3] * bt
    total_s = a[4:5] * as_ + b[4:5] * bs
    return top_t, total_t, weighted, top_s, total_s


def grad_kernel(n, own, chunk, sw, me, order, t_in, s_in, mine, other, q_student, *rest):
    shards, (divergence, q_grad), outs = rest[:n], rest[n : n + 2], rest[n + 2 : -1]
    e_grad = rest[-1]
    top_t, total_t, weighted, top_s, total_s = combine(mine[...], other[...])
    divergence[...] = weighted / total_t - top_t - jnp.log(total_t) + top_s + jnp.log(total_s)
    over_t, over_s = 1.0 / total_t, 1.0 / total_s
    per = chunk // own

    def step(c, total):
        at = slice(c * chunk, (c + 1) * chunk)
        prob_t = jnp.exp(t_in[at, :] - top_t) * over_t
        prob_s = jnp.exp(s_in[at, :] - top_s) * over_s
        weights = (prob_s - prob_t).astype(BF16)
        grad = jnp.dot(weights, q_student[...], preferred_element_type=F32).astype(BF16)
        for k in range(per):
            e_grad[order[me[0], c * per + k]] = grad[k * own : (k + 1) * own, :]
        return total + lax.dot_general(
            joined(shards[c * per : (c + 1) * per], slice(0, sw)),
            weights,
            (((0,), (0,)), ((), ())),
            preferred_element_type=F32,
        )

    q = q_student.shape[0]
    total = jnp.zeros((sw, q), F32)
    for c in range(n * own // chunk):
        total = step(c, total)
    q_grad[...] = total.T
    count = n // len(outs)
    for d, out in enumerate(outs):
        out[...] = e_grad[d * count : (d + 1) * count]


def gradients(me, order, near, t, s, mine, other, q_student, shards):
    n, own = len(shards), shards[0].shape[0]
    q, sw = q_student.shape
    slab = n * own
    shape_total = shards[0].shape[1]
    chunk = 512 if slab % 512 == 0 else own
    return pl.pallas_call(
        functools.partial(grad_kernel, n, own, chunk, sw),
        out_shape=(
            jax.ShapeDtypeStruct((1, q), F32),
            jax.ShapeDtypeStruct((q, sw), F32),
        )
        + (jax.ShapeDtypeStruct((n // near, own, sw), BF16),) * near,
        in_specs=[SMEM] * 2 + [VMEM] * (5 + n),
        out_specs=(VMEM,) * (2 + near),
        scratch_shapes=[pltpu.VMEM((n, own, sw), BF16)],
        compiler_params=pltpu.CompilerParams(vmem_limit_bytes=8 * slab * q + 2 * slab * shape_total + 10 * MIB),
        cost_estimate=pl.CostEstimate(
            flops=4 * q * slab * sw, bytes_accessed=8 * slab * q, transcendentals=2 * slab * q
        ),
        name="gradients",
    )(me, order, t, s, mine, other, q_student, *shards)


def add_kernel(count, *refs):
    terms, outs = refs[:count], refs[count:]
    for e, out in enumerate(outs):
        total = terms[0][e].astype(F32)
        for term in terms[1:]:
            total += term[e].astype(F32)
        out[...] = total.astype(out.dtype)


def add_blocks(terms):
    far, own, sw = terms[0].shape
    return pl.pallas_call(
        functools.partial(add_kernel, len(terms)),
        out_shape=(jax.ShapeDtypeStruct((own, sw), F32),)
        + (jax.ShapeDtypeStruct((own, sw), BF16),) * (far - 1),
        in_specs=[VMEM] * len(terms),
        out_specs=(VMEM,) * far,
        compiler_params=pltpu.CompilerParams(vmem_limit_bytes=8 * MIB),
        name="add_blocks",
    )(*terms)


def reduce_blocks(blocks, beside, n):
    near, far = len(blocks), n // len(blocks)
    terms = [blocks[0]]
    for d in range(1, near):
        terms.append(lax.ppermute(blocks[d], "query", [(i, i ^ d) for i in range(n)]))
    terms[-1], beside = lax.optimization_barrier((terms[-1], beside))
    sums = add_blocks(terms)
    total = sums[0]
    for e in range(1, far):
        pairs = [(h * near + r, (h + e) % far * near + r) for h in range(far) for r in range(near)]
        total = total + lax.ppermute(sums[e], "query", pairs).astype(F32)
    return total, beside


def make(n, groups):
    place = places(n)
    steps, held = spread_steps(len(place), len(place[0]) == 2)
    table = owners(place, held, n)
    near = next(k for k in (4, 2, 1) if n % k == 0)
    me = np.arange(n)[:, None]
    position = ((table % near) ^ (me % near)) * (n // near) + (table // near - me // near) % (n // near)

    def per_device(
        anchor_ids,
        relation_ids,
        side_flags,
        teacher_entities,
        student_entities,
        teacher_relations,
        student_relations,
    ):
        own, tw = teacher_entities.shape
        shape = Shape(tw, student_entities.shape[1])
        me = lax.axis_index("query")[None]
        spot = (me, lax.axis_index("entity")[None], jnp.asarray(table))
        packed, cols = pack(
            teacher_entities, student_entities, (anchor_ids, relation_ids, side_flags), shape
        )
        have = {(0, 0): packed}
        block = -(-teacher_relations.shape[0] // 512) * 256
        base = (lax.axis_index("entity") % 2).astype(jnp.int32)[None]
        own_key = (0, 0)
        have[own_key], base = lax.optimization_barrier((have[own_key], base))
        anchors, counted = None, 0
        kept, last = {}, {}
        for number, step in enumerate(steps):
            got = {}
            for shift, old, new in step:
                operand = have[old]
                if shift in last and last[shift] != old:
                    before = last[shift]
                    operand, kept[before] = lax.optimization_barrier((operand, have[before]))
                got[new] = move(operand, place, shift)
                last[shift] = new
            if number == 0:
                relation = relation_rows(base, cols, teacher_relations, student_relations, block, shape)
                got, relation = lax.optimization_barrier((got, relation))
                relation_b = partner(relation, groups, 1)
            if number == len(steps) - 1:
                counted = len(have)
                names = held[:counted]
                anchors = anchor_rows(spot, 0, cols, [kept.get(h, have[h]) for h in names], None, shape)
            have.update(got)
        have.update(kept)
        shards = [have[h] for h in held]
        mine = anchor_rows(spot, counted, cols, shards[counted:], anchors, shape)
        far = 1
        while far < groups // 2:
            mine = mine + partner(mine, groups, far)
            far *= 2
        other = partner(mine, groups, far)
        t, s, stats, q_student = scores(mine, other, relation, relation_b, cols, shards, shape)
        far = 1
        while far < groups // 2:
            found = combine(stats, partner(stats, groups, far))
            stats = jnp.concatenate(list(found) + [jnp.zeros_like(found[0])] * 3, axis=0)
            far *= 2
        divergence, q_grad, *blocks = gradients(
            me, jnp.asarray(position), near, t, s, stats, partner(stats, groups, far), q_student, shards
        )
        far = 1
        while far < groups:
            q_grad = q_grad + partner(q_grad, groups, far)
            far *= 2
        entity_grad, q_grad = reduce_blocks(blocks, q_grad, n)
        return (divergence[0], entity_grad, q_grad)

    return per_device


def solution(mesh):
    in_specs = (
        P("query"),
        P("query"),
        P("query"),
        P(("entity", "query"), None),
        P(("entity", "query"), None),
        P(),
        P(),
    )
    out_specs = (P("query"), P(("entity", "query"), None), P("query", None))
    return jax.shard_map(
        make(mesh.shape["query"], mesh.shape["entity"]),
        mesh=mesh, in_specs=in_specs, out_specs=out_specs, check_vma=False,
    )
```

```python
import functools

import jax
import jax.numpy as jnp
import numpy as np
from jax import lax
from jax.experimental import pallas as pl
from jax.experimental.pallas import tpu as pltpu
from jax.sharding import PartitionSpec as P

F32 = jnp.float32
BF16 = jnp.bfloat16
VMEM = pl.BlockSpec(memory_space=pltpu.VMEM)
SMEM = pl.BlockSpec(memory_space=pltpu.SMEM)
MIB = 1 << 20


def places(n):
    sides = 2 if n % 2 == 0 else 1
    m = n // sides
    order = list(range(m))
    if m % 2 == 0:
        order = [2 * z for z in range(m // 2)] + [2 * z + 1 for z in reversed(range(m // 2))]
    return [[order[p] * sides + x for x in range(sides)] for p in range(m)]


def spread_steps(m, across):
    held = [(0, 0)]
    steps = []
    while len(held) < m * (2 if across else 1):
        taken = []
        for shift in (1, -1, 0):
            if shift == 0 and not across:
                continue
            if shift:
                found = [((k, o), (k, (o + shift) % m)) for k, o in held]
            else:
                found = [((k, o), (1 - k, o)) for k, o in held]
            names = [t[2] for t in taken]
            found = [f for f in found if f[1] not in held and f[1] not in names]
            if found:
                best = min(found, key=lambda f: (f[1][0], -min(f[1][1], m - f[1][1]), f[1][1]))
                taken.append((shift,) + best)
        held += [t[2] for t in taken]
        steps.append(taken)
    return steps, held


def move(x, place, shift):
    m = len(place)
    pairs = []
    for p in range(m):
        for side in range(len(place[0])):
            source = place[(p + shift) % m][side] if shift else place[p][1 - side]
            pairs.append((source, place[p][side]))
    return lax.ppermute(x, "query", sorted(pairs))


def owners(place, held, n):
    owner = np.zeros((n, n), np.int32)
    for p in range(len(place)):
        for side in range(len(place[0])):
            for slot, (k, o) in enumerate(held):
                owner[place[p][side], slot] = place[(p + o) % len(place)][side ^ k]
    return owner


def partner(x, size, far):
    return lax.ppermute(x, "entity", [(i, i ^ far) for i in range(size)])


class Shape:
    def __init__(self, tw, sw):
        self.tw, self.sw = tw, sw
        self.half = tw // 2
        self.wide = -(-self.half // 128) * 128
        self.re, self.im = sw, sw + self.wide
        self.total = sw + 2 * self.wide


def put_row(out, student, teacher, shape):
    out[:, : shape.sw] = student.astype(BF16)
    pad = jnp.zeros((teacher.shape[0], shape.wide - shape.half), F32)
    for start, at in ((0, shape.re), (shape.half, shape.im)):
        piece = teacher[:, start : start + shape.half]
        out[:, at : at + shape.wide] = jnp.concatenate([piece, pad], axis=1).astype(BF16)


def pack_kernel(shape, teacher_t, student, anchor_ids, relation_ids, side_flags, out, cols):
    rows = jnp.concatenate([anchor_ids[...], relation_ids[...], side_flags[...]], axis=0).astype(F32)
    rows = jnp.concatenate([rows, jnp.zeros((5, rows.shape[1]), F32)], axis=0)
    cols[...] = rows.T.astype(jnp.int32)
    put_row(out, student[...].astype(F32), teacher_t[...].astype(F32).T, shape)


def pack(teacher, student, ids, shape):
    return pl.pallas_call(
        functools.partial(pack_kernel, shape),
        out_shape=(
            jax.ShapeDtypeStruct((teacher.shape[0], shape.total), BF16),
            jax.ShapeDtypeStruct((ids[0].shape[0], 8), jnp.int32),
        ),
        in_specs=[VMEM] * 5,
        out_specs=(VMEM, VMEM),
        compiler_params=pltpu.CompilerParams(vmem_limit_bytes=60 * MIB),
        name="pack_rows",
    )(teacher.T, student, *[x[None] for x in ids])


def relation_kernel(shape, rel, block, cut, base, cols, table_t, student, out):
    start = base[0] * block
    ids = cols[:, 1:2] - start
    hot = (ids == lax.broadcasted_iota(jnp.int32, (cols.shape[0], block), 1)).astype(F32).astype(BF16)
    tail = block - cut
    lanes = lax.broadcasted_iota(jnp.int32, (shape.tw, tail), 1) + cut
    rows = lax.broadcasted_iota(jnp.int32, (tail, shape.sw), 0) + cut
    table = jnp.where(lanes < rel - start, table_t[:, cut:], jnp.zeros((shape.tw, tail), BF16))
    small = jnp.where(rows < rel - start, student[cut:, :], jnp.zeros((tail, shape.sw), BF16))
    dims = (((1,), (1,)), ((), ()))
    found = lax.dot_general(hot[:, cut:], table, dims, preferred_element_type=F32)
    found_s = jnp.dot(hot[:, cut:], small, preferred_element_type=F32)
    if cut:
        found += lax.dot_general(hot[:, :cut], table_t[:, :cut], dims, preferred_element_type=F32)
        found_s += jnp.dot(hot[:, :cut], student[:cut, :], preferred_element_type=F32)
    put_row(out, found_s, found, shape)


def relation_rows(base, cols, table, student, block, shape):
    rel, tw = table.shape
    q = cols.shape[0]
    cut = max(0, rel - rel // block * block) // 128 * 128
    whole = lambda i, base: (0, 0)
    return pl.pallas_call(
        functools.partial(relation_kernel, shape, rel, block, cut),
        out_shape=jax.ShapeDtypeStruct((q, shape.total), BF16),
        grid_spec=pltpu.PrefetchScalarGridSpec(
            num_scalar_prefetch=1,
            grid=(1,),
            in_specs=[
                pl.BlockSpec((q, cols.shape[1]), whole),
                pl.BlockSpec((tw, block), lambda i, base: (0, base[0])),
                pl.BlockSpec((block, shape.sw), lambda i, base: (base[0], 0)),
            ],
            out_specs=pl.BlockSpec((q, shape.total), whole),
        ),
        compiler_params=pltpu.CompilerParams(vmem_limit_bytes=56 * MIB),
        cost_estimate=pl.CostEstimate(
            flops=2 * q * tw * block, bytes_accessed=2 * tw * block, transcendentals=0
        ),
        name="relation_rows",
    )(base, cols, table.T, student)


def joined(shards, columns):
    return jnp.concatenate([shard[:, columns] for shard in shards], axis=0)


def anchor_kernel(count, first_slot, own, has_acc, me, core, owner, cols, *rest):
    acc_in, rest = (rest[0], rest[1:]) if has_acc else (None, rest)
    shards, out = rest[:count], rest[count]
    slab = owner.shape[1] * own
    ids = cols[:, 0:1] - core[0] * slab
    lane = lax.broadcasted_iota(jnp.int32, (cols.shape[0], own), 1)
    group = max(1, 512 // own)
    total = None
    for first in range(0, count, group):
        last = min(count, first + group)
        starts = [owner[me[0], first_slot + j] * own for j in range(first, last)]
        hot = jnp.concatenate([(ids - start == lane).astype(F32).astype(BF16) for start in starts], axis=1)
        found = jnp.dot(hot, joined(shards[first:last], slice(None)), preferred_element_type=F32)
        total = found if total is None else total + found
    total = total.astype(BF16)
    out[...] = total + acc_in[...] if has_acc else total


def anchor_rows(spot, first_slot, cols, shards, acc, shape):
    own = shards[0].shape[0]
    q, count = cols.shape[0], len(shards)
    operands = [*spot, cols] + ([] if acc is None else [acc]) + list(shards)
    return pl.pallas_call(
        functools.partial(anchor_kernel, count, first_slot, own, acc is not None),
        out_shape=jax.ShapeDtypeStruct((q, shape.total), BF16),
        in_specs=[SMEM] * 3 + [VMEM] * (len(operands) - 3),
        out_specs=VMEM,
        compiler_params=pltpu.CompilerParams(vmem_limit_bytes=2 * count * own * (shape.total + q) + 12 * MIB),
        cost_estimate=pl.CostEstimate(
            flops=2 * q * count * own * shape.total,
            bytes_accessed=2 * (count * own + 2 * q) * shape.total,
            transcendentals=0,
        ),
        name="anchor_rows",
    )(*operands)


def score_kernel(shape, own, n, chunk, mine, other, relation, relation_b, cols, *rest):
    shards, (t_out, s_out, stats, q_student, q_teacher) = rest[:n], rest[n:]
    q = mine.shape[0]
    sw, wide = shape.sw, shape.wide
    rows = 128

    def build(i, _):
        at = pl.ds(pl.multiple_of(i * rows, rows), rows)
        g = (2 * cols[at, 2:3] - 1).astype(F32)
        a = mine[at, :].astype(F32) + other[at, :].astype(F32)
        r = relation[at, :].astype(F32) + relation_b[at, :].astype(F32)
        a_re, a_im = a[:, shape.re : shape.re + wide], a[:, shape.im : shape.im + wide]
        r_re, r_im = r[:, shape.re : shape.re + wide], r[:, shape.im : shape.im + wide]
        q_teacher[at, :wide] = (a_re * r_re - g * a_im * r_im).astype(BF16)
        q_teacher[at, wide:] = (a_im * r_re + g * a_re * r_im).astype(BF16)
        a_s, r_s = a[:, :sw], r[:, :sw]
        a_x, r_x = pltpu.roll(a_s, sw // 2, 1), pltpu.roll(r_s, sw // 2, 1)
        low = lax.broadcasted_iota(jnp.int32, (rows, sw), 1) < sw // 2
        re2, im2 = jnp.where(low, r_s, r_x), jnp.where(low, r_x, r_s)
        q_student[at, :] = (a_s * re2 + jnp.where(low, -g, g) * a_x * im2).astype(BF16)
        return 0

    lax.fori_loop(0, q // rows, build, 0)
    dims = (((1,), (1,)), ((), ()))

    def score(c, carry):
        top_t, total_t, weighted, top_s, total_s = carry
        at = slice(c * chunk, (c + 1) * chunk)
        group = shards[c * chunk // own : (c + 1) * chunk // own]
        t = lax.dot_general(joined(group, slice(sw, None)), q_teacher[...], dims, preferred_element_type=F32)
        s = lax.dot_general(joined(group, slice(0, sw)), q_student[...], dims, preferred_element_type=F32)
        t_out[at, :] = t
        s_out[at, :] = s
        new_t = jnp.maximum(top_t, jnp.max(t, axis=0, keepdims=True))
        new_s = jnp.maximum(top_s, jnp.max(s, axis=0, keepdims=True))
        scale_t, scale_s = jnp.exp(top_t - new_t), jnp.exp(top_s - new_s)
        e = jnp.exp(t - new_t)
        total_t = total_t * scale_t + jnp.sum(e, axis=0, keepdims=True)
        weighted = weighted * scale_t + jnp.sum(e * (t - s), axis=0, keepdims=True)
        total_s = total_s * scale_s + jnp.sum(jnp.exp(s - new_s), axis=0, keepdims=True)
        return new_t, total_t, weighted, new_s, total_s

    lowest = jnp.full((1, q), -jnp.inf, F32)
    nothing = jnp.zeros((1, q), F32)
    found = (lowest, nothing, nothing, lowest, nothing)
    for c in range(n * own // chunk):
        found = score(c, found)
    stats[...] = jnp.concatenate(list(found) + [nothing] * 3, axis=0)


def scores(mine, other, relation, relation_b, cols, shards, shape):
    n, own = len(shards), shards[0].shape[0]
    q = mine.shape[0]
    slab = n * own
    chunk = 512 if slab % 512 == 0 else own
    return pl.pallas_call(
        functools.partial(score_kernel, shape, own, n, chunk),
        out_shape=(
            jax.ShapeDtypeStruct((slab, q), F32),
            jax.ShapeDtypeStruct((slab, q), F32),
            jax.ShapeDtypeStruct((8, q), F32),
            jax.ShapeDtypeStruct((q, shape.sw), BF16),
        ),
        in_specs=[VMEM] * (5 + n),
        out_specs=(VMEM,) * 4,
        scratch_shapes=[pltpu.VMEM((q, 2 * shape.wide), BF16)],
        compiler_params=pltpu.CompilerParams(vmem_limit_bytes=8 * slab * q + 2 * slab * shape.total + 10 * MIB),
        cost_estimate=pl.CostEstimate(
            flops=2 * q * slab * shape.total, bytes_accessed=2 * slab * shape.total + 8 * slab * q, transcendentals=2 * slab * q
        ),
        name="scores",
    )(mine, other, relation, relation_b, cols, *shards)


def combine(a, b):
    top_t, top_s = jnp.maximum(a[0:1], b[0:1]), jnp.maximum(a[3:4], b[3:4])
    at, bt = jnp.exp(a[0:1] - top_t), jnp.exp(b[0:1] - top_t)
    as_, bs = jnp.exp(a[3:4] - top_s), jnp.exp(b[3:4] - top_s)
    total_t = a[1:2] * at + b[1:2] * bt
    weighted = a[2:3] * at + b[2:3] * bt
    total_s = a[4:5] * as_ + b[4:5] * bs
    return top_t, total_t, weighted, top_s, total_s


def grad_kernel(n, own, chunk, sw, me, order, t_in, s_in, mine, other, q_student, *rest):
    shards, (divergence, q_grad), outs = rest[:n], rest[n : n + 2], rest[n + 2 : -1]
    e_grad = rest[-1]
    top_t, total_t, weighted, top_s, total_s = combine(mine[...], other[...])
    divergence[...] = weighted / total_t - top_t - jnp.log(total_t) + top_s + jnp.log(total_s)
    over_t, over_s = 1.0 / total_t, 1.0 / total_s
    per = chunk // own

    def step(c, total):
        at = slice(c * chunk, (c + 1) * chunk)
        prob_t = jnp.exp(t_in[at, :] - top_t) * over_t
        prob_s = jnp.exp(s_in[at, :] - top_s) * over_s
        weights = (prob_s - prob_t).astype(BF16)
        grad = jnp.dot(weights, q_student[...], preferred_element_type=F32).astype(BF16)
        for k in range(per):
            e_grad[order[me[0], c * per + k]] = grad[k * own : (k + 1) * own, :]
        return total + lax.dot_general(
            joined(shards[c * per : (c + 1) * per], slice(0, sw)),
            weights,
            (((0,), (0,)), ((), ())),
            preferred_element_type=F32,
        )

    q = q_student.shape[0]
    total = jnp.zeros((sw, q), F32)
    for c in range(n * own // chunk):
        total = step(c, total)
    q_grad[...] = total.T
    count = n // len(outs)
    for d, out in enumerate(outs):
        out[...] = e_grad[d * count : (d + 1) * count]


def gradients(me, order, near, t, s, mine, other, q_student, shards):
    n, own = len(shards), shards[0].shape[0]
    q, sw = q_student.shape
    slab = n * own
    shape_total = shards[0].shape[1]
    chunk = 512 if slab % 512 == 0 else own
    return pl.pallas_call(
        functools.partial(grad_kernel, n, own, chunk, sw),
        out_shape=(
            jax.ShapeDtypeStruct((1, q), F32),
            jax.ShapeDtypeStruct((q, sw), F32),
        )
        + (jax.ShapeDtypeStruct((n // near, own, sw), BF16),) * near,
        in_specs=[SMEM] * 2 + [VMEM] * (5 + n),
        out_specs=(VMEM,) * (2 + near),
        scratch_shapes=[pltpu.VMEM((n, own, sw), BF16)],
        compiler_params=pltpu.CompilerParams(vmem_limit_bytes=8 * slab * q + 2 * slab * shape_total + 10 * MIB),
        cost_estimate=pl.CostEstimate(
            flops=4 * q * slab * sw, bytes_accessed=8 * slab * q, transcendentals=2 * slab * q
        ),
        name="gradients",
    )(me, order, t, s, mine, other, q_student, *shards)


def add_kernel(count, *refs):
    terms, outs = refs[:count], refs[count:]
    for e, out in enumerate(outs):
        total = terms[0][e].astype(F32)
        for term in terms[1:]:
            total += term[e].astype(F32)
        out[...] = total.astype(out.dtype)


def add_blocks(terms):
    far, own, sw = terms[0].shape
    return pl.pallas_call(
        functools.partial(add_kernel, len(terms)),
        out_shape=(jax.ShapeDtypeStruct((own, sw), F32),)
        + (jax.ShapeDtypeStruct((own, sw), BF16),) * (far - 1),
        in_specs=[VMEM] * len(terms),
        out_specs=(VMEM,) * far,
        compiler_params=pltpu.CompilerParams(vmem_limit_bytes=8 * MIB),
        name="add_blocks",
    )(*terms)


def reduce_blocks(blocks, beside, n):
    near, far = len(blocks), n // len(blocks)
    terms = [blocks[0]]
    for d in range(1, near):
        terms.append(lax.ppermute(blocks[d], "query", [(i, i ^ d) for i in range(n)]))
    terms[-1], beside = lax.optimization_barrier((terms[-1], beside))
    sums = add_blocks(terms)
    total = sums[0]
    for e in range(1, far):
        pairs = [(h * near + r, (h + e) % far * near + r) for h in range(far) for r in range(near)]
        total = total + lax.ppermute(sums[e], "query", pairs).astype(F32)
    return total, beside


def make(n, groups):
    place = places(n)
    steps, held = spread_steps(len(place), len(place[0]) == 2)
    table = owners(place, held, n)
    near = next(k for k in (4, 2, 1) if n % k == 0)
    me = np.arange(n)[:, None]
    position = ((table % near) ^ (me % near)) * (n // near) + (table // near - me // near) % (n // near)

    def per_device(
        anchor_ids,
        relation_ids,
        side_flags,
        teacher_entities,
        student_entities,
        teacher_relations,
        student_relations,
    ):
        own, tw = teacher_entities.shape
        shape = Shape(tw, student_entities.shape[1])
        me = lax.axis_index("query")[None]
        spot = (me, lax.axis_index("entity")[None], jnp.asarray(table))
        packed, cols = pack(
            teacher_entities, student_entities, (anchor_ids, relation_ids, side_flags), shape
        )
        have = {(0, 0): packed}
        block = -(-teacher_relations.shape[0] // 512) * 256
        base = (lax.axis_index("entity") % 2).astype(jnp.int32)[None]
        own_key = (0, 0)
        have[own_key], base, spot, me = lax.optimization_barrier((have[own_key], base, spot, me))
        anchors, counted = None, 0
        kept, last = {}, {}
        for number, step in enumerate(steps):
            got = {}
            for shift, old, new in step:
                operand = have[old]
                if shift in last and last[shift] != old:
                    before = last[shift]
                    operand, kept[before] = lax.optimization_barrier((operand, have[before]))
                got[new] = move(operand, place, shift)
                last[shift] = new
            if number == 0:
                relation = relation_rows(base, cols, teacher_relations, student_relations, block, shape)
                got, relation = lax.optimization_barrier((got, relation))
                relation_b = partner(relation, groups, 1)
            if number == len(steps) - 1:
                counted = len(have)
                names = held[:counted]
                anchors = anchor_rows(spot, 0, cols, [kept.get(h, have[h]) for h in names], None, shape)
            have.update(got)
        have.update(kept)
        shards = [have[h] for h in held]
        mine = anchor_rows(spot, counted, cols, shards[counted:], anchors, shape)
        far = 1
        while far < groups // 2:
            mine = mine + partner(mine, groups, far)
            far *= 2
        other = partner(mine, groups, far)
        t, s, stats, q_student = scores(mine, other, relation, relation_b, cols, shards, shape)
        far = 1
        while far < groups // 2:
            found = combine(stats, partner(stats, groups, far))
            stats = jnp.concatenate(list(found) + [jnp.zeros_like(found[0])] * 3, axis=0)
            far *= 2
        divergence, q_grad, *blocks = gradients(
            me, jnp.asarray(position), near, t, s, stats, partner(stats, groups, far), q_student, shards
        )
        far = 1
        while far < groups:
            q_grad = q_grad + partner(q_grad, groups, far)
            far *= 2
        entity_grad, q_grad = reduce_blocks(blocks, q_grad, n)
        return (divergence[0], entity_grad, q_grad)

    return per_device


def solution(mesh):
    in_specs = (
        P("query"),
        P("query"),
        P("query"),
        P(("entity", "query"), None),
        P(("entity", "query"), None),
        P(),
        P(),
    )
    out_specs = (P("query"), P(("entity", "query"), None), P("query", None))
    return jax.shard_map(
        make(mesh.shape["query"], mesh.shape["entity"]),
        mesh=mesh, in_specs=in_specs, out_specs=out_specs, check_vma=False,
    )
```

```python
import functools

import jax
import jax.numpy as jnp
import numpy as np
from jax import lax
from jax.experimental import pallas as pl
from jax.experimental.pallas import tpu as pltpu
from jax.sharding import PartitionSpec as P

F32 = jnp.float32
BF16 = jnp.bfloat16
VMEM = pl.BlockSpec(memory_space=pltpu.VMEM)
SMEM = pl.BlockSpec(memory_space=pltpu.SMEM)
MIB = 1 << 20


def places(n):
    sides = 2 if n % 2 == 0 else 1
    m = n // sides
    order = list(range(m))
    if m % 2 == 0:
        order = [2 * z for z in range(m // 2)] + [2 * z + 1 for z in reversed(range(m // 2))]
    return [[order[p] * sides + x for x in range(sides)] for p in range(m)]


def spread_steps(m, across):
    held = [(0, 0)]
    steps = []
    while len(held) < m * (2 if across else 1):
        taken = []
        for shift in (1, -1, 0):
            if shift == 0 and not across:
                continue
            if shift:
                found = [((k, o), (k, (o + shift) % m)) for k, o in held]
            else:
                found = [((k, o), (1 - k, o)) for k, o in held]
            names = [t[2] for t in taken]
            found = [f for f in found if f[1] not in held and f[1] not in names]
            if found:
                best = min(found, key=lambda f: (f[1][0], -min(f[1][1], m - f[1][1]), f[1][1]))
                taken.append((shift,) + best)
        held += [t[2] for t in taken]
        steps.append(taken)
    return steps, held


def move(x, place, shift):
    m = len(place)
    pairs = []
    for p in range(m):
        for side in range(len(place[0])):
            source = place[(p + shift) % m][side] if shift else place[p][1 - side]
            pairs.append((source, place[p][side]))
    return lax.ppermute(x, "query", sorted(pairs))


def owners(place, held, n):
    owner = np.zeros((n, n), np.int32)
    for p in range(len(place)):
        for side in range(len(place[0])):
            for slot, (k, o) in enumerate(held):
                owner[place[p][side], slot] = place[(p + o) % len(place)][side ^ k]
    return owner


def partner(x, size, far):
    return lax.ppermute(x, "entity", [(i, i ^ far) for i in range(size)])


class Shape:
    def __init__(self, tw, sw):
        self.tw, self.sw = tw, sw
        self.half = tw // 2
        self.wide = -(-self.half // 128) * 128
        self.re, self.im = sw, sw + self.wide
        self.total = sw + 2 * self.wide


def put_row(out, student, teacher, shape):
    out[:, : shape.sw] = student.astype(BF16)
    pad = jnp.zeros((teacher.shape[0], shape.wide - shape.half), F32)
    for start, at in ((0, shape.re), (shape.half, shape.im)):
        piece = teacher[:, start : start + shape.half]
        out[:, at : at + shape.wide] = jnp.concatenate([piece, pad], axis=1).astype(BF16)


def pack_kernel(shape, teacher_t, student, anchor_ids, relation_ids, side_flags, out, cols):
    rows = jnp.concatenate([anchor_ids[...], relation_ids[...], side_flags[...]], axis=0).astype(F32)
    rows = jnp.concatenate([rows, jnp.zeros((5, rows.shape[1]), F32)], axis=0)
    cols[...] = rows.T.astype(jnp.int32)
    put_row(out, student[...].astype(F32), teacher_t[...].astype(F32).T, shape)


def pack(teacher, student, ids, shape):
    return pl.pallas_call(
        functools.partial(pack_kernel, shape),
        out_shape=(
            jax.ShapeDtypeStruct((teacher.shape[0], shape.total), BF16),
            jax.ShapeDtypeStruct((ids[0].shape[0], 8), jnp.int32),
        ),
        in_specs=[VMEM] * 5,
        out_specs=(VMEM, VMEM),
        compiler_params=pltpu.CompilerParams(vmem_limit_bytes=60 * MIB),
        name="pack_rows",
    )(teacher.T, student, *[x[None] for x in ids])


def relation_kernel(shape, rel, block, cut, base, cols, table_t, student, out):
    start = base[0] * block
    ids = cols[:, 1:2] - start
    hot = (ids == lax.broadcasted_iota(jnp.int32, (cols.shape[0], block), 1)).astype(F32).astype(BF16)
    tail = block - cut
    lanes = lax.broadcasted_iota(jnp.int32, (shape.tw, tail), 1) + cut
    rows = lax.broadcasted_iota(jnp.int32, (tail, shape.sw), 0) + cut
    table = jnp.where(lanes < rel - start, table_t[:, cut:], jnp.zeros((shape.tw, tail), BF16))
    small = jnp.where(rows < rel - start, student[cut:, :], jnp.zeros((tail, shape.sw), BF16))
    dims = (((1,), (1,)), ((), ()))
    found = lax.dot_general(hot[:, cut:], table, dims, preferred_element_type=F32)
    found_s = jnp.dot(hot[:, cut:], small, preferred_element_type=F32)
    if cut:
        found += lax.dot_general(hot[:, :cut], table_t[:, :cut], dims, preferred_element_type=F32)
        found_s += jnp.dot(hot[:, :cut], student[:cut, :], preferred_element_type=F32)
    put_row(out, found_s, found, shape)


def relation_rows(base, cols, table, student, block, shape):
    rel, tw = table.shape
    q = cols.shape[0]
    cut = max(0, rel - rel // block * block) // 128 * 128
    whole = lambda i, base: (0, 0)
    return pl.pallas_call(
        functools.partial(relation_kernel, shape, rel, block, cut),
        out_shape=jax.ShapeDtypeStruct((q, shape.total), BF16),
        grid_spec=pltpu.PrefetchScalarGridSpec(
            num_scalar_prefetch=1,
            grid=(1,),
            in_specs=[
                pl.BlockSpec((q, cols.shape[1]), whole),
                pl.BlockSpec((tw, block), lambda i, base: (0, base[0])),
                pl.BlockSpec((block, shape.sw), lambda i, base: (base[0], 0)),
            ],
            out_specs=pl.BlockSpec((q, shape.total), whole),
        ),
        compiler_params=pltpu.CompilerParams(vmem_limit_bytes=56 * MIB),
        cost_estimate=pl.CostEstimate(
            flops=2 * q * tw * block, bytes_accessed=2 * tw * block, transcendentals=0
        ),
        name="relation_rows",
    )(base, cols, table.T, student)


def joined(shards, columns):
    return jnp.concatenate([shard[:, columns] for shard in shards], axis=0)


def anchor_kernel(count, own, has_acc, bases, cols, *rest):
    acc_in, rest = (rest[0], rest[1:]) if has_acc else (None, rest)
    shards, out = rest[:count], rest[count]
    ids = cols[:, 0:1]
    lane = lax.broadcasted_iota(jnp.int32, (cols.shape[0], own), 1)
    group = max(1, 512 // own)
    total = None
    for first in range(0, count, group):
        last = min(count, first + group)
        hot = jnp.concatenate([(ids - bases[j] == lane).astype(F32).astype(BF16) for j in range(first, last)], axis=1)
        found = jnp.dot(hot, joined(shards[first:last], slice(None)), preferred_element_type=F32)
        total = found if total is None else total + found
    total = total.astype(BF16)
    out[...] = total + acc_in[...] if has_acc else total


def anchor_rows(bases, cols, shards, acc, shape):
    own = shards[0].shape[0]
    q, count = cols.shape[0], len(shards)
    operands = [bases, cols] + ([] if acc is None else [acc]) + list(shards)
    return pl.pallas_call(
        functools.partial(anchor_kernel, count, own, acc is not None),
        out_shape=jax.ShapeDtypeStruct((q, shape.total), BF16),
        in_specs=[SMEM, VMEM] + ([] if acc is None else [VMEM]) + [VMEM] * count,
        out_specs=VMEM,
        compiler_params=pltpu.CompilerParams(vmem_limit_bytes=2 * count * own * (shape.total + q) + 12 * MIB),
        cost_estimate=pl.CostEstimate(
            flops=2 * q * count * own * shape.total,
            bytes_accessed=2 * (count * own + 2 * q) * shape.total,
            transcendentals=0,
        ),
        name="anchor_rows",
    )(*operands)


def score_kernel(shape, own, n, chunk, mine, other, relation, relation_b, cols, *rest):
    shards, (t_out, s_out, tops, stats, q_student, q_teacher) = rest[:n], rest[n:]
    q = mine.shape[0]
    sw, wide = shape.sw, shape.wide
    rows = 128

    def build(i, _):
        at = pl.ds(pl.multiple_of(i * rows, rows), rows)
        g = (2 * cols[at, 2:3] - 1).astype(F32)
        a = mine[at, :].astype(F32) + other[at, :].astype(F32)
        r = relation[at, :].astype(F32) + relation_b[at, :].astype(F32)
        a_re, a_im = a[:, shape.re : shape.re + wide], a[:, shape.im : shape.im + wide]
        r_re, r_im = r[:, shape.re : shape.re + wide], r[:, shape.im : shape.im + wide]
        q_teacher[at, :wide] = (a_re * r_re - g * a_im * r_im).astype(BF16)
        q_teacher[at, wide:] = (a_im * r_re + g * a_re * r_im).astype(BF16)
        a_s, r_s = a[:, :sw], r[:, :sw]
        a_x, r_x = pltpu.roll(a_s, sw // 2, 1), pltpu.roll(r_s, sw // 2, 1)
        low = lax.broadcasted_iota(jnp.int32, (rows, sw), 1) < sw // 2
        re2, im2 = jnp.where(low, r_s, r_x), jnp.where(low, r_x, r_s)
        q_student[at, :] = (a_s * re2 + jnp.where(low, -g, g) * a_x * im2).astype(BF16)
        return 0

    lax.fori_loop(0, q // rows, build, 0)
    dims = (((1,), (1,)), ((), ()))

    def score(c, carry):
        top_t, total_t, weighted, top_s, total_s = carry
        at = slice(c * chunk, (c + 1) * chunk)
        group = shards[c * chunk // own : (c + 1) * chunk // own]
        t = lax.dot_general(joined(group, slice(sw, None)), q_teacher[...], dims, preferred_element_type=F32)
        s = lax.dot_general(joined(group, slice(0, sw)), q_student[...], dims, preferred_element_type=F32)
        new_t = jnp.maximum(top_t, jnp.max(t, axis=0, keepdims=True))
        new_s = jnp.maximum(top_s, jnp.max(s, axis=0, keepdims=True))
        scale_t, scale_s = jnp.exp(top_t - new_t), jnp.exp(top_s - new_s)
        e = jnp.exp(t - new_t)
        f = jnp.exp(s - new_s)
        t_out[at, :] = e
        s_out[at, :] = f
        tops[2 * c : 2 * c + 1, :] = new_t
        tops[2 * c + 1 : 2 * c + 2, :] = new_s
        total_t = total_t * scale_t + jnp.sum(e, axis=0, keepdims=True)
        weighted = weighted * scale_t + jnp.sum(e * (t - s), axis=0, keepdims=True)
        total_s = total_s * scale_s + jnp.sum(f, axis=0, keepdims=True)
        return new_t, total_t, weighted, new_s, total_s

    lowest = jnp.full((1, q), -jnp.inf, F32)
    nothing = jnp.zeros((1, q), F32)
    found = (lowest, nothing, nothing, lowest, nothing)
    for c in range(n * own // chunk):
        found = score(c, found)
    stats[...] = jnp.concatenate(list(found) + [nothing] * 3, axis=0)


def scores(mine, other, relation, relation_b, cols, shards, shape):
    n, own = len(shards), shards[0].shape[0]
    q = mine.shape[0]
    slab = n * own
    chunk = 512 if slab % 512 == 0 else own
    return pl.pallas_call(
        functools.partial(score_kernel, shape, own, n, chunk),
        out_shape=(
            jax.ShapeDtypeStruct((slab, q), F32),
            jax.ShapeDtypeStruct((slab, q), F32),
            jax.ShapeDtypeStruct((2 * slab // chunk, q), F32),
            jax.ShapeDtypeStruct((8, q), F32),
            jax.ShapeDtypeStruct((q, shape.sw), BF16),
        ),
        in_specs=[VMEM] * (5 + n),
        out_specs=(VMEM,) * 5,
        scratch_shapes=[pltpu.VMEM((q, 2 * shape.wide), BF16)],
        compiler_params=pltpu.CompilerParams(vmem_limit_bytes=8 * slab * q + 2 * slab * shape.total + 10 * MIB),
        cost_estimate=pl.CostEstimate(
            flops=2 * q * slab * shape.total, bytes_accessed=2 * slab * shape.total + 8 * slab * q, transcendentals=2 * slab * q
        ),
        name="scores",
    )(mine, other, relation, relation_b, cols, *shards)


def combine(a, b):
    top_t, top_s = jnp.maximum(a[0:1], b[0:1]), jnp.maximum(a[3:4], b[3:4])
    at, bt = jnp.exp(a[0:1] - top_t), jnp.exp(b[0:1] - top_t)
    as_, bs = jnp.exp(a[3:4] - top_s), jnp.exp(b[3:4] - top_s)
    total_t = a[1:2] * at + b[1:2] * bt
    weighted = a[2:3] * at + b[2:3] * bt
    total_s = a[4:5] * as_ + b[4:5] * bs
    return top_t, total_t, weighted, top_s, total_s


def grad_kernel(n, own, chunk, sw, order, t_in, s_in, tops, mine, other, q_student, *rest):
    shards, (divergence, q_grad), outs = rest[:n], rest[n : n + 2], rest[n + 2 : -1]
    e_grad = rest[-1]
    top_t, total_t, weighted, top_s, total_s = combine(mine[...], other[...])
    divergence[...] = weighted / total_t - top_t - jnp.log(total_t) + top_s + jnp.log(total_s)
    over_t, over_s = 1.0 / total_t, 1.0 / total_s
    per = chunk // own

    def step(c, total):
        at = slice(c * chunk, (c + 1) * chunk)
        scale_t = jnp.exp(tops[2 * c : 2 * c + 1, :] - top_t) * over_t
        scale_s = jnp.exp(tops[2 * c + 1 : 2 * c + 2, :] - top_s) * over_s
        weights = (s_in[at, :] * scale_s - t_in[at, :] * scale_t).astype(BF16)
        grad = jnp.dot(weights, q_student[...], preferred_element_type=F32).astype(BF16)
        for k in range(per):
            e_grad[order[c * per + k]] = grad[k * own : (k + 1) * own, :]
        return total + lax.dot_general(
            joined(shards[c * per : (c + 1) * per], slice(0, sw)),
            weights,
            (((0,), (0,)), ((), ())),
            preferred_element_type=F32,
        )

    q = q_student.shape[0]
    total = jnp.zeros((sw, q), F32)
    for c in range(n * own // chunk):
        total = step(c, total)
    q_grad[...] = total.T
    count = n // len(outs)
    for d, out in enumerate(outs):
        out[...] = e_grad[d * count : (d + 1) * count]


def gradients(order, near, t, s, tops, mine, other, q_student, shards):
    n, own = len(shards), shards[0].shape[0]
    q, sw = q_student.shape
    slab = n * own
    shape_total = shards[0].shape[1]
    chunk = 512 if slab % 512 == 0 else own
    return pl.pallas_call(
        functools.partial(grad_kernel, n, own, chunk, sw),
        out_shape=(
            jax.ShapeDtypeStruct((1, q), F32),
            jax.ShapeDtypeStruct((q, sw), F32),
        )
        + (jax.ShapeDtypeStruct((n // near, own, sw), BF16),) * near,
        in_specs=[SMEM] + [VMEM] * (6 + n),
        out_specs=(VMEM,) * (2 + near),
        scratch_shapes=[pltpu.VMEM((n, own, sw), BF16)],
        compiler_params=pltpu.CompilerParams(vmem_limit_bytes=8 * slab * q + 2 * slab * shape_total + 10 * MIB),
        cost_estimate=pl.CostEstimate(
            flops=4 * q * slab * sw, bytes_accessed=8 * slab * q, transcendentals=2 * slab * q
        ),
        name="gradients",
    )(order, t, s, tops, mine, other, q_student, *shards)


def add_kernel(count, *refs):
    terms, outs = refs[:count], refs[count:]
    for e, out in enumerate(outs):
        total = terms[0][e].astype(F32)
        for term in terms[1:]:
            total += term[e].astype(F32)
        out[...] = total.astype(out.dtype)


def add_blocks(terms):
    far, own, sw = terms[0].shape
    return pl.pallas_call(
        functools.partial(add_kernel, len(terms)),
        out_shape=(jax.ShapeDtypeStruct((own, sw), F32),)
        + (jax.ShapeDtypeStruct((own, sw), BF16),) * (far - 1),
        in_specs=[VMEM] * len(terms),
        out_specs=(VMEM,) * far,
        compiler_params=pltpu.CompilerParams(vmem_limit_bytes=8 * MIB),
        name="add_blocks",
    )(*terms)


def reduce_blocks(blocks, beside, n):
    near, far = len(blocks), n // len(blocks)
    terms = [blocks[0]]
    for d in range(1, near):
        terms.append(lax.ppermute(blocks[d], "query", [(i, i ^ d) for i in range(n)]))
    terms[-1], beside = lax.optimization_barrier((terms[-1], beside))
    sums = add_blocks(terms)
    total = sums[0]
    for e in range(1, far):
        pairs = [(h * near + r, (h + e) % far * near + r) for h in range(far) for r in range(near)]
        total = total + lax.ppermute(sums[e], "query", pairs).astype(F32)
    return total, beside


def make(n, groups):
    place = places(n)
    steps, held = spread_steps(len(place), len(place[0]) == 2)
    table = owners(place, held, n)
    near = next(k for k in (4, 2, 1) if n % k == 0)
    me = np.arange(n)[:, None]
    position = ((table % near) ^ (me % near)) * (n // near) + (table // near - me // near) % (n // near)

    def per_device(
        anchor_ids,
        relation_ids,
        side_flags,
        teacher_entities,
        student_entities,
        teacher_relations,
        student_relations,
    ):
        own, tw = teacher_entities.shape
        shape = Shape(tw, student_entities.shape[1])
        owner, order = jnp.asarray(np.stack([table, position], axis=1))[lax.axis_index("query")]
        bases = (owner + lax.axis_index("entity") * n) * own
        packed, cols = pack(
            teacher_entities, student_entities, (anchor_ids, relation_ids, side_flags), shape
        )
        have = {(0, 0): packed}
        block = -(-teacher_relations.shape[0] // 512) * 256
        base = (lax.axis_index("entity") % 2).astype(jnp.int32)[None]
        own_key = (0, 0)
        have[own_key], base = lax.optimization_barrier((have[own_key], base))
        anchors, counted = None, 0
        kept, last = {}, {}
        for number, step in enumerate(steps):
            got = {}
            for shift, old, new in step:
                operand = have[old]
                if shift in last and last[shift] != old:
                    before = last[shift]
                    operand, kept[before] = lax.optimization_barrier((operand, have[before]))
                got[new] = move(operand, place, shift)
                last[shift] = new
            if number == 0:
                relation = relation_rows(base, cols, teacher_relations, student_relations, block, shape)
                got, relation = lax.optimization_barrier((got, relation))
                relation_b = partner(relation, groups, 1)
            if number == len(steps) - 1:
                counted = len(have)
                names = held[:counted]
                anchors = anchor_rows(bases, cols, [kept.get(h, have[h]) for h in names], None, shape)
            have.update(got)
        have.update(kept)
        shards = [have[h] for h in held]
        mine = anchor_rows(bases[counted:], cols, shards[counted:], anchors, shape)
        far = 1
        while far < groups // 2:
            mine = mine + partner(mine, groups, far)
            far *= 2
        other = partner(mine, groups, far)
        expo_t, expo_s, tops, stats, q_student = scores(mine, other, relation, relation_b, cols, shards, shape)
        far = 1
        while far < groups // 2:
            found = combine(stats, partner(stats, groups, far))
            stats = jnp.concatenate(list(found) + [jnp.zeros_like(found[0])] * 3, axis=0)
            far *= 2
        divergence, q_grad, *blocks = gradients(
            order, near, expo_t, expo_s, tops, stats, partner(stats, groups, far), q_student, shards
        )
        far = 1
        while far < groups:
            q_grad = q_grad + partner(q_grad, groups, far)
            far *= 2
        entity_grad, q_grad = reduce_blocks(blocks, q_grad, n)
        return (divergence[0], entity_grad, q_grad)

    return per_device


def solution(mesh):
    in_specs = (
        P("query"),
        P("query"),
        P("query"),
        P(("entity", "query"), None),
        P(("entity", "query"), None),
        P(),
        P(),
    )
    out_specs = (P("query"), P(("entity", "query"), None), P("query", None))
    return jax.shard_map(
        make(mesh.shape["query"], mesh.shape["entity"]),
        mesh=mesh, in_specs=in_specs, out_specs=out_specs, check_vma=False,
    )
```
